32 devices in a mesh: replica: 4 (over z), fsdp: 8 (over y, x, core).
Axes of the slice: x: 2, y: 2, z: 4, core: 2. Of those that a mesh axis runs over, the one named last changes fastest.
Arguments:
- tokens_in: bfloat16 [16384, 1024], P(('replica', 'fsdp')), may hold values from -6 to 6
- cotangent: bfloat16 [16384, 1024], P(('replica', 'fsdp')), may hold values from -6 to 6
- document_lengths: int32 [32, 4], P(('replica', 'fsdp')), may hold values from 4 to 256, as said below
- expert_choice: int32 [16384, 8], P(('replica', 'fsdp')), may hold values from 0 to 15, all different within a row; in each aligned block of 512 rows (0 to 511, 512 to 1023, ...) at most 384 rows name the same one
- norm_gains: float32 [2, 1024], P(None, 'fsdp'), may hold values from 0.5 to 1.5
- gains_first: float32 [2, 1024], P(None, 'fsdp'), may hold values from -128 to 128
- gains_second: float32 [2, 1024], P(None, 'fsdp'), may hold values from 2621.44 to 10321.92
- query_weight: float32 [1024, 1024], P('fsdp'), may hold values from -0.1875 to 0.1875
- query_first: float32 [1024, 1024], P('fsdp'), may hold values from -80 to 80
- query_second: float32 [1024, 1024], P('fsdp'), may hold values from 868.352 to 3440.64
- keyvalue_weight: float32 [2, 1024, 512], P(None, 'fsdp'), may hold values from -0.1875 to 0.1875
- keyvalue_first_moment: float32 [2, 1024, 512], P(None, 'fsdp'), may hold values from -128 to 128
- keyvalue_second_moment: float32 [2, 1024, 512], P(None, 'fsdp'), may hold values from 1720.32 to 6881.28
- output_weight: float32 [1024, 1024], P('fsdp'), may hold values from -0.75 to 0.75
- output_first: float32 [1024, 1024], P('fsdp'), may hold values from -20 to 20
- output_second: float32 [1024, 1024], P('fsdp'), may hold values from 52.4288 to 206.4384
- router_weight: float32 [1024, 16], P('fsdp'), may hold values from -0.09375 to 0.09375
- router_first: float32 [1024, 16], P('fsdp'), may hold values from -640 to 640
- router_second: float32 [1024, 16], P('fsdp'), may hold values from 42598.4 to 172032
- gateup_weight: float32 [16, 2, 1024, 512], P(None, None, 'fsdp'), may hold values from -0.1875 to 0.1875
- gateup_first: float32 [16, 2, 1024, 512], P(None, None, 'fsdp'), may hold values from -28 to 28
- gateup_second: float32 [16, 2, 1024, 512], P(None, None, 'fsdp'), may hold values from 103.2192 to 409.6
- down_weight: float32 [16, 512, 1024], P(None, None, 'fsdp'), may hold values from -1 to 1
- down_first: float32 [16, 512, 1024], P(None, None, 'fsdp'), may hold values from -4 to 4
- down_second: float32 [16, 512, 1024], P(None, None, 'fsdp'), may hold values from 2.12992 to 8.68352
Outputs:
- block_output: bfloat16 [16384, 1024], P(('replica', 'fsdp'))
- input_gradient: float32 [16384, 1024], P(('replica', 'fsdp'))
- gains_moment: float32 [2, 1024], P(None, 'fsdp')
- gains_square: float32 [2, 1024], P(None, 'fsdp')
- gains_renewed: float32 [2, 1024], P(None, 'fsdp')
- query_moment: float32 [1024, 1024], P('fsdp')
- query_square: float32 [1024, 1024], P('fsdp')
- query_renewed: float32 [1024, 1024], P('fsdp')
- keyval_moment: float32 [2, 1024, 512], P(None, 'fsdp')
- keyval_square: float32 [2, 1024, 512], P(None, 'fsdp')
- keyval_renewed: float32 [2, 1024, 512], P(None, 'fsdp')
- output_moment: float32 [1024, 1024], P('fsdp')
- output_square: float32 [1024, 1024], P('fsdp')
- output_renewed: float32 [1024, 1024], P('fsdp')
- router_moment: float32 [1024, 16], P('fsdp')
- router_square: float32 [1024, 16], P('fsdp')
- router_renewed: float32 [1024, 16], P('fsdp')
- gateup_moment: float32 [16, 2, 1024, 512], P(None, None, 'fsdp')
- gateup_square: float32 [16, 2, 1024, 512], P(None, None, 'fsdp')
- gateup_renewed: float32 [16, 2, 1024, 512], P(None, None, 'fsdp')
- down_moment: float32 [16, 512, 1024], P(None, None, 'fsdp')
- down_square: float32 [16, 512, 1024], P(None, None, 'fsdp')
- down_renewed: float32 [16, 512, 1024], P(None, None, 'fsdp')
The draws below stay inside these ranges and needn't reach their ends.
Inputs may be any that keep to these rules, and one draw needn't show every extreme that they name: `document_lengths`: each row holds the lengths of one device's 4 documents, packed from its first slot; one of them has exactly 256 tokens, the others 4 to 85; slots after their sum are padding. `expert_choice`: among the rows of one device no expert is named more than 384 times, and on some devices an expert is named exactly 384 times.
All inputs are finite; a program needn't handle non-finite values.
Results may differ from the reference program's by a relative error of at most 0.014.
The reference program's roundings to bfloat16 on the way count: a program that leaves them out, or rounds other values in their place, can miss the bound.
Values may be sent and summed in bfloat16 or wider, within the bound.
No kernel may reach another device: no remote copies, remote signals or barrier semaphores. Data moves between devices by JAX's collectives and lax.ppermute only.
A program may use at most 320 MiB of HBM per device.

```python
import math
import jax
import jax.numpy as jnp
import numpy as np
from jax import lax

MODEL_WIDTH = 1024
QUERY_HEADS = 16
KEYVALUE_HEADS = 8
HEAD_SIZE = 64
F = 512
TOPK = 8
EXPERTS = 16
TOK_DEV = 512
DOCS = 4
ADAM_STEP = 5
MAXLEN = 256
CAP = 384
GROUPS = 32
TOKEN_SLOTS = 16384


def draw_document_lengths(key, part):
    key = jax.random.fold_in(key, 17)
    short_key, long_key = jax.random.split(key)
    longest_short = (TOK_DEV - MAXLEN) // (DOCS - 1)
    others = jax.random.randint(short_key, (GROUPS, DOCS), 4, longest_short + 1, dtype=jnp.int32)
    where_long = jax.random.randint(long_key, (GROUPS, 1), 0, DOCS, dtype=jnp.int32)
    column = jnp.arange(DOCS, dtype=jnp.int32)[None, :]
    return jnp.where(column == where_long, MAXLEN, others).astype(jnp.int32)


def block_levels(own_key, dims, cuts, smallest, high):
    loudness, own = 1.0, jax.random.fold_in(own_key, 6)
    for dim, shards_of in cuts:
        draws = jnp.exp(jax.random.uniform(jax.random.fold_in(own, dim), (shards_of,), jnp.float32, smallest / len(cuts), high / len(cuts)))
        loudness = loudness * jnp.repeat(draws, dims[dim] // shards_of).reshape([-1 if axis == dim else 1 for axis in range(len(dims))])
    return loudness


def assign_block(stream_key, own, number, rows, amount, top, reach, skew):
    sequence = jax.random.permutation(stream_key, amount)
    heavy_load, ordinary = load_shares(amount, rows * top, reach, skew, True), load_shares(amount, rows * top, reach, skew, False)
    places = jnp.arange(amount)

    def named(sizes, offset_by):
        used = int((sizes > 0).sum())
        fixed = max(1, used // 4)
        shifted = fixed + (places - fixed + offset_by * (used - fixed)) % max(1, amount - fixed)
        return jnp.zeros((amount,), jnp.int32).at[sequence[jnp.where(places < fixed, places, shifted)]].set(jnp.asarray(sizes, jnp.int32))

    sizes = jnp.where(number % 4 == 0, named(heavy_load, number // 4), named(ordinary, number - number // 4 - 1))
    mixed = jax.random.permutation(jax.random.fold_in(own, 3), amount)
    giver, sink = mixed[0:amount // 2 * 2:2], mixed[1:amount // 2 * 2:2]
    margin = jnp.minimum(sizes[giver] - 1, reach - sizes[sink]) // 2
    margin = jnp.where((giver == sequence[0]) | (sink == sequence[0]) | (sizes[sink] == 0), 0, jnp.maximum(margin, 0))
    shifted = jax.random.randint(jax.random.fold_in(own, 4), (amount // 2,), 0, 1 << 20) % (margin + 1)
    sizes = sizes.at[giver].add(-shifted).at[sink].add(shifted)
    items = jnp.searchsorted(jnp.cumsum(sizes), jnp.arange(rows * top), side="right").astype(jnp.int32)
    listing = items.reshape(top, rows).T
    listing = listing[jax.random.permutation(jax.random.fold_in(own, 1), rows)]
    offset_by = jax.random.randint(jax.random.fold_in(own, 2), (rows, 1), 0, top)
    return jnp.take_along_axis(listing, (jnp.arange(top)[None, :] + offset_by) % top, axis=1)


def load_shares(count, total, most, lean, full):
    portions = [(1 << 20) // math.isqrt(grade ** lean) + 1 for grade in range(1, count + 1)]
    largest = most if full else min(most, max(-(-total // count), total * portions[0] // sum(portions)))
    least = 1 if total - largest >= count - 1 else 0
    counts, rest = [largest] + [least] * (count - 1), total - largest - least * (count - 1)
    while rest > 0:
        candidates = [i for i in range(1, count) if counts[i] < largest] or [i for i in range(1, count) if counts[i] < most]
        whole, budget = sum([portions[i] for i in candidates]), rest
        for i in candidates:
            addition = min(most - counts[i], max(1, budget * portions[i] // whole), rest)
            counts[i] = counts[i] + addition
            rest = rest - addition
    return np.array(counts)


def scatter_about(key, dims, scale, reach, cuts=(), kind=jnp.bfloat16):
    entries = scale * jax.random.normal(key, dims, jnp.float32)
    if cuts:
        entries = entries * block_levels(key, dims, cuts, -0.22, 0.18)
    return jnp.clip(entries, -reach, reach).astype(kind)


def setup_inputs(seed: int = 0) -> dict:
    key_of = jax.random.split(jax.random.key(seed), 26)
    tokens_in = scatter_about(key_of[0], (TOKEN_SLOTS, MODEL_WIDTH), 1.0, 6.0, ((0, 32),))
    cotangent = scatter_about(key_of[1], (TOKEN_SLOTS, MODEL_WIDTH), 1.0, 6.0, ((0, 32),))
    document_lengths = draw_document_lengths(jax.random.fold_in(key_of[25], 71), 0)
    expert_choice_keys = jax.random.split(jax.random.fold_in(key_of[3], 1), TOKEN_SLOTS // TOK_DEV)
    expert_choice_turns = jax.random.permutation(jax.random.fold_in(key_of[3], 3), TOKEN_SLOTS // TOK_DEV)
    expert_choice = jax.vmap(lambda own, number: assign_block(jax.random.fold_in(key_of[3], 2), own, number, TOK_DEV, EXPERTS, TOPK, CAP, 1))(expert_choice_keys, expert_choice_turns).reshape((TOKEN_SLOTS, TOPK))
    norm_gains = jnp.clip(1.0 + 0.1 * jax.random.normal(key_of[4], (2, MODEL_WIDTH), jnp.float32), 0.5, 1.5)
    gains_first = scatter_about(key_of[5], (2, MODEL_WIDTH), (0.19 * TOKEN_SLOTS ** 0.5), 128.0, ((1, 8),), jnp.float32)
    gains_second = jnp.clip(jnp.exp(math.log(10321.92) - 1.370546 * jax.random.uniform(key_of[6], (2, MODEL_WIDTH), jnp.float32) ** block_levels(key_of[6], (2, MODEL_WIDTH), ((1, 8),), -0.2, 0.2)), 2621.44, 10321.92)
    query_weight = scatter_about(key_of[7], (MODEL_WIDTH, QUERY_HEADS * HEAD_SIZE), MODEL_WIDTH ** -0.5, 0.1875, ((0, 8),), jnp.float32)
    query_first = scatter_about(key_of[8], (MODEL_WIDTH, QUERY_HEADS * HEAD_SIZE), (0.11 * TOKEN_SLOTS ** 0.5), 80.0, ((0, 8),), jnp.float32)
    query_second = jnp.clip(jnp.exp(math.log(3440.64) - 1.3768156 * jax.random.uniform(key_of[9], (MODEL_WIDTH, QUERY_HEADS * HEAD_SIZE), jnp.float32) ** block_levels(key_of[9], (MODEL_WIDTH, QUERY_HEADS * HEAD_SIZE), ((0, 8),), -0.2, 0.2)), 868.352, 3440.64)
    keyvalue_weight = scatter_about(key_of[10], (2, MODEL_WIDTH, KEYVALUE_HEADS * HEAD_SIZE), MODEL_WIDTH ** -0.5, 0.1875, ((1, 8),), jnp.float32)
    keyvalue_first_moment = scatter_about(key_of[11], (2, MODEL_WIDTH, KEYVALUE_HEADS * HEAD_SIZE), (0.16 * TOKEN_SLOTS ** 0.5), 128.0, ((1, 8),), jnp.float32)
    keyvalue_second_moment = jnp.clip(jnp.exp(math.log(6881.28) - 1.3862944 * jax.random.uniform(key_of[12], (2, MODEL_WIDTH, KEYVALUE_HEADS * HEAD_SIZE), jnp.float32) ** block_levels(key_of[12], (2, MODEL_WIDTH, KEYVALUE_HEADS * HEAD_SIZE), ((1, 8),), -0.2, 0.2)), 1720.32, 6881.28)
    output_weight = scatter_about(key_of[13], (QUERY_HEADS * HEAD_SIZE, MODEL_WIDTH), (QUERY_HEADS * HEAD_SIZE // 16) ** -0.5, 0.75, ((0, 8),), jnp.float32)
    output_first = scatter_about(key_of[14], (QUERY_HEADS * HEAD_SIZE, MODEL_WIDTH), (0.027 * TOKEN_SLOTS ** 0.5), 20.0, ((0, 8),), jnp.float32)
    output_second = jnp.clip(jnp.exp(math.log(206.4384) - 1.370546 * jax.random.uniform(key_of[15], (QUERY_HEADS * HEAD_SIZE, MODEL_WIDTH), jnp.float32) ** block_levels(key_of[15], (QUERY_HEADS * HEAD_SIZE, MODEL_WIDTH), ((0, 8),), -0.2, 0.2)), 52.4288, 206.4384)
    router_weight = scatter_about(key_of[16], (MODEL_WIDTH, EXPERTS), (4 * MODEL_WIDTH) ** -0.5, 0.09375, ((0, 8),), jnp.float32)
    router_first = scatter_about(key_of[17], (MODEL_WIDTH, EXPERTS), (0.79 * TOKEN_SLOTS ** 0.5), 640.0, ((0, 8),), jnp.float32)
    router_second = jnp.clip(jnp.exp(math.log(172032.0) - 1.39586385 * jax.random.uniform(key_of[18], (MODEL_WIDTH, EXPERTS), jnp.float32) ** block_levels(key_of[18], (MODEL_WIDTH, EXPERTS), ((0, 8),), -0.2, 0.2)), 42598.4, 172032.0)
    gateup_weight = scatter_about(key_of[19], (EXPERTS, 2, MODEL_WIDTH, F), MODEL_WIDTH ** -0.5, 0.1875, ((2, 8),), jnp.float32)
    gateup_first = scatter_about(key_of[20], (EXPERTS, 2, MODEL_WIDTH, F), (0.038 * TOKEN_SLOTS ** 0.5), 28.0, ((2, 8),), jnp.float32)
    gateup_second = jnp.clip(jnp.exp(math.log(409.6) - 1.3783262 * jax.random.uniform(key_of[21], (EXPERTS, 2, MODEL_WIDTH, F), jnp.float32) ** block_levels(key_of[21], (EXPERTS, 2, MODEL_WIDTH, F), ((2, 8),), -0.2, 0.2)), 103.2192, 409.6)
    down_weight = scatter_about(key_of[22], (EXPERTS, F, MODEL_WIDTH), (F // 16) ** -0.5, 1.0, ((2, 8),), jnp.float32)
    down_first = scatter_about(key_of[23], (EXPERTS, F, MODEL_WIDTH), (0.0055 * TOKEN_SLOTS ** 0.5), 4.0, ((2, 8),), jnp.float32)
    down_second = jnp.clip(jnp.exp(math.log(8.68352) - 1.4053426 * jax.random.uniform(key_of[24], (EXPERTS, F, MODEL_WIDTH), jnp.float32) ** block_levels(key_of[24], (EXPERTS, F, MODEL_WIDTH), ((2, 8),), -0.2, 0.2)), 2.12992, 8.68352)
    return {"tokens_in": tokens_in, "cotangent": cotangent, "document_lengths": document_lengths, "expert_choice": expert_choice, "norm_gains": norm_gains, "gains_first": gains_first, "gains_second": gains_second, "query_weight": query_weight, "query_first": query_first, "query_second": query_second, "keyvalue_weight": keyvalue_weight, "keyvalue_first_moment": keyvalue_first_moment, "keyvalue_second_moment": keyvalue_second_moment, "output_weight": output_weight, "output_first": output_first, "output_second": output_second, "router_weight": router_weight, "router_first": router_first, "router_second": router_second, "gateup_weight": gateup_weight, "gateup_first": gateup_first, "gateup_second": gateup_second, "down_weight": down_weight, "down_first": down_first, "down_second": down_second}


norm_eps = 1e-06
rope_base = 10000.0
beta_one = 0.9
beta_two = 0.95
adam_eps = 1e-08
decay_rate = 0.1
gain_rate = 0.25
masked_value = -1e+30
highest = lax.Precision.HIGHEST

@jax.custom_vjp
def lower_precision(v):
    return lax.optimization_barrier(v.astype(jnp.bfloat16)).astype(jnp.float32)

@jax.custom_vjp
def low_back(v):
    return v

def low_keep(v):
    return (lower_precision(v), None)

def low_pass(kept, grad):
    return (grad,)

def back_keep(v):
    return (v, None)

def back_low(kept, grad):
    return (lower_precision(grad),)
lower_precision.defvjp(low_keep, low_pass)
low_back.defvjp(back_keep, back_low)

def layout(lengths, count_of_rows):
    document_ends = jnp.cumsum(lengths).astype(jnp.int32)
    row_index = jnp.arange(count_of_rows, dtype=jnp.int32)
    passed = row_index[:, None] >= document_ends[None, :]
    segment = lax.optimization_barrier(jnp.sum(passed.astype(jnp.int32), axis=1)).astype(jnp.int32)
    start_row = lax.optimization_barrier(jnp.sum(jnp.where(passed, lengths[None, :], 0), axis=1)).astype(jnp.int32)
    position = (row_index - start_row).astype(jnp.float32)
    alive_mask = (segment < lengths.shape[0]).astype(jnp.float32)
    allowed = (segment[:, None] == segment[None, :]) & (row_index[None, :] <= row_index[:, None])
    return (position, alive_mask, allowed)

def rope_tables(position):
    half_width = HEAD_SIZE // 2
    exponents = jnp.arange(half_width, dtype=jnp.float32) * (2.0 / HEAD_SIZE)
    inverse = jnp.exp(exponents * -math.log(rope_base))
    angles = position[:, None] * inverse[None, :]
    return (jnp.cos(angles)[:, None, :], jnp.sin(angles)[:, None, :])

def apply_rotary(values, cosine_lookup, sine_lookup):
    half_width = values.shape[-1] // 2
    front_half = values[..., :half_width]
    back_half = values[..., half_width:]
    return jnp.concatenate([front_half * cosine_lookup - back_half * sine_lookup, back_half * cosine_lookup + front_half * sine_lookup], axis=-1)

def rms_scaled(values):
    return values * lax.rsqrt(lax.optimization_barrier(jnp.mean(values * values, axis=-1, keepdims=True)) + norm_eps)

def adamw_step(weight, moment_old, square_old, gradient, step_rate, shrink):
    moment = beta_one * moment_old + (1.0 - beta_one) * gradient
    square = beta_two * square_old + (1.0 - beta_two) * gradient * gradient
    moment_hat = moment / (1.0 - beta_one ** ADAM_STEP)
    square_hat = square / (1.0 - beta_two ** ADAM_STEP)
    renewed = weight - step_rate * (moment_hat / (jnp.sqrt(square_hat) + adam_eps) + shrink * weight)
    return (moment, square, renewed)

def group_forward(lowered, rows_in, lengths, picked):
    gains_full, query_full, keyval_full, output_full, router_full, gateup_full, down_full = lowered
    count_of_rows = rows_in.shape[0]
    heads_per_group = QUERY_HEADS // KEYVALUE_HEADS
    position, alive_mask, allowed = layout(lengths, count_of_rows)
    cosine_lookup, sine_lookup = rope_tables(position)
    alive_rows = alive_mask[:, None]
    normed = lower_precision(rms_scaled(rows_in) * gains_full[0])
    query_projected = low_back(jnp.dot(normed, query_full, precision=highest))
    key_projected = low_back(jnp.dot(normed, keyval_full[0], precision=highest))
    value_projected = low_back(jnp.dot(normed, keyval_full[1], precision=highest))
    query_rows = lower_precision(apply_rotary(query_projected.reshape(count_of_rows, QUERY_HEADS, HEAD_SIZE), cosine_lookup, sine_lookup)).reshape(count_of_rows, KEYVALUE_HEADS, heads_per_group, HEAD_SIZE)
    rows_of_keys = lower_precision(apply_rotary(key_projected.reshape(count_of_rows, KEYVALUE_HEADS, HEAD_SIZE), cosine_lookup, sine_lookup))
    rows_of_values = lower_precision(value_projected.reshape(count_of_rows, KEYVALUE_HEADS, HEAD_SIZE))
    raw_scores = low_back(jnp.einsum('qhgd,khd->hgqk', query_rows, rows_of_keys, precision=highest) * HEAD_SIZE ** (-0.5))
    scores = jnp.where(allowed[None, None], raw_scores, masked_value)
    soft_weights = lower_precision(jax.nn.softmax(scores, axis=-1))
    mixed_heads = lower_precision(low_back(jnp.einsum('hgqk,khd->qhgd', soft_weights, rows_of_values, precision=highest).reshape(count_of_rows, QUERY_HEADS * HEAD_SIZE)))
    attended = low_back(jnp.dot(mixed_heads, output_full, precision=highest))
    middle = rows_in + alive_rows * attended
    normed_two = lower_precision(rms_scaled(middle) * gains_full[1])
    logits = low_back(jnp.dot(normed_two, router_full, precision=highest))
    expert_row = jnp.arange(EXPERTS, dtype=jnp.int32)
    onehot = (picked[:, :, None] == expert_row[None, None, :]).astype(jnp.float32)
    chosen = lax.optimization_barrier(jnp.sum(onehot * logits[:, None, :], axis=-1))
    gate_weights = jax.nn.softmax(chosen, axis=-1)
    flat_expert = picked.reshape(-1).astype(jnp.int32)
    flat_hot = (flat_expert[:, None] == expert_row[None, :]).astype(jnp.int32)
    rank_rows = jnp.cumsum(flat_hot, axis=0).astype(jnp.int32) - flat_hot
    slot_index = lax.optimization_barrier(jnp.sum(rank_rows * flat_hot, axis=1)).astype(jnp.int32)
    buffers = jnp.zeros((EXPERTS, CAP, MODEL_WIDTH), jnp.float32).at[flat_expert, slot_index].set(jnp.repeat(normed_two, TOPK, axis=0))
    gate_linear = low_back(jnp.einsum('ecd,edf->ecf', buffers, gateup_full[:, 0], precision=highest))
    up_linear = low_back(jnp.einsum('ecd,edf->ecf', buffers, gateup_full[:, 1], precision=highest))
    activated = lower_precision(jax.nn.silu(gate_linear) * up_linear)
    expert_out = low_back(jnp.einsum('ecf,efd->ecd', activated, down_full, precision=highest))
    picked_rows = expert_out[flat_expert, slot_index].reshape(count_of_rows, TOPK, MODEL_WIDTH)
    mixture = lax.optimization_barrier(jnp.sum(gate_weights[:, :, None] * picked_rows, axis=1))
    return middle + alive_rows * mixture

def reference(tokens_in, cotangent, document_lengths, expert_choice, norm_gains, gains_first, gains_second, query_weight, query_first, query_second, keyvalue_weight, keyvalue_first_moment, keyvalue_second_moment, output_weight, output_first, output_second, router_weight, router_first, router_second, gateup_weight, gateup_first, gateup_second, down_weight, down_first, down_second):
    groups = document_lengths.shape[0]

    def forward(inputs, gains_in, query_in, keyval_in, output_in, router_in, gateup_in, down_in):
        lowered = (lower_precision(gains_in), lower_precision(query_in), lower_precision(keyval_in), lower_precision(output_in), lower_precision(router_in), lower_precision(gateup_in), lower_precision(down_in))

        def per_group(pieces):
            return group_forward(lowered, pieces[0], pieces[1], pieces[2])
        outputs = lax.map(jax.checkpoint(per_group), (inputs.reshape(groups, -1, MODEL_WIDTH), document_lengths, expert_choice.reshape(groups, -1, TOPK)))
        return outputs.reshape(-1, MODEL_WIDTH)
    result, pullback = jax.vjp(forward, tokens_in.astype(jnp.float32), norm_gains, query_weight, keyvalue_weight, output_weight, router_weight, gateup_weight, down_weight)
    gradients = pullback(cotangent.astype(jnp.float32))
    settings = ((norm_gains, gains_first, gains_second, gain_rate, 0.0), (query_weight, query_first, query_second, MODEL_WIDTH ** (-0.5), decay_rate), (keyvalue_weight, keyvalue_first_moment, keyvalue_second_moment, MODEL_WIDTH ** (-0.5), decay_rate), (output_weight, output_first, output_second, (QUERY_HEADS * HEAD_SIZE // 16) ** (-0.5), decay_rate), (router_weight, router_first, router_second, (4 * MODEL_WIDTH) ** (-0.5), decay_rate), (gateup_weight, gateup_first, gateup_second, MODEL_WIDTH ** (-0.5), decay_rate), (down_weight, down_first, down_second, (F // 16) ** (-0.5), decay_rate))
    updated = []
    for gradient, setting in zip(gradients[1:], settings):
        updated.extend(adamw_step(setting[0], setting[1], setting[2], gradient, setting[3], setting[4]))
    return (result.astype(jnp.bfloat16), gradients[0], updated[0], updated[1], updated[2], updated[3], updated[4], updated[5], updated[6], updated[7], updated[8], updated[9], updated[10], updated[11], updated[12], updated[13], updated[14], updated[15], updated[16], updated[17], updated[18], updated[19], updated[20])
```

```python
import functools
import math

import jax
import jax.numpy as jnp
from jax import lax
from jax.experimental import pallas as pl
from jax.experimental.pallas import tpu as pltpu
from jax.sharding import Mesh
from jax.sharding import PartitionSpec as P

MODEL_WIDTH = 1024
QUERY_HEADS = 16
KEYVALUE_HEADS = 8
HEAD_SIZE = 64
F = 512
TOPK = 8
EXPERTS = 16
ADAM_STEP = 5
GROUP = 8
LOCAL = EXPERTS // GROUP
EXTRA = 128
CHUNKS = 2
TILE = 512
SPAN = 256
LANES = 128
WIDTH = QUERY_HEADS * HEAD_SIZE
KV_WIDTH = KEYVALUE_HEADS * HEAD_SIZE
PROJECTED = WIDTH + 2 * KV_WIDTH
SCORE_SCALE = HEAD_SIZE ** (-0.5)
ROUTER_BLOCK = (PROJECTED + MODEL_WIDTH) // EXTRA


norm_eps = 1e-06
rope_base = 10000.0
beta_one = 0.9
beta_two = 0.95
adam_eps = 1e-08
decay_rate = 0.1
gain_rate = 0.25
masked_value = -1e30
brain_floating = jnp.bfloat16


def layout(lengths, count_of_rows):
    document_ends = jnp.cumsum(lengths)
    row_index = jnp.arange(count_of_rows, dtype=jnp.int32)
    passed = row_index[:, None] >= document_ends[None, :]
    segment = jnp.sum(passed.astype(jnp.int32), axis=1)
    start_row = jnp.sum(jnp.where(passed, lengths[None, :], 0), axis=1)
    position = (row_index - start_row).astype(jnp.float32)
    alive_mask = (segment < lengths.shape[0]).astype(jnp.float32)
    allowed = (segment[:, None] == segment[None, :]) & (row_index[None, :] <= row_index[:, None])
    return (position, alive_mask, allowed)


def rope_tables(position):
    half_width = HEAD_SIZE // 2
    exponents = jnp.arange(half_width, dtype=jnp.float32) * (2.0 / HEAD_SIZE)
    inverse = jnp.exp(exponents * -math.log(rope_base))
    angles = position[:, None] * inverse[None, :]
    cosine, sine = (jnp.cos(angles), jnp.sin(angles))
    return (
        jnp.concatenate([cosine] * 4, axis=1),
        jnp.concatenate([-sine, sine, -sine, sine], axis=1),
    )


def product(left, right):
    return jnp.dot(left, right, preferred_element_type=jnp.float32)


def times_transposed(left, right):
    return lax.dot_general(
        left, right, (((1,), (1,)), ((), ())), preferred_element_type=jnp.float32
    )


def transposed_times(left, right):
    return lax.dot_general(
        left, right, (((0,), (0,)), ((), ())), preferred_element_type=jnp.float32
    )


def normalize(values):
    inverse = lax.rsqrt(jnp.mean(values * values, axis=-1, keepdims=True) + norm_eps)
    return (values * inverse, inverse)


def norm_back(upstream, scaled_rows, inverse, gain_row):
    weighted = upstream * gain_row
    inner = jnp.mean(weighted * scaled_rows, axis=-1, keepdims=True)
    return inverse * (weighted - scaled_rows * inner)


def column_sums(values):
    ones = jnp.ones((values.shape[0], LANES), brain_floating)
    high = values.astype(brain_floating)
    low = (values - high.astype(jnp.float32)).astype(brain_floating)
    return transposed_times(high, ones) + transposed_times(low, ones)


def lanes_of(shape):
    return lax.broadcasted_iota(jnp.int32, shape, 1)


def rotate(values, cosine, sine):
    half = HEAD_SIZE // 2
    front = lax.rem(lanes_of(values.shape), HEAD_SIZE) < half
    swapped = jnp.where(
        front, pltpu.roll(values, LANES - half, 1), pltpu.roll(values, half, 1)
    )
    return values * cosine + swapped * sine


def both_halves(values, which):
    turned = pltpu.roll(values, HEAD_SIZE, 1)
    first = lanes_of(values.shape) < HEAD_SIZE
    return jnp.where(first == (which == 0), values, turned)


def only_half(values, which):
    first = lanes_of(values.shape) < HEAD_SIZE
    return jnp.where(first == (which == 0), values, 0.0)


def gates_of(rows, router, mask):
    logits = product(rows, router)
    peak = jnp.max(jnp.where(mask, logits, masked_value), axis=1, keepdims=True)
    weights = jnp.where(mask, jnp.exp(logits - peak), 0.0)
    return weights / jnp.sum(weights, axis=1, keepdims=True)


def adamw_step(weight, moment_old, square_old, gradient, step_rate, shrink):
    moment = beta_one * moment_old + (1.0 - beta_one) * gradient
    square = beta_two * square_old + (1.0 - beta_two) * gradient * gradient
    moment_hat = moment / (1.0 - beta_one**ADAM_STEP)
    square_hat = square / (1.0 - beta_two**ADAM_STEP)
    renewed = weight - step_rate * (
        moment_hat / (jnp.sqrt(square_hat) + adam_eps) + shrink * weight
    )
    return (moment, square, renewed)


MIB = 1024 * 1024
ANYWHERE = pl.BlockSpec(memory_space=pl.ANY)


def whole(shape):
    return pl.BlockSpec(shape, lambda *_: (0,) * len(shape), pipeline_mode=pl.Buffered(1))


def part(shape, place):
    return pl.BlockSpec(shape, lambda *_: place, pipeline_mode=pl.Buffered(1))


def out(shape, dtype):
    return jax.ShapeDtypeStruct(shape, dtype)


def split_kernel(gateup_ref, down_ref, out_ref):
    out_ref[0, 0, 0] = gateup_ref[0, 0].astype(brain_floating)
    out_ref[0, 0, 1] = gateup_ref[0, 1].astype(brain_floating)
    out_ref[0, 0, 2] = down_ref[0].T.astype(brain_floating)


def split_by_owner(gateup, down):
    shard = gateup.shape[2]
    return pl.pallas_call(
        split_kernel,
        grid=(EXPERTS,),
        in_specs=[
            pl.BlockSpec((1, 2, shard, F), lambda e: (e, 0, 0, 0)),
            pl.BlockSpec((1, F, shard), lambda e: (e, 0, 0)),
        ],
        out_specs=pl.BlockSpec(
            (1, 1, 3, shard, F), lambda e: (lax.rem(e, GROUP), e // GROUP, 0, 0, 0)
        ),
        out_shape=out((GROUP, LOCAL, 3, shard, F), brain_floating),
        name="split",
    )(gateup, down)


def front_kernel(
    x_ref, pack_ref, gains_ref, alive_ref, bias_ref, cos_ref, sin_ref, wait_ref,
    normed_ref, qkv_ref, mixed_ref, totals_ref, middle_ref, normed_two_ref, linear_ref,
):
    rows = x_ref.shape[0]
    scaled, _ = normalize(x_ref[...].astype(jnp.float32))
    normed = (scaled * gains_ref[0:1, :]).astype(brain_floating)
    normed_ref[...] = normed
    linear_ref[...] = product(normed, pack_ref[:, :PROJECTED])
    cosine, sine = (cos_ref[...], sin_ref[...])
    for at in range(0, WIDTH + KV_WIDTH, LANES):
        qkv_ref[:, at : at + LANES] = rotate(
            linear_ref[:, at : at + LANES], cosine, sine
        ).astype(brain_floating)
    qkv_ref[:, WIDTH + KV_WIDTH :] = linear_ref[:, WIDTH + KV_WIDTH :].astype(brain_floating)
    totals_ref[...] = jnp.zeros_like(totals_ref)

    @pl.loop(0, KEYVALUE_HEADS // 2)
    def _(pair):
        at = pl.multiple_of(pair * LANES, LANES)
        keys = qkv_ref[:, pl.ds(WIDTH + at, LANES)].astype(jnp.float32)
        values = qkv_ref[:, pl.ds(WIDTH + KV_WIDTH + at, LANES)].astype(jnp.float32)
        for a in range(2):
            head_keys = both_halves(keys, a).astype(brain_floating)
            head_values = both_halves(values, a)
            place = pl.multiple_of((2 * pair + a) * LANES, LANES)
            queries = qkv_ref[:, pl.ds(place, LANES)].astype(jnp.float32)
            for start in range(0, rows, SPAN):
                seen = min(start + SPAN, rows)
                mixed = jnp.zeros((SPAN, LANES), jnp.float32)
                for j in range(2):
                    head = 2 * (2 * pair + a) + j
                    query = only_half(queries[start : start + SPAN], j).astype(brain_floating)
                    scores = (
                        times_transposed(query, head_keys[:seen]) * SCORE_SCALE
                        + bias_ref[start : start + SPAN, :seen]
                    )
                    peak = jnp.max(scores, axis=1, keepdims=True)
                    weights = jnp.exp(scores - peak)
                    total = jnp.sum(weights, axis=1, keepdims=True)
                    probs = (weights * (1.0 / total)).astype(brain_floating)
                    mixed += product(probs, only_half(head_values[:seen], j).astype(brain_floating))
                    held = totals_ref[start : start + SPAN, :]
                    totals_ref[start : start + SPAN, :] = jnp.where(
                        lanes_of(held.shape) == head, peak + jnp.log(total), held
                    )
                mixed_ref[start : start + SPAN, pl.ds(place, LANES)] = mixed.astype(brain_floating)

    attended = product(mixed_ref[...], pack_ref[:, PROJECTED : PROJECTED + MODEL_WIDTH])
    middle = x_ref[...].astype(jnp.float32) + alive_ref[...] * attended
    middle_ref[...] = middle
    scaled_two, _ = normalize(middle)
    normed_two_ref[...] = (scaled_two * gains_ref[1:2, :]).astype(brain_floating)


def run_front(x, pack, gains, alive, bias, cosine, sine, wait):
    rows = x.shape[0]
    return pl.pallas_call(
        front_kernel,
        in_specs=[pl.BlockSpec(memory_space=pltpu.VMEM)] * 7 + [ANYWHERE],
        out_shape=[
            out((rows, MODEL_WIDTH), brain_floating),
            out((rows, PROJECTED), brain_floating),
            out((rows, WIDTH), brain_floating),
            out((rows, LANES), jnp.float32),
            out((rows, MODEL_WIDTH), jnp.float32),
            out((rows, MODEL_WIDTH), brain_floating),
        ],
        scratch_shapes=[pltpu.VMEM((rows, PROJECTED), jnp.float32)],
        compiler_params=pltpu.CompilerParams(vmem_limit_bytes=52 * MIB),
        name="front",
    )(x, pack, gains, alive, bias, cosine, sine, wait)


def middle_kernel(
    dx_one_ref, dx_two_ref, normed_two_ref, middle_ref, cot_ref, mask_ref, alive_ref, gains_ref,
    router_ref, output_ref, mixed_ref, wait_ref, d_middle_ref, d_mixed_ref, grads_ref,
):
    dx = jnp.concatenate([dx_one_ref[...], dx_two_ref[...]], axis=0).astype(jnp.float32)
    normed_two = normed_two_ref[...]
    mask = mask_ref[...].astype(jnp.float32) > 0.5
    gates = gates_of(normed_two, router_ref[...], mask)
    extra = dx[:, MODEL_WIDTH:]
    d_gates = extra + pltpu.roll(extra, LANES - EXPERTS, 1)
    d_logits = (
        gates * (d_gates - jnp.sum(gates * d_gates, axis=1, keepdims=True))
    ).astype(brain_floating)
    d_normed = dx[:, :MODEL_WIDTH] + times_transposed(d_logits, router_ref[...])
    scaled, inverse = normalize(middle_ref[...])
    d_middle = cot_ref[...].astype(jnp.float32) + norm_back(
        d_normed, scaled, inverse, gains_ref[1:2, :]
    )
    d_middle_ref[...] = d_middle
    d_attended = (alive_ref[...] * d_middle).astype(brain_floating)
    grads_ref[:, :MODEL_WIDTH] = transposed_times(mixed_ref[...], d_attended).astype(brain_floating)
    small = transposed_times(normed_two, d_logits)
    small = jnp.where(lanes_of(small.shape) == EXPERTS, column_sums(d_normed * scaled), small)
    grads_ref[:, MODEL_WIDTH:] = small.astype(brain_floating)
    d_mixed_ref[...] = times_transposed(d_attended, output_ref[...]).astype(brain_floating)


def run_middle(dx_one, dx_two, normed_two, middle, cot, mask, alive, gains, pack, mixed, wait):
    rows = middle.shape[0]
    full = [whole(v.shape) for v in (dx_one, dx_two, normed_two, middle, cot, mask, alive, gains)]
    return pl.pallas_call(
        middle_kernel,
        grid=(1,),
        in_specs=full
        + [
            part((MODEL_WIDTH, EXTRA), (0, ROUTER_BLOCK)),
            part((WIDTH, MODEL_WIDTH), (0, PROJECTED // MODEL_WIDTH)),
            whole(mixed.shape),
            ANYWHERE,
        ],
        out_specs=[
            whole((rows, MODEL_WIDTH)),
            whole((rows, WIDTH)),
            whole((MODEL_WIDTH, MODEL_WIDTH + EXTRA)),
        ],
        out_shape=[
            out((rows, MODEL_WIDTH), jnp.float32),
            out((rows, WIDTH), brain_floating),
            out((MODEL_WIDTH, MODEL_WIDTH + EXTRA), brain_floating),
        ],
        compiler_params=pltpu.CompilerParams(vmem_limit_bytes=52 * MIB),
        name="middle_back",
    )(dx_one, dx_two, normed_two, middle, cot, mask, alive, gains, pack, pack, mixed, wait)


def back_kernel(
    d_mixed_ref, qkv_ref, totals_ref, bias_ref, cos_ref, sin_ref, normed_ref, x_ref, d_middle_ref,
    gains_ref, pack_ref, wait_ref, grads_ref, d_input_ref, d_linear_ref, d_keys_ref, d_values_ref,
):
    rows = x_ref.shape[0]
    cosine, sine = (cos_ref[...], -sin_ref[...])

    @pl.loop(0, KEYVALUE_HEADS // 2)
    def _(pair):
        at = pl.multiple_of(pair * LANES, LANES)
        keys = qkv_ref[:, pl.ds(WIDTH + at, LANES)].astype(jnp.float32)
        values = qkv_ref[:, pl.ds(WIDTH + KV_WIDTH + at, LANES)].astype(jnp.float32)
        pair_keys = jnp.zeros((rows, LANES), jnp.float32)
        pair_values = jnp.zeros((rows, LANES), jnp.float32)
        for a in range(2):
            both_keys = both_halves(keys, a)
            head_keys = both_keys.astype(brain_floating)
            head_values = both_halves(values, a).astype(brain_floating)
            place = pl.multiple_of((2 * pair + a) * LANES, LANES)
            queries = qkv_ref[:, pl.ds(place, LANES)].astype(jnp.float32)
            d_outs = d_mixed_ref[:, pl.ds(place, LANES)].astype(jnp.float32)
            d_keys_ref[...] = jnp.zeros_like(d_keys_ref)
            d_values_ref[...] = jnp.zeros_like(d_values_ref)
            for start in range(0, rows, SPAN):
                seen = min(start + SPAN, rows)
                d_query = jnp.zeros((SPAN, LANES), jnp.float32)
                for j in range(2):
                    head = 2 * (2 * pair + a) + j
                    query = only_half(queries[start : start + SPAN], j).astype(brain_floating)
                    d_out = only_half(d_outs[start : start + SPAN], j).astype(brain_floating)
                    held = totals_ref[start : start + SPAN, :]
                    total = jnp.sum(
                        jnp.where(lanes_of(held.shape) == head, held, 0.0), axis=1, keepdims=True
                    )
                    scores = (
                        times_transposed(query, head_keys[:seen]) * SCORE_SCALE
                        + bias_ref[start : start + SPAN, :seen]
                    )
                    probs = jnp.exp(scores - total)
                    d_probs = times_transposed(d_out, head_values[:seen])
                    inner = jnp.sum(probs * d_probs, axis=1, keepdims=True)
                    d_scores = (probs * (d_probs - inner)).astype(brain_floating)
                    d_query += product(
                        d_scores, only_half(both_keys[:seen], j).astype(brain_floating)
                    )
                    d_keys_ref[:seen, :] += transposed_times(d_scores, query)
                    d_values_ref[:seen, :] += transposed_times(probs.astype(brain_floating), d_out)
                d_linear_ref[start : start + SPAN, pl.ds(place, LANES)] = rotate(
                    d_query * SCORE_SCALE,
                    cosine[start : start + SPAN],
                    sine[start : start + SPAN],
                ).astype(brain_floating)
            d_keys = d_keys_ref[...]
            d_values = d_values_ref[...]
            pair_keys += only_half(d_keys + pltpu.roll(d_keys, HEAD_SIZE, 1), a)
            pair_values += only_half(d_values + pltpu.roll(d_values, HEAD_SIZE, 1), a)
        d_linear_ref[:, pl.ds(WIDTH + at, LANES)] = rotate(
            pair_keys * SCORE_SCALE, cosine, sine
        ).astype(brain_floating)
        d_linear_ref[:, pl.ds(WIDTH + KV_WIDTH + at, LANES)] = pair_values.astype(brain_floating)

    normed = normed_ref[...]
    for at in range(0, PROJECTED, 512):
        grads_ref[:, at : at + 512] = transposed_times(
            normed, d_linear_ref[:, at : at + 512]
        ).astype(brain_floating)
    d_normed = times_transposed(d_linear_ref[...], pack_ref[...])
    scaled, inverse = normalize(x_ref[...].astype(jnp.float32))
    sums = column_sums(d_normed * scaled)
    grads_ref[:, PROJECTED:] = jnp.where(lanes_of(sums.shape) == 0, sums, 0.0).astype(
        brain_floating
    )
    d_input_ref[...] = d_middle_ref[...] + norm_back(d_normed, scaled, inverse, gains_ref[0:1, :])


def run_back(d_mixed, qkv, totals, bias, cosine, sine, normed, x, d_middle, gains, pack, wait):
    rows = x.shape[0]
    held = (d_mixed, qkv, totals, bias, cosine, sine, normed, x, d_middle, gains)
    return pl.pallas_call(
        back_kernel,
        grid=(1,),
        in_specs=[whole(v.shape) for v in held]
        + [part((MODEL_WIDTH, PROJECTED), (0, 0)), ANYWHERE],
        out_specs=[whole((MODEL_WIDTH, PROJECTED + EXTRA)), whole((rows, MODEL_WIDTH))],
        out_shape=[
            out((MODEL_WIDTH, PROJECTED + EXTRA), brain_floating),
            out((rows, MODEL_WIDTH), jnp.float32),
        ],
        scratch_shapes=[
            pltpu.VMEM((rows, PROJECTED), brain_floating),
            pltpu.VMEM((rows, LANES), jnp.float32),
            pltpu.VMEM((rows, LANES), jnp.float32),
        ],
        compiler_params=pltpu.CompilerParams(vmem_limit_bytes=52 * MIB),
        name="attention_back",
    )(*held, pack, wait)


def expert_kernel(me_ref, x_ref, b_ref, w_ref, router_ref, ga_ref, dgu_ref, dx_ref):
    x = x_ref[...]
    branch = b_ref[:, :MODEL_WIDTH]
    mask = b_ref[:, MODEL_WIDTH:].astype(jnp.float32) > 0.5
    gates = gates_of(x, router_ref[...], mask)
    lane = lanes_of(gates.shape)
    d_gates = jnp.zeros_like(gates)
    dx = jnp.zeros((x.shape[0], MODEL_WIDTH), jnp.float32)
    for local in range(LOCAL):
        expert = me_ref[0] + GROUP * local
        gate_weight, up_weight, down_weight = (
            w_ref[:, local, p].reshape(MODEL_WIDTH, F) for p in range(3)
        )
        gate = jnp.sum(jnp.where(lane == expert, gates, 0.0), axis=1, keepdims=True)
        gate_linear = product(x, gate_weight)
        up_linear = product(x, up_weight)
        back = product(branch, down_weight)
        sig = jax.nn.sigmoid(gate_linear)
        silu = gate_linear * sig
        act = silu * up_linear
        ga_ref[:, local * F : (local + 1) * F] = (gate * act).astype(brain_floating)
        d_gate = jnp.sum(act * back, axis=1, keepdims=True)
        high = d_gate.astype(brain_floating).astype(jnp.float32)
        d_gates += jnp.where(lane == expert, high, 0.0)
        d_gates += jnp.where(lane == expert + EXPERTS, d_gate - high, 0.0)
        d_act = gate * back
        d_gl = (d_act * up_linear * (sig + silu * (1.0 - sig))).astype(brain_floating)
        d_ul = (d_act * silu).astype(brain_floating)
        dgu_ref[:, 2 * local * F : (2 * local + 1) * F] = d_gl
        dgu_ref[:, (2 * local + 1) * F : (2 * local + 2) * F] = d_ul
        dx += times_transposed(d_gl, gate_weight) + times_transposed(d_ul, up_weight)
    dx_ref[:, :MODEL_WIDTH] = dx.astype(brain_floating)
    dx_ref[:, MODEL_WIDTH:] = d_gates.astype(brain_floating)


def run_experts(me, x, b, weights, pack):
    rows = x.shape[0]
    tile = min(TILE, rows)
    wide = MODEL_WIDTH + EXTRA

    def rowed(width):
        return pl.BlockSpec((tile, width), lambda i, me_ref: (i, 0))

    return pl.pallas_call(
        expert_kernel,
        grid_spec=pltpu.PrefetchScalarGridSpec(
            num_scalar_prefetch=1,
            grid=(rows // tile,),
            in_specs=[
                rowed(MODEL_WIDTH),
                rowed(wide),
                whole(weights.shape),
                part((MODEL_WIDTH, EXTRA), (0, ROUTER_BLOCK)),
            ],
            out_specs=[rowed(LOCAL * F), rowed(2 * LOCAL * F), rowed(wide)],
        ),
        out_shape=[
            out((rows, LOCAL * F), brain_floating),
            out((rows, 2 * LOCAL * F), brain_floating),
            out((rows, wide), brain_floating),
        ],
        compiler_params=pltpu.CompilerParams(vmem_limit_bytes=56 * MIB),
        name="experts",
    )(me, x, b, weights, pack)


def chunked_specs(count, tile, steps, width, column):
    def index(c):
        return lambda i, *_: (jnp.clip(i - c * steps, 0, steps - 1), column)

    return [pl.BlockSpec((tile, width), index(c)) for c in range(count)]


def grads_kernel(steps, *refs):
    ins, wait_ref, outs, sums = (refs[:-7], refs[-7], refs[-6:-3], refs[-3:])
    i = pl.program_id(0)

    @pl.when(i == 0)
    def _():
        for total in sums:
            total[...] = jnp.zeros_like(total)

    for c in range(CHUNKS):

        @pl.when(i // steps == c)
        def _():
            x_ref, b_ref, ga_ref, dgu_ref = ins[4 * c : 4 * c + 4]
            x = x_ref[...]
            sums[0][...] += transposed_times(x, dgu_ref[:, :F])
            sums[1][...] += transposed_times(x, dgu_ref[:, F:])
            sums[2][...] += transposed_times(b_ref[...], ga_ref[...])

    @pl.when(i == CHUNKS * steps - 1)
    def _():
        for result, total in zip(outs, sums):
            result[...] = total[...].astype(brain_floating)


def run_grads(local, xs, bs, gas, dgus, wait):
    tile = min(TILE, xs[0].shape[0])
    steps = xs[0].shape[0] // tile
    columns = (
        chunked_specs(CHUNKS, tile, steps, MODEL_WIDTH, 0),
        chunked_specs(CHUNKS, tile, steps, MODEL_WIDTH, 0),
        chunked_specs(CHUNKS, tile, steps, F, local),
        chunked_specs(CHUNKS, tile, steps, 2 * F, local),
    )
    return pl.pallas_call(
        functools.partial(grads_kernel, steps),
        grid=(CHUNKS * steps,),
        in_specs=[columns[k][c] for c in range(CHUNKS) for k in range(4)] + [ANYWHERE],
        out_specs=[whole((MODEL_WIDTH, F))] * 3,
        out_shape=[out((MODEL_WIDTH, F), brain_floating)] * 3,
        scratch_shapes=[pltpu.VMEM((MODEL_WIDTH, F), jnp.float32)] * 3,
        compiler_params=pltpu.CompilerParams(vmem_limit_bytes=52 * MIB),
        name="grads",
    )(*[v[c] for c in range(CHUNKS) for v in (xs, bs, gas, dgus)], wait)


def mix_kernel(steps, *refs):
    gas, w_ref, out_ref = (refs[:CHUNKS], refs[CHUNKS], refs[-1])
    i = pl.program_id(0)
    for c in range(CHUNKS):

        @pl.when(i // steps == c)
        def _():
            total = jnp.zeros((gas[c].shape[0], MODEL_WIDTH), jnp.float32)
            for local in range(LOCAL):
                total += times_transposed(
                    gas[c][:, local * F : (local + 1) * F],
                    w_ref[:, local, 0].reshape(MODEL_WIDTH, F),
                )
            out_ref[0] = total.astype(brain_floating)


def run_mix(gas, weights, wait):
    rows = gas[0].shape[0]
    tile = min(TILE, rows)
    steps = rows // tile
    blocks, _, _, shard, _ = weights.shape
    return pl.pallas_call(
        functools.partial(mix_kernel, steps),
        grid=(CHUNKS * steps,),
        in_specs=chunked_specs(CHUNKS, tile, steps, LOCAL * F, 0)
        + [part((blocks, LOCAL, 1, shard, F), (0, 0, 2, 0, 0)), ANYWHERE],
        out_specs=pl.BlockSpec(
            (1, tile, MODEL_WIDTH), lambda i: (i // steps, lax.rem(i, steps), 0)
        ),
        out_shape=out((CHUNKS, rows, MODEL_WIDTH), brain_floating),
        compiler_params=pltpu.CompilerParams(vmem_limit_bytes=52 * MIB),
        name="mixture",
    )(*gas, weights, wait)


def sums_kernel(count, waits, *refs):
    ins, outs = (refs[: 2 * count], refs[2 * count + waits :])
    for k in range(count):
        left, right = (ins[2 * k][...], ins[2 * k + 1][...])
        outs[k][...] = (left.astype(jnp.float32) + right.astype(jnp.float32)).astype(
            brain_floating
        )


def run_sums(pairs, waits):
    flat = [v for pair in pairs for v in pair]
    return pl.pallas_call(
        functools.partial(sums_kernel, len(pairs), len(waits)),
        in_specs=[pl.BlockSpec(memory_space=pltpu.VMEM)] * len(flat) + [ANYWHERE] * len(waits),
        out_shape=[out(pair[0].shape, brain_floating) for pair in pairs],
        compiler_params=pltpu.CompilerParams(vmem_limit_bytes=40 * MIB),
        name="sums",
    )(*flat, *waits)


def adam_kernel(turned, rate, shrink, place_ref, t_ref, r_ref, w_ref, m_ref, v_ref, *rest):
    m_out, v_out, w_out = rest[-3:]
    inner = (place_ref[0] == 1) | (place_ref[0] == 2)
    for k in range(t_ref.shape[0]):
        gradient = jnp.where(inner, t_ref[k].astype(jnp.float32), r_ref[k].astype(jnp.float32))
        if turned:
            at = (k,)
            gradient = gradient.T
        else:
            at = (k, 0)
        moment, square, renewed = adamw_step(
            w_ref[at], m_ref[at], v_ref[at], gradient, rate, shrink
        )
        m_out[at] = moment
        v_out[at] = square
        w_out[at] = renewed


def adam_part(place, total, ends, state, local, side, rate, before, wait):
    weight, first, second = state
    turned = side == 2
    shard = total.shape[1]
    held = [] if before is None else list(before)
    if turned:
        spec = pl.BlockSpec((2, F, shard), lambda i, _: (i + local * (GROUP // 2), 0, 0))
    else:
        spec = pl.BlockSpec((2, 1, shard, F), lambda i, _: (i + local * (GROUP // 2), side, 0, 0))
    piece = pl.BlockSpec((2, shard, F), lambda i, _: (i, 0, 0))
    return pl.pallas_call(
        functools.partial(adam_kernel, turned, rate, decay_rate),
        grid_spec=pltpu.PrefetchScalarGridSpec(
            num_scalar_prefetch=1,
            grid=(GROUP // 2,),
            in_specs=[piece, piece, spec, spec, spec] + [ANYWHERE] * (len(held) + 1),
            out_specs=[spec] * 3,
        ),
        out_shape=[out(weight.shape, jnp.float32)] * 3,
        input_output_aliases={6 + i: i for i in range(len(held))},
        compiler_params=pltpu.CompilerParams(vmem_limit_bytes=40 * MIB),
        name="adam",
    )(place, total, ends, weight, first, second, *held, wait)


fsdp = ("outer", "inner")


def body(
    sizes,
    tokens_in,
    cotangent,
    document_lengths,
    expert_choice,
    norm_gains,
    gains_first,
    gains_second,
    query_weight,
    query_first,
    query_second,
    keyvalue_weight,
    keyvalue_first_moment,
    keyvalue_second_moment,
    output_weight,
    output_first,
    output_second,
    router_weight,
    router_first,
    router_second,
    gateup_weight,
    gateup_first,
    gateup_second,
    down_weight,
    down_first,
    down_second,
):
    replicas, outer = sizes
    count_of_rows = tokens_in.shape[0]
    shard = query_weight.shape[0]
    me = lax.axis_index("inner").astype(jnp.int32).reshape(1)
    place = lax.axis_index("replica").astype(jnp.int32).reshape(1)

    pack_own = jnp.concatenate(
        [
            query_weight,
            keyvalue_weight[0],
            keyvalue_weight[1],
            output_weight,
            router_weight,
            norm_gains.T,
            jnp.zeros((shard, EXTRA - EXPERTS - 2), jnp.float32),
        ],
        axis=1,
    ).astype(brain_floating)
    pack = lax.all_gather(pack_own, fsdp, axis=0, tiled=True)
    at = PROJECTED + MODEL_WIDTH + EXPERTS
    gains_value = pack[:, at : at + 2].astype(jnp.float32).T

    weights = lax.all_to_all(split_by_owner(gateup_weight, down_weight), "inner", 0, 0)
    if outer > 1:
        weights = lax.all_gather(weights, "outer", axis=0, tiled=True)

    position, alive_mask, allowed = layout(document_lengths[0], count_of_rows)
    cosine, sine = rope_tables(position)
    alive = alive_mask[:, None]
    bias = jnp.where(allowed, 0.0, masked_value)

    expert_row = jnp.arange(EXPERTS, dtype=jnp.int32)
    chosen = jnp.any(expert_choice[:, :, None] == expert_row[None, None, :], axis=1)
    mask = jnp.concatenate(
        [
            chosen.astype(brain_floating),
            jnp.zeros((count_of_rows, EXTRA - EXPERTS), brain_floating),
        ],
        axis=1,
    )
    branch = (alive * cotangent.astype(jnp.float32)).astype(brain_floating)
    branch_pack = jnp.concatenate([branch, mask], axis=1)
    part_rows = count_of_rows // CHUNKS

    def gathered(values, c):
        return lax.all_gather(
            values[c * part_rows : (c + 1) * part_rows], "inner", axis=0, tiled=True
        )

    branch_all = [gathered(branch_pack, c) for c in range(CHUNKS)]

    normed, qkv, mixed, totals, middle, normed_two = run_front(
        tokens_in, pack, gains_value, alive, bias, cosine, sine, weights
    )

    x_all, ga_all, dgu_all, dx_parts = ([], [], [], [])
    for c in range(CHUNKS):
        x_part = gathered(normed_two, c)
        ga, dgu, dx = run_experts(me, x_part, branch_all[c], weights, pack)
        x_all.append(x_part)
        ga_all.append(ga)
        dgu_all.append(dgu)
        dx_parts.append(lax.psum_scatter(dx, "inner", scatter_dimension=0, tiled=True))

    def to_owner(grad):
        parts = grad.reshape(GROUP * outer, shard, F)
        if outer > 1:
            parts = lax.psum_scatter(parts, "outer", scatter_dimension=0, tiled=True)
        return lax.all_to_all(parts, "inner", 0, 0)

    def inward(values):
        return lax.ppermute(values, "replica", [(0, 1), (3, 2)])

    def across(values):
        return lax.ppermute(values, "replica", [(1, 2), (2, 1)])

    def outward(values):
        return lax.ppermute(values, "replica", [(1, 0), (2, 3)])

    grads = [list(run_grads(0, x_all, branch_all, ga_all, dgu_all, dgu_all[-1])), None]
    queue = {0: (to_owner(grads[0][0]),)}
    gateup_new, down_new = (None, None)
    held = {"token": grads[0][0]}
    halves, sums, ends = ({}, {}, {})
    root = MODEL_WIDTH ** (-0.5)
    gateup_state = (gateup_weight, gateup_first, gateup_second)
    down_state = (down_weight, down_first, down_second)

    def adam_of(k, wait):
        nonlocal gateup_new, down_new
        local, side = divmod(k, 3)
        if side == 2:
            down_new = adam_part(
                place, sums[k][0], ends[k][0], down_state, local, side, (F // 16) ** (-0.5),
                down_new, wait,
            )
            return down_new[0]
        gateup_new = adam_part(
            place, sums[k][0], ends[k][0], gateup_state, local, side, root, gateup_new, wait
        )
        return gateup_new[0]

    count = 3 * LOCAL + 1
    token = grads[0][2]
    for k in range(-1, count + 2):
        arrived, waits = ([], [])
        if k in queue:
            halves[k] = tuple(inward(v) for v in queue[k])
            arrived += list(zip(queue[k], halves[k]))
        if k - 1 in queue:
            crossed = tuple(across(v) for v in sums[k - 1])
            arrived += list(zip(sums[k - 1], crossed))
        if k - 2 in queue:
            ends[k - 2] = tuple(outward(v) for v in sums[k - 2])
            waits += list(ends[k - 2])
        if 0 <= k + 1 < 3 * LOCAL and k + 1 not in queue:
            local, side = divmod(k + 1, 3)
            queue[k + 1] = (to_owner(grads[local][side]),)
        if k + 1 in queue:
            waits += list(queue[k + 1])

        if k == -1:
            grads[1] = list(run_grads(1, x_all, branch_all, ga_all, dgu_all, token))
            waits += [grads[1][0]]
        elif k == 0:
            mixture = run_mix(ga_all, weights, token)
            waits += [mixture]
        elif k == 1:
            d_middle, d_mixed, second_grads = run_middle(
                dx_parts[0], dx_parts[1], normed_two, middle, cotangent, mask, alive, gains_value,
                pack, mixed, token,
            )
            second_part = lax.psum_scatter(second_grads, fsdp, scatter_dimension=0, tiled=True)
            waits += [d_mixed]
        elif k == 2:
            first_grads, input_gradient = run_back(
                d_mixed, qkv, totals, bias, cosine, sine, normed, tokens_in, d_middle, gains_value,
                pack, token,
            )
            first_part = lax.psum_scatter(first_grads, fsdp, scatter_dimension=0, tiled=True)
            queue[count - 1] = (first_part, second_part)
            waits += [input_gradient]
        elif k - 3 in ends and k - 3 < 3 * LOCAL:
            waits += [adam_of(k - 3, token)]

        if not arrived:
            continue
        results = run_sums(arrived, waits)
        token = results[0]
        if k in queue:
            size = len(queue[k])
            sums[k] = None
            halves[k], results = (tuple(results[:size]), results[size:])
        if k - 1 in queue:
            crossed_sums = tuple(results)
        if k - 1 in queue:
            sums[k - 1] = crossed_sums
        if k in queue:
            sums[k] = halves[k]
    for k in range(3 * LOCAL):
        if k + 3 > count + 1:
            adam_of(k, token)

    mixture_own = lax.psum_scatter(mixture, "inner", scatter_dimension=1, tiled=True)
    mixture_own = mixture_own.reshape(count_of_rows, MODEL_WIDTH).astype(jnp.float32)
    block_output = (middle + alive * mixture_own).astype(brain_floating)

    inner = (place[0] == 1) | (place[0] == 2)
    first_sum, second_sum = (
        jnp.where(inner, total, end).astype(jnp.float32)
        for total, end in zip(sums[count - 1], ends[count - 1])
    )
    gains_part = jnp.stack([first_sum[:, PROJECTED], second_sum[:, MODEL_WIDTH + EXPERTS]])
    keyval_part = jnp.stack(
        [first_sum[:, WIDTH : WIDTH + KV_WIDTH], first_sum[:, WIDTH + KV_WIDTH : PROJECTED]]
    )
    settings = (
        (gains_part, norm_gains, gains_first, gains_second, gain_rate, 0.0),
        (first_sum[:, :WIDTH], query_weight, query_first, query_second, root, decay_rate),
        (
            keyval_part,
            keyvalue_weight,
            keyvalue_first_moment,
            keyvalue_second_moment,
            root,
            decay_rate,
        ),
        (
            second_sum[:, :MODEL_WIDTH],
            output_weight,
            output_first,
            output_second,
            (WIDTH // 16) ** (-0.5),
            decay_rate,
        ),
        (
            second_sum[:, MODEL_WIDTH : MODEL_WIDTH + EXPERTS],
            router_weight,
            router_first,
            router_second,
            (4 * MODEL_WIDTH) ** (-0.5),
            decay_rate,
        ),
    )
    updated = []
    for gradient, weight, first, second, rate, shrink in settings:
        updated.extend(adamw_step(weight, first, second, gradient, rate, shrink))
    return (block_output, input_gradient) + tuple(updated) + tuple(gateup_new) + tuple(down_new)


def solution(mesh):
    replicas, shards = (mesh.shape["replica"], mesh.shape["fsdp"])
    outer = shards // GROUP
    split = Mesh(mesh.devices.reshape(replicas, outer, GROUP), ("replica",) + fsdp)
    rows = P(("replica",) + fsdp, None)
    by_first = P(fsdp, None)
    by_second = P(None, fsdp)
    by_middle = P(None, fsdp, None)
    by_third = P(None, None, fsdp, None)
    by_last = P(None, None, fsdp)
    weights = (by_second, by_first, by_middle, by_first, by_first, by_third, by_last)
    states = tuple(spec for spec in weights for _ in range(3))
    return jax.shard_map(
        functools.partial(body, (replicas, outer)),
        mesh=split,
        in_specs=(rows,) * 4 + states,
        out_specs=(rows,) * 2 + states,
        check_vma=False,
    )
```

```python
import functools
import math

import jax
import jax.numpy as jnp
from jax import lax
from jax.experimental import pallas as pl
from jax.experimental.pallas import tpu as pltpu
from jax.sharding import Mesh
from jax.sharding import PartitionSpec as P

MODEL_WIDTH = 1024
QUERY_HEADS = 16
KEYVALUE_HEADS = 8
HEAD_SIZE = 64
F = 512
TOPK = 8
EXPERTS = 16
ADAM_STEP = 5
GROUP = 8
LOCAL = EXPERTS // GROUP
EXTRA = 128
CHUNKS = 2
TILE = 512
SPAN = 256
LANES = 128
WIDTH = QUERY_HEADS * HEAD_SIZE
KV_WIDTH = KEYVALUE_HEADS * HEAD_SIZE
PROJECTED = WIDTH + 2 * KV_WIDTH
SCORE_SCALE = HEAD_SIZE ** (-0.5)
ROUTER_BLOCK = (PROJECTED + MODEL_WIDTH) // EXTRA


norm_eps = 1e-06
rope_base = 10000.0
beta_one = 0.9
beta_two = 0.95
adam_eps = 1e-08
decay_rate = 0.1
gain_rate = 0.25
masked_value = -1e30
brain_floating = jnp.bfloat16


def layout(lengths, count_of_rows):
    document_ends = jnp.cumsum(lengths)
    row_index = jnp.arange(count_of_rows, dtype=jnp.int32)
    passed = row_index[:, None] >= document_ends[None, :]
    segment = jnp.sum(passed.astype(jnp.int32), axis=1)
    start_row = jnp.sum(jnp.where(passed, lengths[None, :], 0), axis=1)
    position = (row_index - start_row).astype(jnp.float32)
    alive_mask = (segment < lengths.shape[0]).astype(jnp.float32)
    allowed = (segment[:, None] == segment[None, :]) & (row_index[None, :] <= row_index[:, None])
    return (position, alive_mask, allowed)


def rope_tables(position):
    half_width = HEAD_SIZE // 2
    exponents = jnp.arange(half_width, dtype=jnp.float32) * (2.0 / HEAD_SIZE)
    inverse = jnp.exp(exponents * -math.log(rope_base))
    angles = position[:, None] * inverse[None, :]
    cosine, sine = (jnp.cos(angles), jnp.sin(angles))
    return (
        jnp.concatenate([cosine] * 4, axis=1),
        jnp.concatenate([-sine, sine, -sine, sine], axis=1),
    )


def product(left, right):
    return jnp.dot(left, right, preferred_element_type=jnp.float32)


def times_transposed(left, right):
    return lax.dot_general(
        left, right, (((1,), (1,)), ((), ())), preferred_element_type=jnp.float32
    )


def transposed_times(left, right):
    return lax.dot_general(
        left, right, (((0,), (0,)), ((), ())), preferred_element_type=jnp.float32
    )


def normalize(values):
    inverse = lax.rsqrt(jnp.mean(values * values, axis=-1, keepdims=True) + norm_eps)
    return (values * inverse, inverse)


def norm_back(upstream, scaled_rows, inverse, gain_row):
    weighted = upstream * gain_row
    inner = jnp.mean(weighted * scaled_rows, axis=-1, keepdims=True)
    return inverse * (weighted - scaled_rows * inner)


def column_sums(values):
    ones = jnp.ones((values.shape[0], LANES), brain_floating)
    high = values.astype(brain_floating)
    low = (values - high.astype(jnp.float32)).astype(brain_floating)
    return transposed_times(high, ones) + transposed_times(low, ones)


def lanes_of(shape):
    return lax.broadcasted_iota(jnp.int32, shape, 1)


def rotate(values, cosine, sine):
    half = HEAD_SIZE // 2
    front = lax.rem(lanes_of(values.shape), HEAD_SIZE) < half
    swapped = jnp.where(
        front, pltpu.roll(values, LANES - half, 1), pltpu.roll(values, half, 1)
    )
    return values * cosine + swapped * sine


def both_halves(values, which):
    turned = pltpu.roll(values, HEAD_SIZE, 1)
    first = lanes_of(values.shape) < HEAD_SIZE
    return jnp.where(first == (which == 0), values, turned)


def only_half(values, which):
    first = lanes_of(values.shape) < HEAD_SIZE
    return jnp.where(first == (which == 0), values, 0.0)


def gates_of(rows, router, mask):
    logits = product(rows, router)
    peak = jnp.max(jnp.where(mask, logits, masked_value), axis=1, keepdims=True)
    weights = jnp.where(mask, jnp.exp(logits - peak), 0.0)
    return weights / jnp.sum(weights, axis=1, keepdims=True)


def adamw_step(weight, moment_old, square_old, gradient, step_rate, shrink):
    moment = beta_one * moment_old + (1.0 - beta_one) * gradient
    square = beta_two * square_old + (1.0 - beta_two) * gradient * gradient
    moment_hat = moment / (1.0 - beta_one**ADAM_STEP)
    square_hat = square / (1.0 - beta_two**ADAM_STEP)
    renewed = weight - step_rate * (
        moment_hat / (jnp.sqrt(square_hat) + adam_eps) + shrink * weight
    )
    return (moment, square, renewed)


MIB = 1024 * 1024
ANYWHERE = pl.BlockSpec(memory_space=pl.ANY)


def takes(microseconds):
    return pl.CostEstimate(
        flops=int(microseconds * 1e9), bytes_accessed=int(microseconds * 3.6e6), transcendentals=0
    )


def whole(shape):
    return pl.BlockSpec(shape, lambda *_: (0,) * len(shape), pipeline_mode=pl.Buffered(1))


def part(shape, place):
    return pl.BlockSpec(shape, lambda *_: place, pipeline_mode=pl.Buffered(1))


def out(shape, dtype):
    return jax.ShapeDtypeStruct(shape, dtype)


def split_kernel(gateup_ref, down_ref, out_ref):
    for k in range(2):
        out_ref[k, 0, 0] = gateup_ref[k, 0].astype(brain_floating)
        out_ref[k, 0, 1] = gateup_ref[k, 1].astype(brain_floating)
        out_ref[k, 0, 2] = down_ref[k].T.astype(brain_floating)


def split_by_owner(gateup, down):
    shard = gateup.shape[2]
    steps = GROUP // 2
    return pl.pallas_call(
        split_kernel,
        grid=(EXPERTS // 2,),
        in_specs=[
            pl.BlockSpec((2, 2, shard, F), lambda e: (e, 0, 0, 0)),
            pl.BlockSpec((2, F, shard), lambda e: (e, 0, 0)),
        ],
        out_specs=pl.BlockSpec(
            (2, 1, 3, shard, F), lambda e: (lax.rem(e, steps), e // steps, 0, 0, 0)
        ),
        out_shape=out((GROUP, LOCAL, 3, shard, F), brain_floating),
        name="split",
    )(gateup, down)


def front_kernel(
    x_ref, pack_ref, gains_ref, alive_ref, bias_ref, cos_ref, sin_ref, wait_ref,
    normed_ref, qkv_ref, mixed_ref, totals_ref, middle_ref, normed_two_ref, linear_ref,
):
    rows = x_ref.shape[0]
    scaled, _ = normalize(x_ref[...].astype(jnp.float32))
    normed = (scaled * gains_ref[0:1, :]).astype(brain_floating)
    normed_ref[...] = normed
    linear_ref[...] = product(normed, pack_ref[:, :PROJECTED])
    cosine, sine = (cos_ref[...], sin_ref[...])
    for at in range(0, WIDTH + KV_WIDTH, LANES):
        qkv_ref[:, at : at + LANES] = rotate(
            linear_ref[:, at : at + LANES], cosine, sine
        ).astype(brain_floating)
    qkv_ref[:, WIDTH + KV_WIDTH :] = linear_ref[:, WIDTH + KV_WIDTH :].astype(brain_floating)
    totals_ref[...] = jnp.zeros_like(totals_ref)

    @pl.loop(0, KEYVALUE_HEADS // 2)
    def _(pair):
        at = pl.multiple_of(pair * LANES, LANES)
        keys = qkv_ref[:, pl.ds(WIDTH + at, LANES)].astype(jnp.float32)
        values = qkv_ref[:, pl.ds(WIDTH + KV_WIDTH + at, LANES)].astype(jnp.float32)
        for a in range(2):
            head_keys = both_halves(keys, a).astype(brain_floating)
            head_values = both_halves(values, a)
            place = pl.multiple_of((2 * pair + a) * LANES, LANES)
            queries = qkv_ref[:, pl.ds(place, LANES)].astype(jnp.float32)
            for start in range(0, rows, SPAN):
                seen = min(start + SPAN, rows)
                mixed = jnp.zeros((SPAN, LANES), jnp.float32)
                for j in range(2):
                    head = 2 * (2 * pair + a) + j
                    query = only_half(queries[start : start + SPAN], j).astype(brain_floating)
                    scores = (
                        times_transposed(query, head_keys[:seen]) * SCORE_SCALE
                        + bias_ref[start : start + SPAN, :seen]
                    )
                    peak = jnp.max(scores, axis=1, keepdims=True)
                    weights = jnp.exp(scores - peak)
                    total = jnp.sum(weights, axis=1, keepdims=True)
                    probs = (weights * (1.0 / total)).astype(brain_floating)
                    mixed += product(probs, only_half(head_values[:seen], j).astype(brain_floating))
                    held = totals_ref[start : start + SPAN, :]
                    totals_ref[start : start + SPAN, :] = jnp.where(
                        lanes_of(held.shape) == head, peak + jnp.log(total), held
                    )
                mixed_ref[start : start + SPAN, pl.ds(place, LANES)] = mixed.astype(brain_floating)

    attended = product(mixed_ref[...], pack_ref[:, PROJECTED : PROJECTED + MODEL_WIDTH])
    middle = x_ref[...].astype(jnp.float32) + alive_ref[...] * attended
    middle_ref[...] = middle
    scaled_two, _ = normalize(middle)
    normed_two_ref[...] = (scaled_two * gains_ref[1:2, :]).astype(brain_floating)


def run_front(x, pack, gains, alive, bias, cosine, sine, wait):
    rows = x.shape[0]
    return pl.pallas_call(
        front_kernel,
        in_specs=[pl.BlockSpec(memory_space=pltpu.VMEM)] * 7 + [ANYWHERE],
        out_shape=[
            out((rows, MODEL_WIDTH), brain_floating),
            out((rows, PROJECTED), brain_floating),
            out((rows, WIDTH), brain_floating),
            out((rows, LANES), jnp.float32),
            out((rows, MODEL_WIDTH), jnp.float32),
            out((rows, MODEL_WIDTH), brain_floating),
        ],
        scratch_shapes=[pltpu.VMEM((rows, PROJECTED), jnp.float32)],
        compiler_params=pltpu.CompilerParams(vmem_limit_bytes=52 * MIB),
        name="front",
    )(x, pack, gains, alive, bias, cosine, sine, wait)


def middle_kernel(
    dx_one_ref, dx_two_ref, normed_two_ref, middle_ref, cot_ref, mask_ref, alive_ref, gains_ref,
    router_ref, output_ref, mixed_ref, wait_ref, d_middle_ref, d_mixed_ref, grads_ref,
):
    dx = jnp.concatenate([dx_one_ref[...], dx_two_ref[...]], axis=0).astype(jnp.float32)
    normed_two = normed_two_ref[...]
    mask = mask_ref[...].astype(jnp.float32) > 0.5
    gates = gates_of(normed_two, router_ref[...], mask)
    extra = dx[:, MODEL_WIDTH:]
    d_gates = extra + pltpu.roll(extra, LANES - EXPERTS, 1)
    d_logits = (
        gates * (d_gates - jnp.sum(gates * d_gates, axis=1, keepdims=True))
    ).astype(brain_floating)
    d_normed = dx[:, :MODEL_WIDTH] + times_transposed(d_logits, router_ref[...])
    scaled, inverse = normalize(middle_ref[...])
    d_middle = cot_ref[...].astype(jnp.float32) + norm_back(
        d_normed, scaled, inverse, gains_ref[1:2, :]
    )
    d_middle_ref[...] = d_middle
    d_attended = (alive_ref[...] * d_middle).astype(brain_floating)
    grads_ref[:, :MODEL_WIDTH] = transposed_times(mixed_ref[...], d_attended).astype(brain_floating)
    small = transposed_times(normed_two, d_logits)
    small = jnp.where(lanes_of(small.shape) == EXPERTS, column_sums(d_normed * scaled), small)
    grads_ref[:, MODEL_WIDTH:] = small.astype(brain_floating)
    d_mixed_ref[...] = times_transposed(d_attended, output_ref[...]).astype(brain_floating)


def run_middle(dx_one, dx_two, normed_two, middle, cot, mask, alive, gains, pack, mixed, wait):
    rows = middle.shape[0]
    full = [whole(v.shape) for v in (dx_one, dx_two, normed_two, middle, cot, mask, alive, gains)]
    return pl.pallas_call(
        middle_kernel,
        grid=(1,),
        in_specs=full
        + [
            part((MODEL_WIDTH, EXTRA), (0, ROUTER_BLOCK)),
            part((WIDTH, MODEL_WIDTH), (0, PROJECTED // MODEL_WIDTH)),
            whole(mixed.shape),
            ANYWHERE,
        ],
        out_specs=[
            whole((rows, MODEL_WIDTH)),
            whole((rows, WIDTH)),
            whole((MODEL_WIDTH, MODEL_WIDTH + EXTRA)),
        ],
        out_shape=[
            out((rows, MODEL_WIDTH), jnp.float32),
            out((rows, WIDTH), brain_floating),
            out((MODEL_WIDTH, MODEL_WIDTH + EXTRA), brain_floating),
        ],
        compiler_params=pltpu.CompilerParams(vmem_limit_bytes=52 * MIB),
        cost_estimate=takes(30),
        name="middle_back",
    )(dx_one, dx_two, normed_two, middle, cot, mask, alive, gains, pack, pack, mixed, wait)


def back_kernel(
    d_mixed_ref, qkv_ref, totals_ref, bias_ref, cos_ref, sin_ref, normed_ref, x_ref, d_middle_ref,
    gains_ref, other_ref, pack_ref, wait_ref, also_ref, grads_ref, d_input_ref, d_linear_ref, d_keys_ref, d_values_ref,
):
    rows = x_ref.shape[0]
    cosine, sine = (cos_ref[...], -sin_ref[...])

    @pl.loop(0, KEYVALUE_HEADS // 2)
    def _(pair):
        at = pl.multiple_of(pair * LANES, LANES)
        keys = qkv_ref[:, pl.ds(WIDTH + at, LANES)].astype(jnp.float32)
        values = qkv_ref[:, pl.ds(WIDTH + KV_WIDTH + at, LANES)].astype(jnp.float32)
        pair_keys = jnp.zeros((rows, LANES), jnp.float32)
        pair_values = jnp.zeros((rows, LANES), jnp.float32)
        for a in range(2):
            both_keys = both_halves(keys, a)
            head_keys = both_keys.astype(brain_floating)
            head_values = both_halves(values, a).astype(brain_floating)
            place = pl.multiple_of((2 * pair + a) * LANES, LANES)
            queries = qkv_ref[:, pl.ds(place, LANES)].astype(jnp.float32)
            d_outs = d_mixed_ref[:, pl.ds(place, LANES)].astype(jnp.float32)
            d_keys_ref[...] = jnp.zeros_like(d_keys_ref)
            d_values_ref[...] = jnp.zeros_like(d_values_ref)
            for start in range(0, rows, SPAN):
                seen = min(start + SPAN, rows)
                d_query = jnp.zeros((SPAN, LANES), jnp.float32)
                for j in range(2):
                    head = 2 * (2 * pair + a) + j
                    query = only_half(queries[start : start + SPAN], j).astype(brain_floating)
                    d_out = only_half(d_outs[start : start + SPAN], j).astype(brain_floating)
                    held = totals_ref[start : start + SPAN, :]
                    total = jnp.sum(
                        jnp.where(lanes_of(held.shape) == head, held, 0.0), axis=1, keepdims=True
                    )
                    scores = (
                        times_transposed(query, head_keys[:seen]) * SCORE_SCALE
                        + bias_ref[start : start + SPAN, :seen]
                    )
                    probs = jnp.exp(scores - total)
                    d_probs = times_transposed(d_out, head_values[:seen])
                    inner = jnp.sum(probs * d_probs, axis=1, keepdims=True)
                    d_scores = (probs * (d_probs - inner)).astype(brain_floating)
                    d_query += product(
                        d_scores, only_half(both_keys[:seen], j).astype(brain_floating)
                    )
                    d_keys_ref[:seen, :] += transposed_times(d_scores, query)
                    d_values_ref[:seen, :] += transposed_times(probs.astype(brain_floating), d_out)
                d_linear_ref[start : start + SPAN, pl.ds(place, LANES)] = rotate(
                    d_query * SCORE_SCALE,
                    cosine[start : start + SPAN],
                    sine[start : start + SPAN],
                ).astype(brain_floating)
            d_keys = d_keys_ref[...]
            d_values = d_values_ref[...]
            pair_keys += only_half(d_keys + pltpu.roll(d_keys, HEAD_SIZE, 1), a)
            pair_values += only_half(d_values + pltpu.roll(d_values, HEAD_SIZE, 1), a)
        d_linear_ref[:, pl.ds(WIDTH + at, LANES)] = rotate(
            pair_keys * SCORE_SCALE, cosine, sine
        ).astype(brain_floating)
        d_linear_ref[:, pl.ds(WIDTH + KV_WIDTH + at, LANES)] = pair_values.astype(brain_floating)

    normed = normed_ref[...]
    for at in range(0, PROJECTED, 512):
        grads_ref[:, at : at + 512] = transposed_times(
            normed, d_linear_ref[:, at : at + 512]
        ).astype(brain_floating)
    d_normed = times_transposed(d_linear_ref[...], pack_ref[...])
    scaled, inverse = normalize(x_ref[...].astype(jnp.float32))
    sums = column_sums(d_normed * scaled)
    grads_ref[:, PROJECTED : PROJECTED + EXTRA] = jnp.where(
        lanes_of(sums.shape) == 0, sums, 0.0
    ).astype(brain_floating)
    grads_ref[:, PROJECTED + EXTRA :] = other_ref[...]
    d_input_ref[...] = d_middle_ref[...] + norm_back(d_normed, scaled, inverse, gains_ref[0:1, :])


def run_back(
    d_mixed, qkv, totals, bias, cosine, sine, normed, x, d_middle, gains, other, pack, wait, also
):
    rows = x.shape[0]
    held = (d_mixed, qkv, totals, bias, cosine, sine, normed, x, d_middle, gains, other)
    width = PROJECTED + EXTRA + other.shape[1]
    return pl.pallas_call(
        back_kernel,
        grid=(1,),
        in_specs=[whole(v.shape) for v in held]
        + [part((MODEL_WIDTH, PROJECTED), (0, 0)), ANYWHERE, ANYWHERE],
        out_specs=[whole((MODEL_WIDTH, width)), whole((rows, MODEL_WIDTH))],
        out_shape=[
            out((MODEL_WIDTH, width), brain_floating),
            out((rows, MODEL_WIDTH), jnp.float32),
        ],
        scratch_shapes=[
            pltpu.VMEM((rows, PROJECTED), brain_floating),
            pltpu.VMEM((rows, LANES), jnp.float32),
            pltpu.VMEM((rows, LANES), jnp.float32),
        ],
        compiler_params=pltpu.CompilerParams(vmem_limit_bytes=52 * MIB),
        cost_estimate=takes(30),
        name="attention_back",
    )(*held, pack, wait, also)


def expert_kernel(me_ref, x_ref, b_ref, w_ref, router_ref, ga_ref, dgu_ref, dx_ref):
    x = x_ref[...]
    branch = b_ref[:, 0, :, :MODEL_WIDTH].reshape(x.shape)
    mask = b_ref[:, 0, :, MODEL_WIDTH:].reshape(x.shape[0], EXTRA).astype(jnp.float32) > 0.5
    gates = gates_of(x, router_ref[...], mask)
    lane = lanes_of(gates.shape)
    d_gates = jnp.zeros_like(gates)
    dx = jnp.zeros((x.shape[0], MODEL_WIDTH), jnp.float32)
    for local in range(LOCAL):
        expert = me_ref[0] + GROUP * local
        gate_weight, up_weight, down_weight = (
            w_ref[:, local, p].reshape(MODEL_WIDTH, F) for p in range(3)
        )
        gate = jnp.sum(jnp.where(lane == expert, gates, 0.0), axis=1, keepdims=True)
        gate_linear = product(x, gate_weight)
        up_linear = product(x, up_weight)
        back = product(branch, down_weight)
        sig = jax.nn.sigmoid(gate_linear)
        silu = gate_linear * sig
        act = silu * up_linear
        ga_ref[:, local * F : (local + 1) * F] = (gate * act).astype(brain_floating)
        d_gate = jnp.sum(act * back, axis=1, keepdims=True)
        high = d_gate.astype(brain_floating).astype(jnp.float32)
        d_gates += jnp.where(lane == expert, high, 0.0)
        d_gates += jnp.where(lane == expert + EXPERTS, d_gate - high, 0.0)
        d_act = gate * back
        d_gl = (d_act * up_linear * (sig + silu * (1.0 - sig))).astype(brain_floating)
        d_ul = (d_act * silu).astype(brain_floating)
        dgu_ref[:, 2 * local * F : (2 * local + 1) * F] = d_gl
        dgu_ref[:, (2 * local + 1) * F : (2 * local + 2) * F] = d_ul
        dx += times_transposed(d_gl, gate_weight) + times_transposed(d_ul, up_weight)
    dx_ref[:, :MODEL_WIDTH] = dx.astype(brain_floating)
    dx_ref[:, MODEL_WIDTH:] = d_gates.astype(brain_floating)


def run_experts(me, c, x, b, weights, pack):
    rows = x.shape[0]
    part_rows = b.shape[2]
    tile = 2 * part_rows
    wide = MODEL_WIDTH + EXTRA

    def rowed(width):
        return pl.BlockSpec((tile, width), lambda i, me_ref: (i, 0))

    return pl.pallas_call(
        expert_kernel,
        grid_spec=pltpu.PrefetchScalarGridSpec(
            num_scalar_prefetch=1,
            grid=(rows // tile,),
            in_specs=[
                rowed(MODEL_WIDTH),
                pl.BlockSpec((2, 1, part_rows, wide), lambda i, me_ref: (i, c, 0, 0)),
                whole(weights.shape),
                part((MODEL_WIDTH, EXTRA), (0, ROUTER_BLOCK)),
            ],
            out_specs=[rowed(LOCAL * F), rowed(2 * LOCAL * F), rowed(wide)],
        ),
        out_shape=[
            out((rows, LOCAL * F), brain_floating),
            out((rows, 2 * LOCAL * F), brain_floating),
            out((rows, wide), brain_floating),
        ],
        compiler_params=pltpu.CompilerParams(vmem_limit_bytes=56 * MIB),
        name="experts",
    )(me, x, b, weights, pack)


def chunked_specs(steps, shape, place):
    def index(c):
        return lambda i, *_: place(jnp.clip(i - c * steps, 0, steps - 1), c)

    return [pl.BlockSpec(shape, index(c)) for c in range(CHUNKS)]


def grads_kernel(steps, sides, *refs):
    count = len(sides)
    ins, outs, sums = (
        refs[: CHUNKS * 2 * count],
        refs[CHUNKS * 2 * count + 1 : -count],
        refs[-count:],
    )
    i = pl.program_id(0)

    @pl.when(i == 0)
    def _():
        for total in sums:
            total[...] = jnp.zeros_like(total)

    for c in range(CHUNKS):

        @pl.when(i // steps == c)
        def _():
            for k in range(count):
                left, right = (ins[2 * (k * CHUNKS + c)], ins[2 * (k * CHUNKS + c) + 1])
                sums[k][...] += transposed_times(
                    left[...].reshape(right.shape[0], MODEL_WIDTH), right[...]
                )

    @pl.when(i == CHUNKS * steps - 1)
    def _():
        for result, total in zip(outs, sums):
            result[...] = total[...].astype(brain_floating)


def run_grads(local, sides, xs, b, gas, dgus, wait, cost):
    rows, part_rows = (xs[0].shape[0], b.shape[2])
    tile = 2 * part_rows
    steps = rows // tile
    specs, arrays = ([], [])
    for side in sides:
        if side == 2:
            left = chunked_specs(
                steps, (2, 1, part_rows, MODEL_WIDTH), lambda i, c: (i, c, 0, 0)
            )
            right = chunked_specs(steps, (tile, F), lambda i, c: (i, local))
        else:
            left = chunked_specs(steps, (tile, MODEL_WIDTH), lambda i, c: (i, 0))
            right = chunked_specs(
                steps, (tile, F), lambda i, c, side=side: (i, 2 * local + side)
            )
        for c in range(CHUNKS):
            specs += [left[c], right[c]]
            arrays += [b, gas[c]] if side == 2 else [xs[c], dgus[c]]
    return pl.pallas_call(
        functools.partial(grads_kernel, steps, sides),
        grid=(CHUNKS * steps,),
        in_specs=specs + [ANYWHERE],
        out_specs=[whole((MODEL_WIDTH, F))] * len(sides),
        out_shape=[out((MODEL_WIDTH, F), brain_floating)] * len(sides),
        scratch_shapes=[pltpu.VMEM((MODEL_WIDTH, F), jnp.float32)] * len(sides),
        compiler_params=pltpu.CompilerParams(vmem_limit_bytes=52 * MIB),
        cost_estimate=takes(cost),
        name="grads",
    )(*arrays, wait)


def mix_kernel(ga_ref, w_ref, wait_ref, out_ref):
    total = jnp.zeros((ga_ref.shape[0], MODEL_WIDTH), jnp.float32)
    for local in range(LOCAL):
        total += times_transposed(
            ga_ref[:, local * F : (local + 1) * F], w_ref[:, local, 0].reshape(MODEL_WIDTH, F)
        )
    out_ref[...] = total.astype(brain_floating)


def run_mix(ga, weights, wait, cost):
    rows = ga.shape[0]
    tile = min(TILE, rows)
    blocks, _, _, shard, _ = weights.shape
    return pl.pallas_call(
        mix_kernel,
        grid=(rows // tile,),
        in_specs=[
            pl.BlockSpec((tile, LOCAL * F), lambda i: (i, 0)),
            part((blocks, LOCAL, 1, shard, F), (0, 0, 2, 0, 0)),
            ANYWHERE,
        ],
        out_specs=pl.BlockSpec((tile, MODEL_WIDTH), lambda i: (i, 0)),
        out_shape=out((rows, MODEL_WIDTH), brain_floating),
        compiler_params=pltpu.CompilerParams(vmem_limit_bytes=52 * MIB),
        cost_estimate=takes(cost),
        name="mixture",
    )(ga, weights, wait)


def sums_kernel(count, copies, waits, *refs):
    ins, outs = (refs[: 2 * count + copies], refs[2 * count + copies + waits :])
    for k in range(count):
        left, right = (ins[2 * k][...], ins[2 * k + 1][...])
        outs[k][...] = (left.astype(jnp.float32) + right.astype(jnp.float32)).astype(
            brain_floating
        )
    for k in range(copies):
        outs[count + k][...] = ins[2 * count + k][...]


def run_sums(pairs, copies, waits):
    flat = [v for pair in pairs for v in pair] + list(copies)
    return pl.pallas_call(
        functools.partial(sums_kernel, len(pairs), len(copies), len(waits)),
        in_specs=[pl.BlockSpec(memory_space=pltpu.VMEM)] * len(flat) + [ANYWHERE] * len(waits),
        out_shape=[out(v.shape, brain_floating) for v in [pair[0] for pair in pairs] + list(copies)],
        compiler_params=pltpu.CompilerParams(vmem_limit_bytes=40 * MIB),
        cost_estimate=takes(2),
        name="sums",
    )(*flat, *waits)


def after_kernel(values_ref, wait_ref, out_ref):
    del values_ref, wait_ref, out_ref


def after(values, wait):
    return pl.pallas_call(
        after_kernel,
        in_specs=[ANYWHERE] * 2,
        out_specs=ANYWHERE,
        out_shape=out(values.shape, values.dtype),
        input_output_aliases={0: 0},
        name="after",
    )(values, wait)


def adam_kernel(turned, rate, shrink, place_ref, t_ref, r_ref, w_ref, m_ref, v_ref, *rest):
    m_out, v_out, w_out = rest[-3:]
    inner = (place_ref[0] == 1) | (place_ref[0] == 2)
    for k in range(t_ref.shape[0]):
        gradient = jnp.where(inner, t_ref[k].astype(jnp.float32), r_ref[k].astype(jnp.float32))
        if turned:
            at = (k,)
            gradient = gradient.T
        else:
            at = (k, 0)
        moment, square, renewed = adamw_step(
            w_ref[at], m_ref[at], v_ref[at], gradient, rate, shrink
        )
        m_out[at] = moment
        v_out[at] = square
        w_out[at] = renewed


def adam_part(place, total, ends, state, local, side, rate, before, wait, cost):
    weight, first, second = state
    turned = side == 2
    shard = total.shape[1]
    held = [] if before is None else list(before)
    if turned:
        spec = pl.BlockSpec((2, F, shard), lambda i, _: (i + local * (GROUP // 2), 0, 0))
    else:
        spec = pl.BlockSpec((2, 1, shard, F), lambda i, _: (i + local * (GROUP // 2), side, 0, 0))
    piece = pl.BlockSpec((2, shard, F), lambda i, _: (i, 0, 0))
    return pl.pallas_call(
        functools.partial(adam_kernel, turned, rate, decay_rate),
        grid_spec=pltpu.PrefetchScalarGridSpec(
            num_scalar_prefetch=1,
            grid=(GROUP // 2,),
            in_specs=[piece, piece, spec, spec, spec] + [ANYWHERE] * (len(held) + 1),
            out_specs=[spec] * 3,
        ),
        out_shape=[out(weight.shape, jnp.float32)] * 3,
        input_output_aliases={6 + i: i for i in range(len(held))},
        compiler_params=pltpu.CompilerParams(vmem_limit_bytes=40 * MIB),
        cost_estimate=takes(cost),
        name="adam",
    )(place, total, ends, weight, first, second, *held, wait)


fsdp = ("outer", "inner")


def body(
    sizes,
    tokens_in,
    cotangent,
    document_lengths,
    expert_choice,
    norm_gains,
    gains_first,
    gains_second,
    query_weight,
    query_first,
    query_second,
    keyvalue_weight,
    keyvalue_first_moment,
    keyvalue_second_moment,
    output_weight,
    output_first,
    output_second,
    router_weight,
    router_first,
    router_second,
    gateup_weight,
    gateup_first,
    gateup_second,
    down_weight,
    down_first,
    down_second,
):
    replicas, outer = sizes
    count_of_rows = tokens_in.shape[0]
    shard = query_weight.shape[0]
    me = lax.axis_index("inner").astype(jnp.int32).reshape(1)
    place = lax.axis_index("replica").astype(jnp.int32).reshape(1)

    pack_own = jnp.concatenate(
        [
            query_weight,
            keyvalue_weight[0],
            keyvalue_weight[1],
            output_weight,
            router_weight,
            norm_gains.T,
            jnp.zeros((shard, EXTRA - EXPERTS - 2), jnp.float32),
        ],
        axis=1,
    ).astype(brain_floating)
    pack = lax.all_gather(pack_own, fsdp, axis=0, tiled=True)
    at = PROJECTED + MODEL_WIDTH + EXPERTS
    gains_value = pack[:, at : at + 2].astype(jnp.float32).T

    weights = lax.all_to_all(split_by_owner(gateup_weight, down_weight), "inner", 0, 0)
    if outer > 1:
        weights = lax.all_gather(weights, "outer", axis=0, tiled=True)

    position, alive_mask, allowed = layout(document_lengths[0], count_of_rows)
    cosine, sine = rope_tables(position)
    alive = alive_mask[:, None]
    bias = jnp.where(allowed, 0.0, masked_value)

    expert_row = jnp.arange(EXPERTS, dtype=jnp.int32)
    chosen = jnp.any(expert_choice[:, :, None] == expert_row[None, None, :], axis=1)
    mask = jnp.concatenate(
        [
            chosen.astype(brain_floating),
            jnp.zeros((count_of_rows, EXTRA - EXPERTS), brain_floating),
        ],
        axis=1,
    )
    branch = (alive * cotangent.astype(jnp.float32)).astype(brain_floating)
    branch_pack = jnp.concatenate([branch, mask], axis=1)
    part_rows = count_of_rows // CHUNKS

    def gathered(values, c):
        return lax.all_gather(
            values[c * part_rows : (c + 1) * part_rows], "inner", axis=0, tiled=True
        )

    branch_all = lax.all_gather(branch_pack, "inner", axis=0, tiled=True).reshape(
        GROUP, CHUNKS, part_rows, MODEL_WIDTH + EXTRA
    )

    normed, qkv, mixed, totals, middle, normed_two = run_front(
        tokens_in, pack, gains_value, alive, bias, cosine, sine, weights
    )

    x_all, ga_all, dgu_all, dx_parts = ([], [], [], [])
    for c in range(CHUNKS):
        x_part = gathered(normed_two, c)
        ga, dgu, dx = run_experts(me, c, x_part, branch_all, weights, pack)
        x_all.append(x_part)
        ga_all.append(ga)
        dgu_all.append(dgu)
        dx_parts.append(lax.psum_scatter(dx, "inner", scatter_dimension=0, tiled=True))

    def to_owner(grad):
        parts = grad.reshape(GROUP * outer, shard, F)
        if outer > 1:
            parts = lax.psum_scatter(parts, "outer", scatter_dimension=0, tiled=True)
        return lax.all_to_all(parts, "inner", 0, 0)

    def inward(values):
        return lax.ppermute(values, "replica", [(0, 1), (3, 2)])

    def across(values):
        return lax.ppermute(values, "replica", [(1, 2), (2, 1)])

    def outward(values):
        return lax.ppermute(values, "replica", [(1, 0), (2, 3)])

    def grads_of(local, sides, wait, cost):
        return run_grads(local, sides, x_all, branch_all, ga_all, dgu_all, wait, cost)

    chunks = [(local, side) for local in range(LOCAL) for side in (2, 0, 1)]
    last = len(chunks) + 1
    root = MODEL_WIDTH ** (-0.5)
    states = (
        (gateup_weight, gateup_first, gateup_second),
        (down_weight, down_first, down_second),
    )
    renewed = [None, None]
    totals_of, ends = ({}, {})

    def adam_of(k, wait, cost):
        local, side = chunks[k]
        which = side // 2
        renewed[which] = adam_part(
            place, totals_of[k], ends[k], states[which], local, side,
            (F // 16) ** (-0.5) if which else root, renewed[which], wait, cost,
        )
        return renewed[which][0]

    first = grads_of(0, (2,), dgu_all[-1], 1)
    ready = {0: first[0]}
    token = first[0]
    mine, by_pairs = ({}, {})
    mixtures_own = []

    def mix_of(c, wait, cost):
        rows = run_mix(ga_all[c], weights, wait, cost)
        mixtures_own.append(lax.psum_scatter(rows, "inner", scatter_dimension=0, tiled=True))
        return rows

    for k in range(-1, last + 3):
        pairs, copies, waits, keep = ([], [], [], [])
        if k in mine:
            pairs.append((mine[k], inward(mine[k])))
            keep.append((by_pairs, k))
        if k - 1 in by_pairs:
            pairs.append((by_pairs[k - 1], across(by_pairs[k - 1])))
            keep.append((totals_of, k - 1))
        if k - 2 in totals_of:
            ends[k - 2] = outward(totals_of[k - 2])
            waits.append(ends[k - 2])

        arrived = None
        if 0 <= k + 1 < len(chunks):
            arrived = to_owner(after(ready[k + 1], token) if k >= 0 else ready[k + 1])
        if k == -1:
            ready[1], ready[2] = grads_of(0, (0, 1), token, 1)
            done = ready[1]
        elif k == 0:
            ready[3], ready[4], ready[5] = grads_of(1, (2, 0, 1), token, 6)
            done = ready[3]
        elif k == 1:
            done = mix_of(0, token, 6)
        elif k == 2:
            d_middle, d_mixed, second_grads = run_middle(
                dx_parts[0], dx_parts[1], normed_two, middle, cotangent, mask, alive, gains_value,
                pack, mixed, token,
            )
            done = d_mixed
        elif k == 3:
            rest_grads, input_gradient = run_back(
                d_mixed, qkv, totals, bias, cosine, sine, normed, tokens_in, d_middle, gains_value,
                second_grads, pack, token, token,
            )
            rest_own = lax.psum_scatter(rest_grads, fsdp, scatter_dimension=0, tiled=True)
            waits.append(mixtures_own[0])
            done = input_gradient
        elif k == 4:
            done = adam_of(0, mix_of(1, token, 200), 1)
        elif k == 5:
            done = adam_of(2, adam_of(1, token, 200), 1)
        elif k - 3 < len(chunks):
            done = adam_of(k - 3, token, 200)
        waits.append(done)

        if 0 <= k + 1 < len(chunks):
            copies.append(arrived)
            keep.append((mine, k + 1))
        elif k + 1 == last:
            copies.append(rest_own)
            keep.append((mine, k + 1))
        if pairs or copies:
            results = run_sums(pairs, copies, waits)
            token = results[0]
            for (kept, at), value in zip(keep, results):
                kept[at] = value

    mixture_own = jnp.concatenate(mixtures_own, axis=0).astype(jnp.float32)
    block_output = (middle + alive * mixture_own).astype(brain_floating)

    inner = (place[0] == 1) | (place[0] == 2)
    rest_sum = jnp.where(inner, totals_of[last], ends[last]).astype(jnp.float32)
    first_sum, second_sum = (rest_sum[:, : PROJECTED + EXTRA], rest_sum[:, PROJECTED + EXTRA :])
    gains_part = jnp.stack([first_sum[:, PROJECTED], second_sum[:, MODEL_WIDTH + EXPERTS]])
    keyval_part = jnp.stack(
        [first_sum[:, WIDTH : WIDTH + KV_WIDTH], first_sum[:, WIDTH + KV_WIDTH : PROJECTED]]
    )
    settings = (
        (gains_part, norm_gains, gains_first, gains_second, gain_rate, 0.0),
        (first_sum[:, :WIDTH], query_weight, query_first, query_second, root, decay_rate),
        (
            keyval_part,
            keyvalue_weight,
            keyvalue_first_moment,
            keyvalue_second_moment,
            root,
            decay_rate,
        ),
        (
            second_sum[:, :MODEL_WIDTH],
            output_weight,
            output_first,
            output_second,
            (WIDTH // 16) ** (-0.5),
            decay_rate,
        ),
        (
            second_sum[:, MODEL_WIDTH : MODEL_WIDTH + EXPERTS],
            router_weight,
            router_first,
            router_second,
            (4 * MODEL_WIDTH) ** (-0.5),
            decay_rate,
        ),
    )
    updated = []
    for gradient, weight, first, second, rate, shrink in settings:
        updated.extend(adamw_step(weight, first, second, gradient, rate, shrink))
    return (block_output, input_gradient) + tuple(updated) + tuple(renewed[0]) + tuple(renewed[1])


def solution(mesh):
    replicas, shards = (mesh.shape["replica"], mesh.shape["fsdp"])
    outer = shards // GROUP
    split = Mesh(mesh.devices.reshape(replicas, outer, GROUP), ("replica",) + fsdp)
    rows = P(("replica",) + fsdp, None)
    by_first = P(fsdp, None)
    by_second = P(None, fsdp)
    by_middle = P(None, fsdp, None)
    by_third = P(None, None, fsdp, None)
    by_last = P(None, None, fsdp)
    weights = (by_second, by_first, by_middle, by_first, by_first, by_third, by_last)
    states = tuple(spec for spec in weights for _ in range(3))
    return jax.shard_map(
        functools.partial(body, (replicas, outer)),
        mesh=split,
        in_specs=(rows,) * 4 + states,
        out_specs=(rows,) * 2 + states,
        check_vma=False,
    )
```

```python
import functools
import math

import jax
import jax.numpy as jnp
from jax import lax
from jax.experimental import pallas as pl
from jax.experimental.pallas import tpu as pltpu
from jax.sharding import Mesh
from jax.sharding import PartitionSpec as P

MODEL_WIDTH = 1024
QUERY_HEADS = 16
KEYVALUE_HEADS = 8
HEAD_SIZE = 64
F = 512
TOPK = 8
EXPERTS = 16
ADAM_STEP = 5
GROUP = 8
LOCAL = EXPERTS // GROUP
EXTRA = 128
CHUNKS = 2
TILE = 512
SPAN = 256
LANES = 128
WIDTH = QUERY_HEADS * HEAD_SIZE
KV_WIDTH = KEYVALUE_HEADS * HEAD_SIZE
PROJECTED = WIDTH + 2 * KV_WIDTH
SCORE_SCALE = HEAD_SIZE ** (-0.5)
ROUTER_BLOCK = (PROJECTED + MODEL_WIDTH) // EXTRA


norm_eps = 1e-06
rope_base = 10000.0
beta_one = 0.9
beta_two = 0.95
adam_eps = 1e-08
decay_rate = 0.1
gain_rate = 0.25
masked_value = -1e30
brain_floating = jnp.bfloat16


def layout(lengths, count_of_rows):
    document_ends = jnp.cumsum(lengths)
    row_index = jnp.arange(count_of_rows, dtype=jnp.int32)
    passed = row_index[:, None] >= document_ends[None, :]
    segment = jnp.sum(passed.astype(jnp.int32), axis=1)
    start_row = jnp.sum(jnp.where(passed, lengths[None, :], 0), axis=1)
    position = (row_index - start_row).astype(jnp.float32)
    alive_mask = (segment < lengths.shape[0]).astype(jnp.float32)
    allowed = (segment[:, None] == segment[None, :]) & (row_index[None, :] <= row_index[:, None])
    return (position, alive_mask, allowed)


def rope_tables(position):
    half_width = HEAD_SIZE // 2
    exponents = jnp.arange(half_width, dtype=jnp.float32) * (2.0 / HEAD_SIZE)
    inverse = jnp.exp(exponents * -math.log(rope_base))
    angles = position[:, None] * inverse[None, :]
    cosine, sine = (jnp.cos(angles), jnp.sin(angles))
    return (
        jnp.concatenate([cosine] * 4, axis=1),
        jnp.concatenate([-sine, sine, -sine, sine], axis=1),
    )


def product(left, right):
    return jnp.dot(left, right, preferred_element_type=jnp.float32)


def times_transposed(left, right):
    return lax.dot_general(
        left, right, (((1,), (1,)), ((), ())), preferred_element_type=jnp.float32
    )


def transposed_times(left, right):
    return lax.dot_general(
        left, right, (((0,), (0,)), ((), ())), preferred_element_type=jnp.float32
    )


def normalize(values):
    inverse = lax.rsqrt(jnp.mean(values * values, axis=-1, keepdims=True) + norm_eps)
    return (values * inverse, inverse)


def norm_back(upstream, scaled_rows, inverse, gain_row):
    weighted = upstream * gain_row
    inner = jnp.mean(weighted * scaled_rows, axis=-1, keepdims=True)
    return inverse * (weighted - scaled_rows * inner)


def column_sums(values):
    ones = jnp.ones((values.shape[0], LANES), brain_floating)
    high = values.astype(brain_floating)
    low = (values - high.astype(jnp.float32)).astype(brain_floating)
    return transposed_times(high, ones) + transposed_times(low, ones)


def lanes_of(shape):
    return lax.broadcasted_iota(jnp.int32, shape, 1)


def rotate(values, cosine, sine):
    half = HEAD_SIZE // 2
    front = lax.rem(lanes_of(values.shape), HEAD_SIZE) < half
    swapped = jnp.where(
        front, pltpu.roll(values, LANES - half, 1), pltpu.roll(values, half, 1)
    )
    return values * cosine + swapped * sine


def both_halves(values, which):
    turned = pltpu.roll(values, HEAD_SIZE, 1)
    first = lanes_of(values.shape) < HEAD_SIZE
    return jnp.where(first == (which == 0), values, turned)


def only_half(values, which):
    first = lanes_of(values.shape) < HEAD_SIZE
    return jnp.where(first == (which == 0), values, 0.0)


def gates_of(rows, router, mask):
    logits = product(rows, router)
    peak = jnp.max(jnp.where(mask, logits, masked_value), axis=1, keepdims=True)
    weights = jnp.where(mask, jnp.exp(logits - peak), 0.0)
    return weights / jnp.sum(weights, axis=1, keepdims=True)


def adamw_step(weight, moment_old, square_old, gradient, step_rate, shrink):
    moment = beta_one * moment_old + (1.0 - beta_one) * gradient
    square = beta_two * square_old + (1.0 - beta_two) * gradient * gradient
    moment_hat = moment / (1.0 - beta_one**ADAM_STEP)
    square_hat = square / (1.0 - beta_two**ADAM_STEP)
    renewed = weight - step_rate * (
        moment_hat / (jnp.sqrt(square_hat) + adam_eps) + shrink * weight
    )
    return (moment, square, renewed)


MIB = 1024 * 1024
ANYWHERE = pl.BlockSpec(memory_space=pl.ANY)


def takes(microseconds):
    return pl.CostEstimate(
        flops=int(microseconds * 1e9), bytes_accessed=int(microseconds * 3.6e6), transcendentals=0
    )


def whole(shape):
    return pl.BlockSpec(shape, lambda *_: (0,) * len(shape), pipeline_mode=pl.Buffered(1))


def part(shape, place):
    return pl.BlockSpec(shape, lambda *_: place, pipeline_mode=pl.Buffered(1))


def out(shape, dtype):
    return jax.ShapeDtypeStruct(shape, dtype)


def split_kernel(gateup_ref, down_ref, out_ref):
    for k in range(2):
        out_ref[k, 0, 0] = gateup_ref[k, 0].astype(brain_floating)
        out_ref[k, 0, 1] = gateup_ref[k, 1].astype(brain_floating)
        out_ref[k, 0, 2] = down_ref[k].T.astype(brain_floating)


def split_by_owner(gateup, down):
    shard = gateup.shape[2]
    steps = GROUP // 2
    return pl.pallas_call(
        split_kernel,
        grid=(EXPERTS // 2,),
        in_specs=[
            pl.BlockSpec((2, 2, shard, F), lambda e: (e, 0, 0, 0)),
            pl.BlockSpec((2, F, shard), lambda e: (e, 0, 0)),
        ],
        out_specs=pl.BlockSpec(
            (2, 1, 3, shard, F), lambda e: (lax.rem(e, steps), e // steps, 0, 0, 0)
        ),
        out_shape=out((GROUP, LOCAL, 3, shard, F), brain_floating),
        name="split",
    )(gateup, down)


def front_kernel(
    x_ref, pack_ref, gains_ref, alive_ref, bias_ref, cos_ref, sin_ref, wait_ref,
    normed_ref, qkv_ref, mixed_ref, totals_ref, middle_ref, normed_two_ref, linear_ref,
):
    rows = x_ref.shape[0]
    scaled, _ = normalize(x_ref[...].astype(jnp.float32))
    normed = (scaled * gains_ref[0:1, :]).astype(brain_floating)
    normed_ref[...] = normed
    linear_ref[...] = product(normed, pack_ref[:, :PROJECTED])
    cosine, sine = (cos_ref[...], sin_ref[...])
    for at in range(0, WIDTH + KV_WIDTH, LANES):
        qkv_ref[:, at : at + LANES] = rotate(
            linear_ref[:, at : at + LANES], cosine, sine
        ).astype(brain_floating)
    qkv_ref[:, WIDTH + KV_WIDTH :] = linear_ref[:, WIDTH + KV_WIDTH :].astype(brain_floating)
    totals_ref[...] = jnp.zeros_like(totals_ref)

    @pl.loop(0, KEYVALUE_HEADS // 2)
    def _(pair):
        at = pl.multiple_of(pair * LANES, LANES)
        keys = qkv_ref[:, pl.ds(WIDTH + at, LANES)].astype(jnp.float32)
        values = qkv_ref[:, pl.ds(WIDTH + KV_WIDTH + at, LANES)].astype(jnp.float32)
        for a in range(2):
            head_keys = both_halves(keys, a).astype(brain_floating)
            head_values = both_halves(values, a)
            place = pl.multiple_of((2 * pair + a) * LANES, LANES)
            queries = qkv_ref[:, pl.ds(place, LANES)].astype(jnp.float32)
            for start in range(0, rows, SPAN):
                seen = min(start + SPAN, rows)
                mixed = jnp.zeros((SPAN, LANES), jnp.float32)
                for j in range(2):
                    head = 2 * (2 * pair + a) + j
                    query = only_half(queries[start : start + SPAN], j).astype(brain_floating)
                    scores = (
                        times_transposed(query, head_keys[:seen]) * SCORE_SCALE
                        + bias_ref[start : start + SPAN, :seen]
                    )
                    peak = jnp.max(scores, axis=1, keepdims=True)
                    weights = jnp.exp(scores - peak)
                    total = jnp.sum(weights, axis=1, keepdims=True)
                    probs = (weights * (1.0 / total)).astype(brain_floating)
                    mixed += product(probs, only_half(head_values[:seen], j).astype(brain_floating))
                    held = totals_ref[start : start + SPAN, :]
                    totals_ref[start : start + SPAN, :] = jnp.where(
                        lanes_of(held.shape) == head, peak + jnp.log(total), held
                    )
                mixed_ref[start : start + SPAN, pl.ds(place, LANES)] = mixed.astype(brain_floating)

    attended = product(mixed_ref[...], pack_ref[:, PROJECTED : PROJECTED + MODEL_WIDTH])
    middle = x_ref[...].astype(jnp.float32) + alive_ref[...] * attended
    middle_ref[...] = middle
    scaled_two, _ = normalize(middle)
    normed_two_ref[...] = (scaled_two * gains_ref[1:2, :]).astype(brain_floating)


def run_front(x, pack, gains, alive, bias, cosine, sine, wait):
    rows = x.shape[0]
    return pl.pallas_call(
        front_kernel,
        in_specs=[pl.BlockSpec(memory_space=pltpu.VMEM)] * 7 + [ANYWHERE],
        out_shape=[
            out((rows, MODEL_WIDTH), brain_floating),
            out((rows, PROJECTED), brain_floating),
            out((rows, WIDTH), brain_floating),
            out((rows, LANES), jnp.float32),
            out((rows, MODEL_WIDTH), jnp.float32),
            out((rows, MODEL_WIDTH), brain_floating),
        ],
        scratch_shapes=[pltpu.VMEM((rows, PROJECTED), jnp.float32)],
        compiler_params=pltpu.CompilerParams(vmem_limit_bytes=52 * MIB),
        name="front",
    )(x, pack, gains, alive, bias, cosine, sine, wait)


def middle_kernel(
    dx_ref, normed_two_ref, middle_ref, cot_ref, mask_ref, alive_ref, gains_ref, router_ref,
    output_ref, mixed_ref, wait_ref, d_middle_ref, d_mixed_ref, grads_ref,
):
    dx = dx_ref[...].astype(jnp.float32)
    normed_two = normed_two_ref[...]
    mask = mask_ref[...].astype(jnp.float32) > 0.5
    gates = gates_of(normed_two, router_ref[...], mask)
    extra = dx[:, MODEL_WIDTH:]
    d_gates = extra + pltpu.roll(extra, LANES - EXPERTS, 1)
    d_logits = (
        gates * (d_gates - jnp.sum(gates * d_gates, axis=1, keepdims=True))
    ).astype(brain_floating)
    d_normed = dx[:, :MODEL_WIDTH] + times_transposed(d_logits, router_ref[...])
    scaled, inverse = normalize(middle_ref[...])
    d_middle = cot_ref[...].astype(jnp.float32) + norm_back(
        d_normed, scaled, inverse, gains_ref[1:2, :]
    )
    d_middle_ref[...] = d_middle
    d_attended = (alive_ref[...] * d_middle).astype(brain_floating)
    grads_ref[:, :MODEL_WIDTH] = transposed_times(mixed_ref[...], d_attended).astype(brain_floating)
    small = transposed_times(normed_two, d_logits)
    small = jnp.where(lanes_of(small.shape) == EXPERTS + 1, column_sums(d_normed * scaled), small)
    grads_ref[:, MODEL_WIDTH:] = small.astype(brain_floating)
    d_mixed_ref[...] = times_transposed(d_attended, output_ref[...]).astype(brain_floating)


def run_middle(dx, normed_two, middle, cot, mask, alive, gains, pack, mixed, wait):
    rows = middle.shape[0]
    full = [whole(v.shape) for v in (dx, normed_two, middle, cot, mask, alive, gains)]
    return pl.pallas_call(
        middle_kernel,
        grid=(1,),
        in_specs=full
        + [
            part((MODEL_WIDTH, EXTRA), (0, ROUTER_BLOCK)),
            part((WIDTH, MODEL_WIDTH), (0, PROJECTED // MODEL_WIDTH)),
            whole(mixed.shape),
            ANYWHERE,
        ],
        out_specs=[
            whole((rows, MODEL_WIDTH)),
            whole((rows, WIDTH)),
            whole((MODEL_WIDTH, MODEL_WIDTH + EXTRA)),
        ],
        out_shape=[
            out((rows, MODEL_WIDTH), jnp.float32),
            out((rows, WIDTH), brain_floating),
            out((MODEL_WIDTH, MODEL_WIDTH + EXTRA), brain_floating),
        ],
        compiler_params=pltpu.CompilerParams(vmem_limit_bytes=52 * MIB),
        cost_estimate=takes(30),
        name="middle_back",
    )(dx, normed_two, middle, cot, mask, alive, gains, pack, pack, mixed, wait)


def back_kernel(
    d_mixed_ref, qkv_ref, totals_ref, bias_ref, cos_ref, sin_ref, normed_ref, x_ref, d_middle_ref,
    gains_ref, other_ref, pack_ref, wait_ref, also_ref, grads_ref, d_input_ref, d_linear_ref, d_keys_ref, d_values_ref,
):
    rows = x_ref.shape[0]
    cosine, sine = (cos_ref[...], -sin_ref[...])

    @pl.loop(0, KEYVALUE_HEADS // 2)
    def _(pair):
        at = pl.multiple_of(pair * LANES, LANES)
        keys = qkv_ref[:, pl.ds(WIDTH + at, LANES)].astype(jnp.float32)
        values = qkv_ref[:, pl.ds(WIDTH + KV_WIDTH + at, LANES)].astype(jnp.float32)
        pair_keys = jnp.zeros((rows, LANES), jnp.float32)
        pair_values = jnp.zeros((rows, LANES), jnp.float32)
        for a in range(2):
            both_keys = both_halves(keys, a)
            head_keys = both_keys.astype(brain_floating)
            head_values = both_halves(values, a).astype(brain_floating)
            place = pl.multiple_of((2 * pair + a) * LANES, LANES)
            queries = qkv_ref[:, pl.ds(place, LANES)].astype(jnp.float32)
            d_outs = d_mixed_ref[:, pl.ds(place, LANES)].astype(jnp.float32)
            d_keys_ref[...] = jnp.zeros_like(d_keys_ref)
            d_values_ref[...] = jnp.zeros_like(d_values_ref)
            for start in range(0, rows, SPAN):
                seen = min(start + SPAN, rows)
                d_query = jnp.zeros((SPAN, LANES), jnp.float32)
                for j in range(2):
                    head = 2 * (2 * pair + a) + j
                    query = only_half(queries[start : start + SPAN], j).astype(brain_floating)
                    d_out = only_half(d_outs[start : start + SPAN], j).astype(brain_floating)
                    held = totals_ref[start : start + SPAN, :]
                    total = jnp.sum(
                        jnp.where(lanes_of(held.shape) == head, held, 0.0), axis=1, keepdims=True
                    )
                    scores = (
                        times_transposed(query, head_keys[:seen]) * SCORE_SCALE
                        + bias_ref[start : start + SPAN, :seen]
                    )
                    probs = jnp.exp(scores - total)
                    d_probs = times_transposed(d_out, head_values[:seen])
                    inner = jnp.sum(probs * d_probs, axis=1, keepdims=True)
                    d_scores = (probs * (d_probs - inner)).astype(brain_floating)
                    d_query += product(
                        d_scores, only_half(both_keys[:seen], j).astype(brain_floating)
                    )
                    d_keys_ref[:seen, :] += transposed_times(d_scores, query)
                    d_values_ref[:seen, :] += transposed_times(probs.astype(brain_floating), d_out)
                d_linear_ref[start : start + SPAN, pl.ds(place, LANES)] = rotate(
                    d_query * SCORE_SCALE,
                    cosine[start : start + SPAN],
                    sine[start : start + SPAN],
                ).astype(brain_floating)
            d_keys = d_keys_ref[...]
            d_values = d_values_ref[...]
            pair_keys += only_half(d_keys + pltpu.roll(d_keys, HEAD_SIZE, 1), a)
            pair_values += only_half(d_values + pltpu.roll(d_values, HEAD_SIZE, 1), a)
        d_linear_ref[:, pl.ds(WIDTH + at, LANES)] = rotate(
            pair_keys * SCORE_SCALE, cosine, sine
        ).astype(brain_floating)
        d_linear_ref[:, pl.ds(WIDTH + KV_WIDTH + at, LANES)] = pair_values.astype(brain_floating)

    normed = normed_ref[...]
    for at in range(0, PROJECTED, 512):
        grads_ref[:, at : at + 512] = transposed_times(
            normed, d_linear_ref[:, at : at + 512]
        ).astype(brain_floating)
    d_normed = times_transposed(d_linear_ref[...], pack_ref[...])
    scaled, inverse = normalize(x_ref[...].astype(jnp.float32))
    sums = column_sums(d_normed * scaled)
    grads_ref[:, PROJECTED : PROJECTED + MODEL_WIDTH] = other_ref[:, :MODEL_WIDTH]
    small = other_ref[:, MODEL_WIDTH:].astype(jnp.float32)
    grads_ref[:, PROJECTED + MODEL_WIDTH :] = jnp.where(
        lanes_of(sums.shape) == EXPERTS, sums, small
    ).astype(brain_floating)
    d_input_ref[...] = d_middle_ref[...] + norm_back(d_normed, scaled, inverse, gains_ref[0:1, :])


def run_back(
    d_mixed, qkv, totals, bias, cosine, sine, normed, x, d_middle, gains, other, pack, wait, also
):
    rows = x.shape[0]
    held = (d_mixed, qkv, totals, bias, cosine, sine, normed, x, d_middle, gains, other)
    width = PROJECTED + other.shape[1]
    return pl.pallas_call(
        back_kernel,
        grid=(1,),
        in_specs=[whole(v.shape) for v in held]
        + [part((MODEL_WIDTH, PROJECTED), (0, 0)), ANYWHERE, ANYWHERE],
        out_specs=[whole((MODEL_WIDTH, width)), whole((rows, MODEL_WIDTH))],
        out_shape=[
            out((MODEL_WIDTH, width), brain_floating),
            out((rows, MODEL_WIDTH), jnp.float32),
        ],
        scratch_shapes=[
            pltpu.VMEM((rows, PROJECTED), brain_floating),
            pltpu.VMEM((rows, LANES), jnp.float32),
            pltpu.VMEM((rows, LANES), jnp.float32),
        ],
        compiler_params=pltpu.CompilerParams(vmem_limit_bytes=52 * MIB),
        cost_estimate=takes(30),
        name="attention_back",
    )(*held, pack, wait, also)


def expert_kernel(me_ref, x_ref, b_ref, w_ref, router_ref, *refs):
    ga_ref, dgu_ref, dx_ref = refs[-3:]
    x = x_ref[...]
    branch = b_ref[:, 0, :, :MODEL_WIDTH].reshape(x.shape)
    mask = b_ref[:, 0, :, MODEL_WIDTH:].reshape(x.shape[0], EXTRA).astype(jnp.float32) > 0.5
    gates = gates_of(x, router_ref[...], mask)
    lane = lanes_of(gates.shape)
    d_gates = jnp.zeros_like(gates)
    dx = jnp.zeros((x.shape[0], MODEL_WIDTH), jnp.float32)
    for local in range(LOCAL):
        expert = me_ref[0] + GROUP * local
        gate_weight, up_weight, down_weight = (
            w_ref[:, local, p].reshape(MODEL_WIDTH, F) for p in range(3)
        )
        gate = jnp.sum(jnp.where(lane == expert, gates, 0.0), axis=1, keepdims=True)
        gate_linear = product(x, gate_weight)
        up_linear = product(x, up_weight)
        back = product(branch, down_weight)
        sig = jax.nn.sigmoid(gate_linear)
        silu = gate_linear * sig
        act = silu * up_linear
        ga_ref[:, local * F : (local + 1) * F] = (gate * act).astype(brain_floating)
        d_gate = jnp.sum(act * back, axis=1, keepdims=True)
        high = d_gate.astype(brain_floating).astype(jnp.float32)
        d_gates += jnp.where(lane == expert, high, 0.0)
        d_gates += jnp.where(lane == expert + EXPERTS, d_gate - high, 0.0)
        d_act = gate * back
        d_gl = (d_act * up_linear * (sig + silu * (1.0 - sig))).astype(brain_floating)
        d_ul = (d_act * silu).astype(brain_floating)
        dgu_ref[:, 2 * local * F : (2 * local + 1) * F] = d_gl
        dgu_ref[:, (2 * local + 1) * F : (2 * local + 2) * F] = d_ul
        dx += times_transposed(d_gl, gate_weight) + times_transposed(d_ul, up_weight)
    blocks, _, part_rows, _ = dx_ref.shape
    dx_ref[:, 0, :, :MODEL_WIDTH] = dx.astype(brain_floating).reshape(
        blocks, part_rows, MODEL_WIDTH
    )
    dx_ref[:, 0, :, MODEL_WIDTH:] = d_gates.astype(brain_floating).reshape(
        blocks, part_rows, EXTRA
    )


def run_experts(me, c, x, b, weights, pack, before):
    rows = x.shape[0]
    part_rows = b.shape[2]
    tile = 2 * part_rows
    wide = MODEL_WIDTH + EXTRA

    def rowed(width):
        return pl.BlockSpec((tile, width), lambda i, me_ref: (i, 0))

    return pl.pallas_call(
        expert_kernel,
        grid_spec=pltpu.PrefetchScalarGridSpec(
            num_scalar_prefetch=1,
            grid=(rows // tile,),
            in_specs=[
                rowed(MODEL_WIDTH),
                pl.BlockSpec((2, 1, part_rows, wide), lambda i, me_ref: (i, c, 0, 0)),
                whole(weights.shape),
                part((MODEL_WIDTH, EXTRA), (0, ROUTER_BLOCK)),
            ]
            + [ANYWHERE] * len(before),
            out_specs=[
                rowed(LOCAL * F),
                rowed(2 * LOCAL * F),
                pl.BlockSpec((2, 1, part_rows, wide), lambda i, me_ref: (i, c, 0, 0)),
            ],
        ),
        out_shape=[
            out((rows, LOCAL * F), brain_floating),
            out((rows, 2 * LOCAL * F), brain_floating),
            out((rows // part_rows, CHUNKS, part_rows, wide), brain_floating),
        ],
        input_output_aliases={5 + i: 2 for i in range(len(before))},
        compiler_params=pltpu.CompilerParams(vmem_limit_bytes=56 * MIB),
        name="experts",
    )(me, x, b, weights, pack, *before)


def chunked_specs(steps, shape, place):
    def index(c):
        return lambda i, *_: place(jnp.clip(i - c * steps, 0, steps - 1), c)

    return [pl.BlockSpec(shape, index(c)) for c in range(CHUNKS)]


def grads_kernel(steps, sides, *refs):
    count = len(sides)
    ins, out_ref, sums = (refs[: CHUNKS * 2 * count], refs[-count - 1], refs[-count:])
    blocks, _, shard, _ = out_ref.shape
    i = pl.program_id(0)

    @pl.when(i == 0)
    def _():
        for total in sums:
            total[...] = jnp.zeros_like(total)

    for c in range(CHUNKS):

        @pl.when(i // steps == c)
        def _():
            for k in range(count):
                left, right = (ins[2 * (k * CHUNKS + c)], ins[2 * (k * CHUNKS + c) + 1])
                sums[k][...] += transposed_times(
                    left[...].reshape(right.shape[0], MODEL_WIDTH), right[...]
                )

    @pl.when(i == CHUNKS * steps - 1)
    def _():
        for k, total in enumerate(sums):
            out_ref[:, k] = total[...].astype(brain_floating).reshape(blocks, shard, F)


def run_grads(local, sides, shard, xs, b, gas, dgus, wait, cost):
    blocks = MODEL_WIDTH // shard
    rows, part_rows = (xs[0].shape[0], b.shape[2])
    tile = 2 * part_rows
    steps = rows // tile
    specs, arrays = ([], [])
    for side in sides:
        if side == 2:
            left = chunked_specs(
                steps, (2, 1, part_rows, MODEL_WIDTH), lambda i, c: (i, c, 0, 0)
            )
            right = chunked_specs(steps, (tile, F), lambda i, c: (i, local))
        else:
            left = chunked_specs(steps, (tile, MODEL_WIDTH), lambda i, c: (i, 0))
            right = chunked_specs(
                steps, (tile, F), lambda i, c, side=side: (i, 2 * local + side)
            )
        for c in range(CHUNKS):
            specs += [left[c], right[c]]
            arrays += [b, gas[c]] if side == 2 else [xs[c], dgus[c]]
    return pl.pallas_call(
        functools.partial(grads_kernel, steps, sides),
        grid=(CHUNKS * steps,),
        in_specs=specs + [ANYWHERE],
        out_specs=whole((blocks, len(sides), shard, F)),
        out_shape=out((blocks, len(sides), shard, F), brain_floating),
        scratch_shapes=[pltpu.VMEM((MODEL_WIDTH, F), jnp.float32)] * len(sides),
        compiler_params=pltpu.CompilerParams(vmem_limit_bytes=52 * MIB),
        cost_estimate=takes(cost),
        name="grads",
    )(*arrays, wait)


def mix_kernel(steps, *refs):
    gas, w_ref, out_ref = (refs[:CHUNKS], refs[CHUNKS], refs[-1])
    for c in range(CHUNKS):

        @pl.when(pl.program_id(0) // steps == c)
        def _():
            total = jnp.zeros((gas[c].shape[0], MODEL_WIDTH), jnp.float32)
            for local in range(LOCAL):
                total += times_transposed(
                    gas[c][:, local * F : (local + 1) * F],
                    w_ref[:, local, 0].reshape(MODEL_WIDTH, F),
                )
            out_ref[...] = total.astype(brain_floating).reshape(out_ref.shape)


def run_mix(gas, weights, part_rows, wait, cost):
    rows = gas[0].shape[0]
    tile = 2 * part_rows
    steps = rows // tile
    blocks, _, _, shard, _ = weights.shape
    return pl.pallas_call(
        functools.partial(mix_kernel, steps),
        grid=(CHUNKS * steps,),
        in_specs=chunked_specs(steps, (tile, LOCAL * F), lambda i, c: (i, 0))
        + [part((blocks, LOCAL, 1, shard, F), (0, 0, 2, 0, 0)), ANYWHERE],
        out_specs=pl.BlockSpec(
            (2, 1, part_rows, MODEL_WIDTH), lambda i: (lax.rem(i, steps), i // steps, 0, 0)
        ),
        out_shape=out((rows // part_rows, CHUNKS, part_rows, MODEL_WIDTH), brain_floating),
        compiler_params=pltpu.CompilerParams(vmem_limit_bytes=52 * MIB),
        cost_estimate=takes(cost),
        name="mixture",
    )(*gas, weights, wait)


def at_inner(place_ref):
    return (place_ref[0] == 1) | (place_ref[0] == 2)


def round_kernel(kinds, waits, place_ref, *refs):
    has_own, has_pair, has_next = kinds
    refs = list(refs)

    def take(count):
        taken, refs[:count] = (refs[:count], [])
        return [ref[...].astype(jnp.float32) for ref in taken]

    own = take(2) if has_own else None
    pair = take(2) if has_pair else None
    following = take(1) if has_next else None
    outs = refs[waits:]
    edge = None
    if has_next:
        edge = following[0].reshape(outs[-1].shape)
    if has_own:
        outs.pop(0)[...] = (own[0].reshape(own[1].shape) + own[1]).astype(brain_floating)
    if has_pair:
        total = pair[0] + pair[1]
        outs.pop(0)[...] = total.astype(brain_floating)
        edge = total if edge is None else jnp.where(at_inner(place_ref), total, edge)
    outs.pop(0)[...] = edge.astype(brain_floating)


def run_round(place, own, pair, following, waits):
    steps = GROUP // 2
    arrays, specs, count = ([], [], 0)

    def chunk_spec(source):
        values, at = source
        _, _, shard, width = values.shape
        return pl.BlockSpec((2, 1, shard, width), lambda i, _: (i, at, 0, 0))

    flat = None
    for source in (own[:1] if own else ()) + ((following,) if following else ()):
        flat = (GROUP,) + source[0].shape[2:]
    if pair:
        flat = pair[0].shape
    piece = pl.BlockSpec((2,) + flat[1:], lambda i, _: (i, 0, 0))
    if own:
        arrays += [own[0][0], own[1]]
        specs += [chunk_spec(own[0]), piece]
        count += 1
    if pair:
        arrays += list(pair)
        specs += [piece] * 2
        count += 1
    if following:
        arrays.append(following[0])
        specs.append(chunk_spec(following))
    count += 1
    return pl.pallas_call(
        functools.partial(
            round_kernel, (bool(own), bool(pair), bool(following)), len(waits)
        ),
        grid_spec=pltpu.PrefetchScalarGridSpec(
            num_scalar_prefetch=1,
            grid=(steps,),
            in_specs=specs + [ANYWHERE] * len(waits),
            out_specs=[piece] * count,
        ),
        out_shape=[out(flat, brain_floating)] * count,
        compiler_params=pltpu.CompilerParams(vmem_limit_bytes=40 * MIB),
        cost_estimate=takes(2),
        name="round",
    )(place, *arrays, *waits)


def after_kernel(values_ref, wait_ref, out_ref):
    del values_ref, wait_ref, out_ref


def after(values, wait):
    return pl.pallas_call(
        after_kernel,
        in_specs=[ANYWHERE] * 2,
        out_specs=ANYWHERE,
        out_shape=out(values.shape, values.dtype),
        input_output_aliases={0: 0},
        name="after",
    )(values, wait)


def adam_kernel(turned, rate, shrink, place_ref, t_ref, r_ref, w_ref, m_ref, v_ref, *rest):
    m_out, v_out, w_out = rest[-3:]
    inner = at_inner(place_ref)
    for k in range(t_ref.shape[0]):
        gradient = jnp.where(inner, t_ref[k].astype(jnp.float32), r_ref[k].astype(jnp.float32))
        if turned:
            at = (k,)
            gradient = gradient.T
        else:
            at = (k, 0)
        moment, square, renewed = adamw_step(
            w_ref[at], m_ref[at], v_ref[at], gradient, rate, shrink
        )
        m_out[at] = moment
        v_out[at] = square
        w_out[at] = renewed


def adam_part(place, total, ends, state, local, side, rate, before, wait, cost):
    weight, first, second = state
    turned = side == 2
    shard = total.shape[1]
    held = [] if before is None else list(before)
    if turned:
        spec = pl.BlockSpec((2, F, shard), lambda i, _: (i + local * (GROUP // 2), 0, 0))
    else:
        spec = pl.BlockSpec((2, 1, shard, F), lambda i, _: (i + local * (GROUP // 2), side, 0, 0))
    piece = pl.BlockSpec((2, shard, F), lambda i, _: (i, 0, 0))
    return pl.pallas_call(
        functools.partial(adam_kernel, turned, rate, decay_rate),
        grid_spec=pltpu.PrefetchScalarGridSpec(
            num_scalar_prefetch=1,
            grid=(GROUP // 2,),
            in_specs=[piece, piece, spec, spec, spec] + [ANYWHERE] * (len(held) + 1),
            out_specs=[spec] * 3,
        ),
        out_shape=[out(weight.shape, jnp.float32)] * 3,
        input_output_aliases={6 + i: i for i in range(len(held))},
        compiler_params=pltpu.CompilerParams(vmem_limit_bytes=60 * MIB),
        cost_estimate=takes(cost),
        name="adam",
    )(place, total, ends, weight, first, second, *held, wait)


def rest_kernel(rates, place_ref, t_ref, r_ref, *refs):
    inner = at_inner(place_ref)
    states, outs = (refs[:15], refs[15:])

    def gradient(j):
        return jnp.where(inner, t_ref[j].astype(jnp.float32), r_ref[j].astype(jnp.float32))

    def step(which, at, gradient):
        weight, first, second = states[3 * which : 3 * which + 3]
        rate, shrink = rates[which]
        results = adamw_step(weight[at], first[at], second[at], gradient, rate, shrink)
        for ref, value in zip(outs[3 * which : 3 * which + 3], results):
            ref[at] = value

    small = gradient(PROJECTED // F + 2)[:, :EXTRA]
    step(0, ..., small.T[EXPERTS : EXPERTS + 2, :])
    step(4, ..., small[:, :EXPERTS])
    for half in range(2):
        at = (slice(None), slice(half * F, half * F + F))
        step(1, at, gradient(half))
        step(2, half, gradient(2 + half))
        step(3, at, gradient(4 + half))


def adam_rest(place, total, ends, states, rates):
    flat = [v for state in states for v in state]
    in_vmem = pl.BlockSpec(memory_space=pltpu.VMEM)
    return pl.pallas_call(
        functools.partial(rest_kernel, rates),
        in_specs=[pl.BlockSpec(memory_space=pltpu.SMEM)] + [in_vmem] * (2 + len(flat)),
        out_shape=[out(v.shape, jnp.float32) for v in flat],
        compiler_params=pltpu.CompilerParams(vmem_limit_bytes=40 * MIB),
        name="adam_rest",
    )(place, total, ends, *flat)


fsdp = ("outer", "inner")


def body(
    sizes,
    tokens_in,
    cotangent,
    document_lengths,
    expert_choice,
    norm_gains,
    gains_first,
    gains_second,
    query_weight,
    query_first,
    query_second,
    keyvalue_weight,
    keyvalue_first_moment,
    keyvalue_second_moment,
    output_weight,
    output_first,
    output_second,
    router_weight,
    router_first,
    router_second,
    gateup_weight,
    gateup_first,
    gateup_second,
    down_weight,
    down_first,
    down_second,
):
    replicas, outer = sizes
    count_of_rows = tokens_in.shape[0]
    shard = query_weight.shape[0]
    me = lax.axis_index("inner").astype(jnp.int32).reshape(1)
    place = lax.axis_index("replica").astype(jnp.int32).reshape(1)

    pack_own = jnp.concatenate(
        [
            query_weight,
            keyvalue_weight[0],
            keyvalue_weight[1],
            output_weight,
            router_weight,
            norm_gains.T,
            jnp.zeros((shard, EXTRA - EXPERTS - 2), jnp.float32),
        ],
        axis=1,
    ).astype(brain_floating)
    pack = lax.all_gather(pack_own, fsdp, axis=0, tiled=True)
    at = PROJECTED + MODEL_WIDTH + EXPERTS
    gains_value = pack[:, at : at + 2].astype(jnp.float32).T

    weights = lax.all_to_all(split_by_owner(gateup_weight, down_weight), "inner", 0, 0)
    if outer > 1:
        weights = lax.all_gather(weights, "outer", axis=0, tiled=True)

    position, alive_mask, allowed = layout(document_lengths[0], count_of_rows)
    cosine, sine = rope_tables(position)
    alive = alive_mask[:, None]
    bias = jnp.where(allowed, 0.0, masked_value)

    expert_row = jnp.arange(EXPERTS, dtype=jnp.int32)
    chosen = jnp.any(expert_choice[:, :, None] == expert_row[None, None, :], axis=1)
    mask = jnp.concatenate(
        [
            chosen.astype(brain_floating),
            jnp.zeros((count_of_rows, EXTRA - EXPERTS), brain_floating),
        ],
        axis=1,
    )
    branch = (alive * cotangent.astype(jnp.float32)).astype(brain_floating)
    branch_pack = jnp.concatenate([branch, mask], axis=1)
    part_rows = count_of_rows // CHUNKS

    def gathered(values, c):
        return lax.all_gather(
            values[c * part_rows : (c + 1) * part_rows], "inner", axis=0, tiled=True
        )

    branch_all = lax.all_gather(branch_pack, "inner", axis=0, tiled=True).reshape(
        GROUP, CHUNKS, part_rows, MODEL_WIDTH + EXTRA
    )

    normed, qkv, mixed, totals, middle, normed_two = run_front(
        tokens_in, pack, gains_value, alive, bias, cosine, sine, weights
    )

    x_all, ga_all, dgu_all, dx = ([], [], [], None)
    for c in range(CHUNKS):
        x_part = gathered(normed_two, c)
        ga, dgu, dx = run_experts(
            me, c, x_part, branch_all, weights, pack, () if dx is None else (dx,)
        )
        x_all.append(x_part)
        ga_all.append(ga)
        dgu_all.append(dgu)
    dx_own = lax.psum_scatter(
        dx.reshape(GROUP * count_of_rows, MODEL_WIDTH + EXTRA),
        "inner",
        scatter_dimension=0,
        tiled=True,
    )

    def to_owner(parts):
        if outer > 1:
            parts = lax.psum_scatter(parts, "outer", scatter_dimension=0, tiled=True)
        return lax.all_to_all(parts, "inner", 0, 0)

    def swapped(values):
        return lax.ppermute(values, "replica", [(0, 1), (1, 0), (2, 3), (3, 2)])

    def across(values):
        return lax.ppermute(values, "replica", [(1, 2), (2, 1)])

    def grads_of(local, sides, wait, cost):
        return run_grads(local, sides, shard, x_all, branch_all, ga_all, dgu_all, wait, cost)

    chunks = [(local, side) for local in range(LOCAL) for side in (2, 0, 1)]
    last = len(chunks)
    root = MODEL_WIDTH ** (-0.5)
    states = (
        (gateup_weight, gateup_first, gateup_second),
        (down_weight, down_first, down_second),
    )
    renewed = [None, None]
    by_pairs, totals_of, ends, edges = ({}, {}, {}, {})

    def adam_of(k, wait, cost):
        local, side = chunks[k]
        which = side // 2
        renewed[which] = adam_part(
            place, totals_of[k], ends[k], states[which], local, side,
            (F // 16) ** (-0.5) if which else root, renewed[which], wait, cost,
        )
        return renewed[which][0]

    first = grads_of(0, (2,), dgu_all[-1], 1)
    token = first
    mine = {0: (to_owner(first), 0)}
    for k in range(-1, last + 3):
        own, pair, following, waits = (None, None, None, [])
        if k in edges:
            arrived = swapped(edges[k])
            ends[k - 2] = arrived
            if k <= last:
                own = (mine[k], arrived)
            else:
                waits.append(arrived)
        if k - 1 in by_pairs:
            pair = (by_pairs[k - 1], across(by_pairs[k - 1]))

        if k == -1:
            second = grads_of(0, (0, 1), token, 1)
            done = second
        elif k == 0:
            got = to_owner(after(second, token))
            mine[1], mine[2] = ((got, 0), (got, 1))
            third = grads_of(1, (2, 0, 1), token, 6)
            done = third
        elif k == 1:
            got = to_owner(after(third, token))
            mine[3], mine[4], mine[5] = ((got, 0), (got, 1), (got, 2))
            d_middle, d_mixed, second_grads = run_middle(
                dx_own, normed_two, middle, cotangent, mask, alive, gains_value, pack, mixed, token
            )
            done = d_mixed
        elif k == 2:
            rest_grads, input_gradient = run_back(
                d_mixed, qkv, totals, bias, cosine, sine, normed, tokens_in, d_middle, gains_value,
                second_grads, pack, token, token,
            )
            rest_own = lax.psum_scatter(rest_grads, fsdp, scatter_dimension=0, tiled=True)
            rest_own = jnp.pad(rest_own, ((0, 0), (0, GROUP * F - rest_own.shape[1])))
            rest_own = rest_own.reshape(shard, GROUP, F).swapaxes(0, 1)
            mine[last] = (rest_own.reshape(GROUP, 1, shard, F), 0)
            done = input_gradient
        elif k == 3:
            done = adam_of(0, token, 60)
        elif k == 4:
            mixture = run_mix(ga_all, weights, part_rows, token, 60)
            mixture_own = lax.psum_scatter(
                mixture.reshape(GROUP * count_of_rows, MODEL_WIDTH),
                "inner",
                scatter_dimension=0,
                tiled=True,
            )
            done = mixture
        elif k == 5:
            done = adam_of(2, adam_of(1, token, 60), 1)
        elif k - 3 < len(chunks):
            done = adam_of(k - 3, token, 60)
        waits.append(done)

        if k + 1 <= last:
            following = mine[k + 1]
        if k == last + 2:
            continue
        results = list(run_round(place, own, pair, following, waits))
        token = results[0]
        if own:
            by_pairs[k] = results.pop(0)
        if pair:
            totals_of[k - 1] = results.pop(0)
        edges[k + 1] = results.pop(0)

    block_output = (middle + alive * mixture_own.astype(jnp.float32)).astype(brain_floating)

    rest_states = (
        (norm_gains, gains_first, gains_second),
        (query_weight, query_first, query_second),
        (keyvalue_weight, keyvalue_first_moment, keyvalue_second_moment),
        (output_weight, output_first, output_second),
        (router_weight, router_first, router_second),
    )
    rates = (
        (gain_rate, 0.0),
        (root, decay_rate),
        (root, decay_rate),
        ((WIDTH // 16) ** (-0.5), decay_rate),
        ((4 * MODEL_WIDTH) ** (-0.5), decay_rate),
    )
    updated = adam_rest(place, totals_of[last], ends[last], rest_states, rates)
    return (block_output, input_gradient) + tuple(updated) + tuple(renewed[0]) + tuple(renewed[1])


def solution(mesh):
    replicas, shards = (mesh.shape["replica"], mesh.shape["fsdp"])
    outer = shards // GROUP
    split = Mesh(mesh.devices.reshape(replicas, outer, GROUP), ("replica",) + fsdp)
    rows = P(("replica",) + fsdp, None)
    by_first = P(fsdp, None)
    by_second = P(None, fsdp)
    by_middle = P(None, fsdp, None)
    by_third = P(None, None, fsdp, None)
    by_last = P(None, None, fsdp)
    weights = (by_second, by_first, by_middle, by_first, by_first, by_third, by_last)
    states = tuple(spec for spec in weights for _ in range(3))
    return jax.shard_map(
        functools.partial(body, (replicas, outer)),
        mesh=split,
        in_specs=(rows,) * 4 + states,
        out_specs=(rows,) * 2 + states,
        check_vma=False,
    )
```

```python
import functools
import math

import jax
import jax.numpy as jnp
from jax import lax
from jax.experimental import pallas as pl
from jax.experimental.pallas import tpu as pltpu
from jax.sharding import Mesh
from jax.sharding import PartitionSpec as P

MODEL_WIDTH = 1024
QUERY_HEADS = 16
KEYVALUE_HEADS = 8
HEAD_SIZE = 64
F = 512
TOPK = 8
EXPERTS = 16
ADAM_STEP = 5
GROUP = 8
LOCAL = EXPERTS // GROUP
EXTRA = 128
CHUNKS = 2
TILE = 512
SPAN = 256
LANES = 128
WIDTH = QUERY_HEADS * HEAD_SIZE
KV_WIDTH = KEYVALUE_HEADS * HEAD_SIZE
PROJECTED = WIDTH + 2 * KV_WIDTH
SCORE_SCALE = HEAD_SIZE ** (-0.5)
ROUTER_BLOCK = (PROJECTED + MODEL_WIDTH) // EXTRA


norm_eps = 1e-06
rope_base = 10000.0
beta_one = 0.9
beta_two = 0.95
adam_eps = 1e-08
decay_rate = 0.1
gain_rate = 0.25
masked_value = -1e30
brain_floating = jnp.bfloat16


def layout(lengths, count_of_rows):
    document_ends = jnp.cumsum(lengths)
    row_index = jnp.arange(count_of_rows, dtype=jnp.int32)
    passed = row_index[:, None] >= document_ends[None, :]
    segment = jnp.sum(passed.astype(jnp.int32), axis=1)
    start_row = jnp.sum(jnp.where(passed, lengths[None, :], 0), axis=1)
    position = (row_index - start_row).astype(jnp.float32)
    alive_mask = (segment < lengths.shape[0]).astype(jnp.float32)
    allowed = (segment[:, None] == segment[None, :]) & (row_index[None, :] <= row_index[:, None])
    return (position, alive_mask, allowed)


def rope_tables(position):
    half_width = HEAD_SIZE // 2
    exponents = jnp.arange(half_width, dtype=jnp.float32) * (2.0 / HEAD_SIZE)
    inverse = jnp.exp(exponents * -math.log(rope_base))
    angles = position[:, None] * inverse[None, :]
    cosine, sine = (jnp.cos(angles), jnp.sin(angles))
    return (
        jnp.concatenate([cosine] * 4, axis=1),
        jnp.concatenate([-sine, sine, -sine, sine], axis=1),
    )


def product(left, right):
    return jnp.dot(left, right, preferred_element_type=jnp.float32)


def times_transposed(left, right):
    return lax.dot_general(
        left, right, (((1,), (1,)), ((), ())), preferred_element_type=jnp.float32
    )


def transposed_times(left, right):
    return lax.dot_general(
        left, right, (((0,), (0,)), ((), ())), preferred_element_type=jnp.float32
    )


def normalize(values):
    inverse = lax.rsqrt(jnp.mean(values * values, axis=-1, keepdims=True) + norm_eps)
    return (values * inverse, inverse)


def norm_back(upstream, scaled_rows, inverse, gain_row):
    weighted = upstream * gain_row
    inner = jnp.mean(weighted * scaled_rows, axis=-1, keepdims=True)
    return inverse * (weighted - scaled_rows * inner)


def column_sums(values):
    ones = jnp.ones((values.shape[0], LANES), brain_floating)
    high = values.astype(brain_floating)
    low = (values - high.astype(jnp.float32)).astype(brain_floating)
    return transposed_times(high, ones) + transposed_times(low, ones)


def lanes_of(shape):
    return lax.broadcasted_iota(jnp.int32, shape, 1)


def rotate(values, cosine, sine):
    half = HEAD_SIZE // 2
    front = lax.rem(lanes_of(values.shape), HEAD_SIZE) < half
    swapped = jnp.where(
        front, pltpu.roll(values, LANES - half, 1), pltpu.roll(values, half, 1)
    )
    return values * cosine + swapped * sine


def both_halves(values, which):
    turned = pltpu.roll(values, HEAD_SIZE, 1)
    first = lanes_of(values.shape) < HEAD_SIZE
    return jnp.where(first == (which == 0), values, turned)


def only_half(values, which):
    first = lanes_of(values.shape) < HEAD_SIZE
    return jnp.where(first == (which == 0), values, 0.0)


def gates_of(rows, router, mask):
    logits = product(rows, router)
    peak = jnp.max(jnp.where(mask, logits, masked_value), axis=1, keepdims=True)
    weights = jnp.where(mask, jnp.exp(logits - peak), 0.0)
    return weights / jnp.sum(weights, axis=1, keepdims=True)


def adamw_step(weight, moment_old, square_old, gradient, step_rate, shrink):
    moment = beta_one * moment_old + (1.0 - beta_one) * gradient
    square = beta_two * square_old + (1.0 - beta_two) * gradient * gradient
    moment_hat = moment / (1.0 - beta_one**ADAM_STEP)
    square_hat = square / (1.0 - beta_two**ADAM_STEP)
    renewed = weight - step_rate * (
        moment_hat / (jnp.sqrt(square_hat) + adam_eps) + shrink * weight
    )
    return (moment, square, renewed)


MIB = 1024 * 1024
ANYWHERE = pl.BlockSpec(memory_space=pl.ANY)


def takes(microseconds):
    return pl.CostEstimate(
        flops=int(microseconds * 1e9), bytes_accessed=int(microseconds * 3.6e6), transcendentals=0
    )


def whole(shape):
    return pl.BlockSpec(shape, lambda *_: (0,) * len(shape), pipeline_mode=pl.Buffered(1))


def part(shape, place):
    return pl.BlockSpec(shape, lambda *_: place, pipeline_mode=pl.Buffered(1))


def out(shape, dtype):
    return jax.ShapeDtypeStruct(shape, dtype)


def split_kernel(gateup_ref, down_ref, out_ref):
    for k in range(2):
        out_ref[k, 0, 0] = gateup_ref[k, 0].astype(brain_floating)
        out_ref[k, 0, 1] = gateup_ref[k, 1].astype(brain_floating)
        out_ref[k, 0, 2] = down_ref[k].T.astype(brain_floating)


def split_by_owner(gateup, down):
    shard = gateup.shape[2]
    steps = GROUP // 2
    return pl.pallas_call(
        split_kernel,
        grid=(EXPERTS // 2,),
        in_specs=[
            pl.BlockSpec((2, 2, shard, F), lambda e: (e, 0, 0, 0)),
            pl.BlockSpec((2, F, shard), lambda e: (e, 0, 0)),
        ],
        out_specs=pl.BlockSpec(
            (2, 1, 3, shard, F), lambda e: (lax.rem(e, steps), e // steps, 0, 0, 0)
        ),
        out_shape=out((GROUP, LOCAL, 3, shard, F), brain_floating),
        name="split",
    )(gateup, down)


def front_kernel(
    x_ref, pack_ref, gains_ref, alive_ref, bias_ref, cos_ref, sin_ref, wait_ref, normed_ref, qkv_ref, mixed_ref, totals_ref, middle_ref, normed_two_ref, linear_ref,
):
    rows = x_ref.shape[0]
    scaled, _ = normalize(x_ref[...].astype(jnp.float32))
    normed = (scaled * gains_ref[0:1, :]).astype(brain_floating)
    normed_ref[...] = normed
    linear_ref[...] = product(normed, pack_ref[:, :PROJECTED])
    cosine, sine = (cos_ref[...], sin_ref[...])
    for at in range(0, WIDTH + KV_WIDTH, LANES):
        qkv_ref[:, at : at + LANES] = rotate(
            linear_ref[:, at : at + LANES], cosine, sine
        ).astype(brain_floating)
    qkv_ref[:, WIDTH + KV_WIDTH :] = linear_ref[:, WIDTH + KV_WIDTH :].astype(brain_floating)
    totals_ref[...] = jnp.zeros_like(totals_ref)

    @pl.loop(0, KEYVALUE_HEADS // 2)
    def _(pair):
        at = pl.multiple_of(pair * LANES, LANES)
        keys = qkv_ref[:, pl.ds(WIDTH + at, LANES)].astype(jnp.float32)
        values = qkv_ref[:, pl.ds(WIDTH + KV_WIDTH + at, LANES)].astype(jnp.float32)
        for a in range(2):
            head_keys = both_halves(keys, a).astype(brain_floating)
            head_values = both_halves(values, a)
            place = pl.multiple_of((2 * pair + a) * LANES, LANES)
            queries = qkv_ref[:, pl.ds(place, LANES)].astype(jnp.float32)
            for start in range(0, rows, SPAN):
                seen = min(start + SPAN, rows)
                mixed = jnp.zeros((SPAN, LANES), jnp.float32)
                for j in range(2):
                    head = 2 * (2 * pair + a) + j
                    query = only_half(queries[start : start + SPAN], j).astype(brain_floating)
                    scores = (
                        times_transposed(query, head_keys[:seen]) * SCORE_SCALE
                        + bias_ref[start : start + SPAN, :seen]
                    )
                    peak = jnp.max(scores, axis=1, keepdims=True)
                    weights = jnp.exp(scores - peak)
                    total = jnp.sum(weights, axis=1, keepdims=True)
                    probs = (weights * (1.0 / total)).astype(brain_floating)
                    mixed += product(probs, only_half(head_values[:seen], j).astype(brain_floating))
                    held = totals_ref[start : start + SPAN, :]
                    totals_ref[start : start + SPAN, :] = jnp.where(
                        lanes_of(held.shape) == head, peak + jnp.log(total), held
                    )
                mixed_ref[start : start + SPAN, pl.ds(place, LANES)] = mixed.astype(brain_floating)

    attended = product(mixed_ref[...], pack_ref[:, PROJECTED : PROJECTED + MODEL_WIDTH])
    middle = x_ref[...].astype(jnp.float32) + alive_ref[...] * attended
    middle_ref[...] = middle
    scaled_two, _ = normalize(middle)
    normed_two_ref[...] = (scaled_two * gains_ref[1:2, :]).astype(brain_floating)


def run_front(x, pack, gains, alive, bias, cosine, sine, wait):
    rows = x.shape[0]
    return pl.pallas_call(
        front_kernel,
        in_specs=[pl.BlockSpec(memory_space=pltpu.VMEM)] * 7 + [ANYWHERE],
        out_shape=[
            out((rows, MODEL_WIDTH), brain_floating),
            out((rows, PROJECTED), brain_floating),
            out((rows, WIDTH), brain_floating),
            out((rows, LANES), jnp.float32),
            out((rows, MODEL_WIDTH), jnp.float32),
            out((rows, MODEL_WIDTH), brain_floating),
        ],
        scratch_shapes=[pltpu.VMEM((rows, PROJECTED), jnp.float32)],
        compiler_params=pltpu.CompilerParams(vmem_limit_bytes=52 * MIB),
        name="front",
    )(x, pack, gains, alive, bias, cosine, sine, wait)


def middle_kernel(
    dx_ref, normed_two_ref, middle_ref, cot_ref, mask_ref, alive_ref, gains_ref, router_ref,
    output_ref, mixed_ref, wait_ref, d_middle_ref, d_mixed_ref, grads_ref,
):
    dx = dx_ref[...].astype(jnp.float32)
    normed_two = normed_two_ref[...]
    mask = mask_ref[...].astype(jnp.float32) > 0.5
    gates = gates_of(normed_two, router_ref[...], mask)
    extra = dx[:, MODEL_WIDTH:]
    d_gates = extra + pltpu.roll(extra, LANES - EXPERTS, 1)
    d_logits = (
        gates * (d_gates - jnp.sum(gates * d_gates, axis=1, keepdims=True))
    ).astype(brain_floating)
    d_normed = dx[:, :MODEL_WIDTH] + times_transposed(d_logits, router_ref[...])
    scaled, inverse = normalize(middle_ref[...])
    d_middle = cot_ref[...].astype(jnp.float32) + norm_back(
        d_normed, scaled, inverse, gains_ref[1:2, :]
    )
    d_middle_ref[...] = d_middle
    d_attended = (alive_ref[...] * d_middle).astype(brain_floating)
    grads_ref[:, :MODEL_WIDTH] = transposed_times(mixed_ref[...], d_attended).astype(brain_floating)
    small = transposed_times(normed_two, d_logits)
    small = jnp.where(lanes_of(small.shape) == EXPERTS + 1, column_sums(d_normed * scaled), small)
    grads_ref[:, MODEL_WIDTH:] = small.astype(brain_floating)
    d_mixed_ref[...] = times_transposed(d_attended, output_ref[...]).astype(brain_floating)


def run_middle(dx, normed_two, middle, cot, mask, alive, gains, pack, mixed, wait):
    rows = middle.shape[0]
    full = [whole(v.shape) for v in (dx, normed_two, middle, cot, mask, alive, gains)]
    return pl.pallas_call(
        middle_kernel,
        grid=(1,),
        in_specs=full
        + [
            part((MODEL_WIDTH, EXTRA), (0, ROUTER_BLOCK)),
            part((WIDTH, MODEL_WIDTH), (0, PROJECTED // MODEL_WIDTH)),
            whole(mixed.shape),
            ANYWHERE,
        ],
        out_specs=[
            whole((rows, MODEL_WIDTH)),
            whole((rows, WIDTH)),
            whole((MODEL_WIDTH, MODEL_WIDTH + EXTRA)),
        ],
        out_shape=[
            out((rows, MODEL_WIDTH), jnp.float32),
            out((rows, WIDTH), brain_floating),
            out((MODEL_WIDTH, MODEL_WIDTH + EXTRA), brain_floating),
        ],
        compiler_params=pltpu.CompilerParams(vmem_limit_bytes=52 * MIB),
        cost_estimate=takes(30),
        name="middle_back",
    )(dx, normed_two, middle, cot, mask, alive, gains, pack, pack, mixed, wait)


def back_kernel(
    d_mixed_ref, qkv_ref, totals_ref, bias_ref, cos_ref, sin_ref, normed_ref, x_ref, d_middle_ref,
    gains_ref, other_ref, pack_ref, wait_ref, also_ref, grads_ref, d_input_ref, d_linear_ref, d_keys_ref, d_values_ref,
):
    rows = x_ref.shape[0]
    cosine, sine = (cos_ref[...], -sin_ref[...])

    @pl.loop(0, KEYVALUE_HEADS // 2)
    def _(pair):
        at = pl.multiple_of(pair * LANES, LANES)
        keys = qkv_ref[:, pl.ds(WIDTH + at, LANES)].astype(jnp.float32)
        values = qkv_ref[:, pl.ds(WIDTH + KV_WIDTH + at, LANES)].astype(jnp.float32)
        pair_keys = jnp.zeros((rows, LANES), jnp.float32)
        pair_values = jnp.zeros((rows, LANES), jnp.float32)
        for a in range(2):
            both_keys = both_halves(keys, a)
            head_keys = both_keys.astype(brain_floating)
            head_values = both_halves(values, a).astype(brain_floating)
            place = pl.multiple_of((2 * pair + a) * LANES, LANES)
            queries = qkv_ref[:, pl.ds(place, LANES)].astype(jnp.float32)
            d_outs = d_mixed_ref[:, pl.ds(place, LANES)].astype(jnp.float32)
            d_keys_ref[...] = jnp.zeros_like(d_keys_ref)
            d_values_ref[...] = jnp.zeros_like(d_values_ref)
            for start in range(0, rows, SPAN):
                seen = min(start + SPAN, rows)
                d_query = jnp.zeros((SPAN, LANES), jnp.float32)
                for j in range(2):
                    head = 2 * (2 * pair + a) + j
                    query = only_half(queries[start : start + SPAN], j).astype(brain_floating)
                    d_out = only_half(d_outs[start : start + SPAN], j).astype(brain_floating)
                    held = totals_ref[start : start + SPAN, :]
                    total = jnp.sum(
                        jnp.where(lanes_of(held.shape) == head, held, 0.0), axis=1, keepdims=True
                    )
                    scores = (
                        times_transposed(query, head_keys[:seen]) * SCORE_SCALE
                        + bias_ref[start : start + SPAN, :seen]
                    )
                    probs = jnp.exp(scores - total)
                    d_probs = times_transposed(d_out, head_values[:seen])
                    inner = jnp.sum(probs * d_probs, axis=1, keepdims=True)
                    d_scores = (probs * (d_probs - inner)).astype(brain_floating)
                    d_query += product(
                        d_scores, only_half(both_keys[:seen], j).astype(brain_floating)
                    )
                    d_keys_ref[:seen, :] += transposed_times(d_scores, query)
                    d_values_ref[:seen, :] += transposed_times(probs.astype(brain_floating), d_out)
                d_linear_ref[start : start + SPAN, pl.ds(place, LANES)] = rotate(
                    d_query * SCORE_SCALE,
                    cosine[start : start + SPAN],
                    sine[start : start + SPAN],
                ).astype(brain_floating)
            d_keys = d_keys_ref[...]
            d_values = d_values_ref[...]
            pair_keys += only_half(d_keys + pltpu.roll(d_keys, HEAD_SIZE, 1), a)
            pair_values += only_half(d_values + pltpu.roll(d_values, HEAD_SIZE, 1), a)
        d_linear_ref[:, pl.ds(WIDTH + at, LANES)] = rotate(
            pair_keys * SCORE_SCALE, cosine, sine
        ).astype(brain_floating)
        d_linear_ref[:, pl.ds(WIDTH + KV_WIDTH + at, LANES)] = pair_values.astype(brain_floating)

    normed = normed_ref[...]
    for at in range(0, PROJECTED, 512):
        grads_ref[:, at : at + 512] = transposed_times(
            normed, d_linear_ref[:, at : at + 512]
        ).astype(brain_floating)
    d_normed = times_transposed(d_linear_ref[...], pack_ref[...])
    scaled, inverse = normalize(x_ref[...].astype(jnp.float32))
    sums = column_sums(d_normed * scaled)
    grads_ref[:, PROJECTED : PROJECTED + MODEL_WIDTH] = other_ref[:, :MODEL_WIDTH]
    small = other_ref[:, MODEL_WIDTH:].astype(jnp.float32)
    grads_ref[:, PROJECTED + MODEL_WIDTH :] = jnp.where(
        lanes_of(sums.shape) == EXPERTS, sums, small
    ).astype(brain_floating)
    d_input_ref[...] = d_middle_ref[...] + norm_back(d_normed, scaled, inverse, gains_ref[0:1, :])


def run_back(
    d_mixed, qkv, totals, bias, cosine, sine, normed, x, d_middle, gains, other, pack, wait, also
):
    rows = x.shape[0]
    held = (d_mixed, qkv, totals, bias, cosine, sine, normed, x, d_middle, gains, other)
    width = PROJECTED + other.shape[1]
    return pl.pallas_call(
        back_kernel,
        grid=(1,),
        in_specs=[whole(v.shape) for v in held]
        + [part((MODEL_WIDTH, PROJECTED), (0, 0)), ANYWHERE, ANYWHERE],
        out_specs=[whole((MODEL_WIDTH, width)), whole((rows, MODEL_WIDTH))],
        out_shape=[
            out((MODEL_WIDTH, width), brain_floating),
            out((rows, MODEL_WIDTH), jnp.float32),
        ],
        scratch_shapes=[
            pltpu.VMEM((rows, PROJECTED), brain_floating),
            pltpu.VMEM((rows, LANES), jnp.float32),
            pltpu.VMEM((rows, LANES), jnp.float32),
        ],
        compiler_params=pltpu.CompilerParams(vmem_limit_bytes=52 * MIB),
        cost_estimate=takes(30),
        name="attention_back",
    )(*held, pack, wait, also)


def expert_kernel(me_ref, x_ref, b_ref, w_ref, router_ref, *refs):
    ga_ref, dgu_ref, dx_ref = refs[-3:]
    x = x_ref[...]
    branch = b_ref[:, 0, :, :MODEL_WIDTH].reshape(x.shape)
    mask = b_ref[:, 0, :, MODEL_WIDTH:].reshape(x.shape[0], EXTRA).astype(jnp.float32) > 0.5
    gates = gates_of(x, router_ref[...], mask)
    lane = lanes_of(gates.shape)
    d_gates = jnp.zeros_like(gates)
    dx = jnp.zeros((x.shape[0], MODEL_WIDTH), jnp.float32)
    for local in range(LOCAL):
        expert = me_ref[0] + GROUP * local
        gate_weight, up_weight, down_weight = (
            w_ref[:, local, p].reshape(MODEL_WIDTH, F) for p in range(3)
        )
        gate = jnp.sum(jnp.where(lane == expert, gates, 0.0), axis=1, keepdims=True)
        gate_linear = product(x, gate_weight)
        up_linear = product(x, up_weight)
        back = product(branch, down_weight)
        sig = jax.nn.sigmoid(gate_linear)
        silu = gate_linear * sig
        act = silu * up_linear
        ga_ref[:, local * F : (local + 1) * F] = (gate * act).astype(brain_floating)
        d_gate = jnp.sum(act * back, axis=1, keepdims=True)
        high = d_gate.astype(brain_floating).astype(jnp.float32)
        d_gates += jnp.where(lane == expert, high, 0.0)
        d_gates += jnp.where(lane == expert + EXPERTS, d_gate - high, 0.0)
        d_act = gate * back
        d_gl = (d_act * up_linear * (sig + silu * (1.0 - sig))).astype(brain_floating)
        d_ul = (d_act * silu).astype(brain_floating)
        dgu_ref[:, 2 * local * F : (2 * local + 1) * F] = d_gl
        dgu_ref[:, (2 * local + 1) * F : (2 * local + 2) * F] = d_ul
        dx += times_transposed(d_gl, gate_weight) + times_transposed(d_ul, up_weight)
    blocks, _, part_rows, _ = dx_ref.shape
    dx_ref[:, 0, :, :MODEL_WIDTH] = dx.astype(brain_floating).reshape(
        blocks, part_rows, MODEL_WIDTH
    )
    dx_ref[:, 0, :, MODEL_WIDTH:] = d_gates.astype(brain_floating).reshape(
        blocks, part_rows, EXTRA
    )


def run_experts(me, c, x, b, weights, pack, before):
    rows = x.shape[0]
    part_rows = b.shape[2]
    tile = 2 * part_rows
    wide = MODEL_WIDTH + EXTRA

    def rowed(width):
        return pl.BlockSpec((tile, width), lambda i, me_ref: (i, 0))

    return pl.pallas_call(
        expert_kernel,
        grid_spec=pltpu.PrefetchScalarGridSpec(
            num_scalar_prefetch=1,
            grid=(rows // tile,),
            in_specs=[
                rowed(MODEL_WIDTH),
                pl.BlockSpec((2, 1, part_rows, wide), lambda i, me_ref: (i, c, 0, 0)),
                whole(weights.shape),
                part((MODEL_WIDTH, EXTRA), (0, ROUTER_BLOCK)),
            ]
            + [ANYWHERE] * len(before),
            out_specs=[
                rowed(LOCAL * F),
                rowed(2 * LOCAL * F),
                pl.BlockSpec((2, 1, part_rows, wide), lambda i, me_ref: (i, c, 0, 0)),
            ],
        ),
        out_shape=[
            out((rows, LOCAL * F), brain_floating),
            out((rows, 2 * LOCAL * F), brain_floating),
            out((rows // part_rows, CHUNKS, part_rows, wide), brain_floating),
        ],
        input_output_aliases={5 + i: 2 for i in range(len(before))},
        compiler_params=pltpu.CompilerParams(vmem_limit_bytes=56 * MIB),
        name="experts",
    )(me, x, b, weights, pack, *before)


def chunked_specs(steps, shape, place):
    def index(c):
        return lambda i, *_: place(jnp.clip(i - c * steps, 0, steps - 1), c)

    return [pl.BlockSpec(shape, index(c)) for c in range(CHUNKS)]


def grads_kernel(steps, sides, *refs):
    count = len(sides)
    ins, out_ref, sums = (refs[: CHUNKS * 2 * count], refs[-count - 1], refs[-count:])
    blocks, _, shard, _ = out_ref.shape
    i = pl.program_id(0)

    @pl.when(i == 0)
    def _():
        for total in sums:
            total[...] = jnp.zeros_like(total)

    for c in range(CHUNKS):

        @pl.when(i // steps == c)
        def _():
            for k in range(count):
                left, right = (ins[2 * (k * CHUNKS + c)], ins[2 * (k * CHUNKS + c) + 1])
                sums[k][...] += transposed_times(
                    left[...].reshape(right.shape[0], MODEL_WIDTH), right[...]
                )

    @pl.when(i == CHUNKS * steps - 1)
    def _():
        for k, total in enumerate(sums):
            out_ref[:, k] = total[...].astype(brain_floating).reshape(blocks, shard, F)


def run_grads(local, sides, shard, xs, b, gas, dgus, wait, cost):
    blocks = MODEL_WIDTH // shard
    rows, part_rows = (xs[0].shape[0], b.shape[2])
    tile = 2 * part_rows
    steps = rows // tile
    specs, arrays = ([], [])
    for side in sides:
        if side == 2:
            left = chunked_specs(
                steps, (2, 1, part_rows, MODEL_WIDTH), lambda i, c: (i, c, 0, 0)
            )
            right = chunked_specs(steps, (tile, F), lambda i, c: (i, local))
        else:
            left = chunked_specs(steps, (tile, MODEL_WIDTH), lambda i, c: (i, 0))
            right = chunked_specs(
                steps, (tile, F), lambda i, c, side=side: (i, 2 * local + side)
            )
        for c in range(CHUNKS):
            specs += [left[c], right[c]]
            arrays += [b, gas[c]] if side == 2 else [xs[c], dgus[c]]
    return pl.pallas_call(
        functools.partial(grads_kernel, steps, sides),
        grid=(CHUNKS * steps,),
        in_specs=specs + [ANYWHERE],
        out_specs=whole((blocks, len(sides), shard, F)),
        out_shape=out((blocks, len(sides), shard, F), brain_floating),
        scratch_shapes=[pltpu.VMEM((MODEL_WIDTH, F), jnp.float32)] * len(sides),
        compiler_params=pltpu.CompilerParams(vmem_limit_bytes=52 * MIB),
        cost_estimate=takes(cost),
        name="grads",
    )(*arrays, wait)


def mix_kernel(steps, *refs):
    gas, w_ref, out_ref = (refs[:CHUNKS], refs[CHUNKS], refs[-1])
    for c in range(CHUNKS):

        @pl.when(pl.program_id(0) // steps == c)
        def _():
            total = jnp.zeros((gas[c].shape[0], MODEL_WIDTH), jnp.float32)
            for local in range(LOCAL):
                total += times_transposed(
                    gas[c][:, local * F : (local + 1) * F],
                    w_ref[:, local, 0].reshape(MODEL_WIDTH, F),
                )
            out_ref[...] = total.astype(brain_floating).reshape(out_ref.shape)


def run_mix(gas, weights, part_rows, wait, cost):
    rows = gas[0].shape[0]
    tile = 2 * part_rows
    steps = rows // tile
    blocks, _, _, shard, _ = weights.shape
    return pl.pallas_call(
        functools.partial(mix_kernel, steps),
        grid=(CHUNKS * steps,),
        in_specs=chunked_specs(steps, (tile, LOCAL * F), lambda i, c: (i, 0))
        + [part((blocks, LOCAL, 1, shard, F), (0, 0, 2, 0, 0)), ANYWHERE],
        out_specs=pl.BlockSpec(
            (2, 1, part_rows, MODEL_WIDTH), lambda i: (lax.rem(i, steps), i // steps, 0, 0)
        ),
        out_shape=out((rows // part_rows, CHUNKS, part_rows, MODEL_WIDTH), brain_floating),
        compiler_params=pltpu.CompilerParams(vmem_limit_bytes=52 * MIB),
        cost_estimate=takes(cost),
        name="mixture",
    )(*gas, weights, wait)


def at_inner(place_ref):
    return (place_ref[0] == 1) | (place_ref[0] == 2)


def round_kernel(kinds, waits, place_ref, *refs):
    has_own, has_pair, has_next = kinds
    refs = list(refs)

    def take(count):
        taken, refs[:count] = (refs[:count], [])
        return [ref[...].astype(jnp.float32) for ref in taken]

    own = take(2) if has_own else None
    pair = take(2) if has_pair else None
    following = take(1) if has_next else None
    outs = refs[waits:]
    edge = None
    if has_next:
        edge = following[0].reshape(outs[-1].shape)
    if has_own:
        outs.pop(0)[...] = (own[0].reshape(own[1].shape) + own[1]).astype(brain_floating)
    if has_pair:
        total = pair[0] + pair[1]
        outs.pop(0)[...] = total.astype(brain_floating)
        edge = total if edge is None else jnp.where(at_inner(place_ref), total, edge)
    outs.pop(0)[...] = edge.astype(brain_floating)


def run_round(place, own, pair, following, waits):
    steps = GROUP // 2
    arrays, specs, count = ([], [], 0)

    def chunk_spec(source):
        values, at = source
        _, _, shard, width = values.shape
        return pl.BlockSpec((2, 1, shard, width), lambda i, _: (i, at, 0, 0))

    flat = None
    for source in (own[:1] if own else ()) + ((following,) if following else ()):
        flat = (GROUP,) + source[0].shape[2:]
    if pair:
        flat = pair[0].shape
    piece = pl.BlockSpec((2,) + flat[1:], lambda i, _: (i, 0, 0))
    if own:
        arrays += [own[0][0], own[1]]
        specs += [chunk_spec(own[0]), piece]
        count += 1
    if pair:
        arrays += list(pair)
        specs += [piece] * 2
        count += 1
    if following:
        arrays.append(following[0])
        specs.append(chunk_spec(following))
    count += 1
    return pl.pallas_call(
        functools.partial(
            round_kernel, (bool(own), bool(pair), bool(following)), len(waits)
        ),
        grid_spec=pltpu.PrefetchScalarGridSpec(
            num_scalar_prefetch=1,
            grid=(steps,),
            in_specs=specs + [ANYWHERE] * len(waits),
            out_specs=[piece] * count,
        ),
        out_shape=[out(flat, brain_floating)] * count,
        compiler_params=pltpu.CompilerParams(vmem_limit_bytes=40 * MIB),
        cost_estimate=takes(2),
        name="round",
    )(place, *arrays, *waits)


def after_kernel(values_ref, wait_ref, out_ref):
    del values_ref, wait_ref, out_ref


def after(values, wait):
    return pl.pallas_call(
        after_kernel,
        in_specs=[ANYWHERE] * 2,
        out_specs=ANYWHERE,
        out_shape=out(values.shape, values.dtype),
        input_output_aliases={0: 0},
        name="after",
    )(values, wait)


def adam_kernel(turned, rate, shrink, place_ref, t_ref, r_ref, w_ref, m_ref, v_ref, *rest):
    m_out, v_out, w_out, token_ref = rest[-4:]
    token_ref[...] = jnp.zeros_like(token_ref)
    inner = at_inner(place_ref)
    for k in range(t_ref.shape[0]):
        gradient = jnp.where(inner, t_ref[k].astype(jnp.float32), r_ref[k].astype(jnp.float32))
        if turned:
            at = (k,)
            gradient = gradient.T
        else:
            at = (k, 0)
        moment, square, renewed = adamw_step(
            w_ref[at], m_ref[at], v_ref[at], gradient, rate, shrink
        )
        m_out[at] = moment
        v_out[at] = square
        w_out[at] = renewed


def adam_part(place, total, ends, state, local, side, rate, before, wait, cost):
    weight, first, second = state
    turned = side == 2
    shard = total.shape[1]
    held = [] if before is None else list(before)
    if turned:
        spec = pl.BlockSpec((2, F, shard), lambda i, _: (i + local * (GROUP // 2), 0, 0))
    else:
        spec = pl.BlockSpec((2, 1, shard, F), lambda i, _: (i + local * (GROUP // 2), side, 0, 0))
    piece = pl.BlockSpec((2, shard, F), lambda i, _: (i, 0, 0))
    return pl.pallas_call(
        functools.partial(adam_kernel, turned, rate, decay_rate),
        grid_spec=pltpu.PrefetchScalarGridSpec(
            num_scalar_prefetch=1,
            grid=(GROUP // 2,),
            in_specs=[piece, piece, spec, spec, spec] + [ANYWHERE] * (len(held) + 1),
            out_specs=[spec] * 3 + [pl.BlockSpec((8, LANES), lambda i, _: (0, 0))],
        ),
        out_shape=[out(weight.shape, jnp.float32)] * 3 + [out((8, LANES), jnp.float32)],
        input_output_aliases={6 + i: i for i in range(len(held))},
        compiler_params=pltpu.CompilerParams(vmem_limit_bytes=60 * MIB),
        cost_estimate=takes(cost),
        name="adam",
    )(place, total, ends, weight, first, second, *held, wait)


def rest_kernel(rates, place_ref, t_ref, r_ref, *refs):
    inner = at_inner(place_ref)
    states, outs = (refs[:15], refs[15:])

    def gradient(j):
        return jnp.where(inner, t_ref[j].astype(jnp.float32), r_ref[j].astype(jnp.float32))

    def step(which, at, gradient):
        weight, first, second = states[3 * which : 3 * which + 3]
        rate, shrink = rates[which]
        results = adamw_step(weight[at], first[at], second[at], gradient, rate, shrink)
        for ref, value in zip(outs[3 * which : 3 * which + 3], results):
            ref[at] = value

    small = gradient(PROJECTED // F + 2)[:, :EXTRA]
    step(0, ..., small.T[EXPERTS : EXPERTS + 2, :])
    step(4, ..., small[:, :EXPERTS])
    for half in range(2):
        at = (slice(None), slice(half * F, half * F + F))
        step(1, at, gradient(half))
        step(2, half, gradient(2 + half))
        step(3, at, gradient(4 + half))


def adam_rest(place, total, ends, states, rates):
    flat = [v for state in states for v in state]
    in_vmem = pl.BlockSpec(memory_space=pltpu.VMEM)
    return pl.pallas_call(
        functools.partial(rest_kernel, rates),
        in_specs=[pl.BlockSpec(memory_space=pltpu.SMEM)] + [in_vmem] * (2 + len(flat)),
        out_shape=[out(v.shape, jnp.float32) for v in flat],
        compiler_params=pltpu.CompilerParams(vmem_limit_bytes=40 * MIB),
        name="adam_rest",
    )(place, total, ends, *flat)


fsdp = ("outer", "inner")


def body(
    sizes,
    tokens_in,
    cotangent,
    document_lengths,
    expert_choice,
    norm_gains,
    gains_first,
    gains_second,
    query_weight,
    query_first,
    query_second,
    keyvalue_weight,
    keyvalue_first_moment,
    keyvalue_second_moment,
    output_weight,
    output_first,
    output_second,
    router_weight,
    router_first,
    router_second,
    gateup_weight,
    gateup_first,
    gateup_second,
    down_weight,
    down_first,
    down_second,
):
    replicas, outer = sizes
    count_of_rows = tokens_in.shape[0]
    shard = query_weight.shape[0]
    me = lax.axis_index("inner").astype(jnp.int32).reshape(1)
    place = lax.axis_index("replica").astype(jnp.int32).reshape(1)

    pack_own = jnp.concatenate(
        [
            query_weight,
            keyvalue_weight[0],
            keyvalue_weight[1],
            output_weight,
            router_weight,
            norm_gains.T,
            jnp.zeros((shard, EXTRA - EXPERTS - 2), jnp.float32),
        ],
        axis=1,
    ).astype(brain_floating)
    pack = lax.all_gather(pack_own, fsdp, axis=0, tiled=True)
    at = PROJECTED + MODEL_WIDTH + EXPERTS
    gains_value = pack[:, at : at + 2].astype(jnp.float32).T

    weights_own = split_by_owner(gateup_weight, down_weight)
    weights = lax.all_to_all(weights_own, "inner", 0, 0)
    if outer > 1:
        weights = lax.all_gather(weights, "outer", axis=0, tiled=True)

    position, alive_mask, allowed = layout(document_lengths[0], count_of_rows)
    cosine, sine = rope_tables(position)
    alive = alive_mask[:, None]
    bias = jnp.where(allowed, 0.0, masked_value)

    expert_row = jnp.arange(EXPERTS, dtype=jnp.int32)
    chosen = jnp.any(expert_choice[:, :, None] == expert_row[None, None, :], axis=1)
    mask = jnp.concatenate(
        [
            chosen.astype(brain_floating),
            jnp.zeros((count_of_rows, EXTRA - EXPERTS), brain_floating),
        ],
        axis=1,
    )
    branch = (alive * cotangent.astype(jnp.float32)).astype(brain_floating)
    branch_pack = jnp.concatenate([branch, mask], axis=1)
    part_rows = count_of_rows // CHUNKS

    def gathered(values, c):
        return lax.all_gather(
            values[c * part_rows : (c + 1) * part_rows], "inner", axis=0, tiled=True
        )

    branch_all = lax.all_gather(branch_pack, "inner", axis=0, tiled=True).reshape(
        GROUP, CHUNKS, part_rows, MODEL_WIDTH + EXTRA
    )

    normed, qkv, mixed, totals, middle, normed_two = run_front(
        tokens_in, pack, gains_value, alive, bias, cosine, sine, weights_own
    )

    x_all, ga_all, dgu_all, dx = ([], [], [], None)
    for c in range(CHUNKS):
        x_part = gathered(normed_two, c)
        ga, dgu, dx = run_experts(
            me, c, x_part, branch_all, weights, pack, () if dx is None else (dx,)
        )
        x_all.append(x_part)
        ga_all.append(ga)
        dgu_all.append(dgu)
    dx_own = lax.psum_scatter(
        dx.reshape(GROUP * count_of_rows, MODEL_WIDTH + EXTRA),
        "inner",
        scatter_dimension=0,
        tiled=True,
    )

    def to_owner(parts):
        if outer > 1:
            parts = lax.psum_scatter(parts, "outer", scatter_dimension=0, tiled=True)
        return lax.all_to_all(parts, "inner", 0, 0)

    def swapped(values):
        return lax.ppermute(values, "replica", [(0, 1), (1, 0), (2, 3), (3, 2)])

    def across(values):
        return lax.ppermute(values, "replica", [(1, 2), (2, 1)])

    def grads_of(local, sides, wait, cost):
        return run_grads(local, sides, shard, x_all, branch_all, ga_all, dgu_all, wait, cost)

    chunks = [(local, side) for local in range(LOCAL) for side in (2, 0, 1)]
    last = len(chunks)
    root = MODEL_WIDTH ** (-0.5)
    states = (
        (gateup_weight, gateup_first, gateup_second),
        (down_weight, down_first, down_second),
    )
    renewed = [None, None]
    by_pairs, totals_of, ends, edges = ({}, {}, {}, {})

    def adam_of(k, wait, cost):
        local, side = chunks[k]
        which = side // 2
        *renewed[which], done = adam_part(
            place, totals_of[k], ends[k], states[which], local, side,
            (F // 16) ** (-0.5) if which else root, renewed[which], wait, cost,
        )
        return done

    first = grads_of(0, (2,), dgu_all[-1], 1)
    token = first
    mine = {0: (to_owner(first), 0)}
    for k in range(-1, last + 3):
        own, pair, following, waits = (None, None, None, [])
        if k in edges:
            arrived = swapped(edges[k])
            ends[k - 2] = arrived
            if k <= last:
                own = (mine[k], arrived)
            else:
                waits.append(arrived)
        if k - 1 in by_pairs:
            pair = (by_pairs[k - 1], across(by_pairs[k - 1]))

        if k == -1:
            second = grads_of(0, (0, 1), token, 1)
            done = second
        elif k == 0:
            got = to_owner(after(second, token))
            mine[1], mine[2] = ((got, 0), (got, 1))
            third = grads_of(1, (2,), token, 3)
            done = third
        elif k == 1:
            mine[3] = (to_owner(after(third, token)), 0)
            fourth = grads_of(1, (0, 1), token, 3)
            done = fourth
        elif k == 2:
            got = to_owner(after(fourth, token))
            mine[4], mine[5] = ((got, 0), (got, 1))
            d_middle, d_mixed, second_grads = run_middle(
                dx_own, normed_two, middle, cotangent, mask, alive, gains_value, pack, mixed, token
            )
            done = d_mixed
        elif k == 3:
            rest_grads, input_gradient = run_back(
                d_mixed, qkv, totals, bias, cosine, sine, normed, tokens_in, d_middle, gains_value,
                second_grads, pack, token, token,
            )
            rest_own = lax.psum_scatter(rest_grads, fsdp, scatter_dimension=0, tiled=True)
            rest_own = jnp.pad(rest_own, ((0, 0), (0, GROUP * F - rest_own.shape[1])))
            rest_own = rest_own.reshape(shard, GROUP, F).swapaxes(0, 1)
            mine[last] = (rest_own.reshape(GROUP, 1, shard, F), 0)
            done = input_gradient
        elif k == 4:
            mixture = run_mix(ga_all, weights, part_rows, token, 60)
            mixture_own = lax.psum_scatter(
                mixture.reshape(GROUP * count_of_rows, MODEL_WIDTH),
                "inner",
                scatter_dimension=0,
                tiled=True,
            )
            done = mixture
        elif k == 5:
            done = adam_of(1, adam_of(0, token, 60), 1)
        elif k == 6:
            done = adam_of(3, adam_of(2, token, 60), 1)
        elif k - 3 < len(chunks):
            done = adam_of(k - 3, token, 60)
        waits.append(done)

        if k + 1 <= last:
            following = mine[k + 1]
        if k == last + 2:
            continue
        results = list(run_round(place, own, pair, following, waits))
        token = results[0]
        if own:
            by_pairs[k] = results.pop(0)
        if pair:
            totals_of[k - 1] = results.pop(0)
        edges[k + 1] = results.pop(0)

    block_output = (middle + alive * mixture_own.astype(jnp.float32)).astype(brain_floating)

    rest_states = (
        (norm_gains, gains_first, gains_second),
        (query_weight, query_first, query_second),
        (keyvalue_weight, keyvalue_first_moment, keyvalue_second_moment),
        (output_weight, output_first, output_second),
        (router_weight, router_first, router_second),
    )
    rates = (
        (gain_rate, 0.0),
        (root, decay_rate),
        (root, decay_rate),
        ((WIDTH // 16) ** (-0.5), decay_rate),
        ((4 * MODEL_WIDTH) ** (-0.5), decay_rate),
    )
    updated = adam_rest(place, totals_of[last], ends[last], rest_states, rates)
    return (block_output, input_gradient) + tuple(updated) + tuple(renewed[0]) + tuple(renewed[1])


def solution(mesh):
    replicas, shards = (mesh.shape["replica"], mesh.shape["fsdp"])
    outer = shards // GROUP
    split = Mesh(mesh.devices.reshape(replicas, outer, GROUP), ("replica",) + fsdp)
    rows = P(("replica",) + fsdp, None)
    by_first = P(fsdp, None)
    by_second = P(None, fsdp)
    by_middle = P(None, fsdp, None)
    by_third = P(None, None, fsdp, None)
    by_last = P(None, None, fsdp)
    weights = (by_second, by_first, by_middle, by_first, by_first, by_third, by_last)
    states = tuple(spec for spec in weights for _ in range(3))
    return jax.shard_map(
        functools.partial(body, (replicas, outer)),
        mesh=split,
        in_specs=(rows,) * 4 + states,
        out_specs=(rows,) * 2 + states,
        check_vma=False,
    )
```

```python
import functools
import math

import jax
import jax.numpy as jnp
from jax import lax
from jax.experimental import pallas as pl
from jax.experimental.pallas import tpu as pltpu
from jax.sharding import Mesh
from jax.sharding import PartitionSpec as P

MODEL_WIDTH = 1024
QUERY_HEADS = 16
KEYVALUE_HEADS = 8
HEAD_SIZE = 64
F = 512
TOPK = 8
EXPERTS = 16
ADAM_STEP = 5
GROUP = 8
LOCAL = EXPERTS // GROUP
EXTRA = 128
CHUNKS = 2
TILE = 512
SPAN = 256
LANES = 128
WIDTH = QUERY_HEADS * HEAD_SIZE
KV_WIDTH = KEYVALUE_HEADS * HEAD_SIZE
PROJECTED = WIDTH + 2 * KV_WIDTH
SCORE_SCALE = HEAD_SIZE ** (-0.5)
ROUTER_BLOCK = (PROJECTED + MODEL_WIDTH) // EXTRA


norm_eps = 1e-06
rope_base = 10000.0
beta_one = 0.9
beta_two = 0.95
adam_eps = 1e-08
decay_rate = 0.1
gain_rate = 0.25
masked_value = -1e30
brain_floating = jnp.bfloat16


def layout(lengths, count_of_rows):
    document_ends = jnp.cumsum(lengths)
    row_index = jnp.arange(count_of_rows, dtype=jnp.int32)
    passed = row_index[:, None] >= document_ends[None, :]
    segment = jnp.sum(passed.astype(jnp.int32), axis=1)
    start_row = jnp.sum(jnp.where(passed, lengths[None, :], 0), axis=1)
    position = (row_index - start_row).astype(jnp.float32)
    alive_mask = (segment < lengths.shape[0]).astype(jnp.float32)
    allowed = (segment[:, None] == segment[None, :]) & (row_index[None, :] <= row_index[:, None])
    return (position, alive_mask, allowed)


def rope_tables(position):
    half_width = HEAD_SIZE // 2
    exponents = jnp.arange(half_width, dtype=jnp.float32) * (2.0 / HEAD_SIZE)
    inverse = jnp.exp(exponents * -math.log(rope_base))
    angles = position[:, None] * inverse[None, :]
    cosine, sine = (jnp.cos(angles), jnp.sin(angles))
    return (
        jnp.concatenate([cosine] * 4, axis=1),
        jnp.concatenate([-sine, sine, -sine, sine], axis=1),
    )


def product(left, right):
    return jnp.dot(left, right, preferred_element_type=jnp.float32)


def times_transposed(left, right):
    return lax.dot_general(
        left, right, (((1,), (1,)), ((), ())), preferred_element_type=jnp.float32
    )


def transposed_times(left, right):
    return lax.dot_general(
        left, right, (((0,), (0,)), ((), ())), preferred_element_type=jnp.float32
    )


def normalize(values):
    inverse = lax.rsqrt(jnp.mean(values * values, axis=-1, keepdims=True) + norm_eps)
    return (values * inverse, inverse)


def norm_back(upstream, scaled_rows, inverse, gain_row):
    weighted = upstream * gain_row
    inner = jnp.mean(weighted * scaled_rows, axis=-1, keepdims=True)
    return inverse * (weighted - scaled_rows * inner)


def column_sums(values):
    ones = jnp.ones((values.shape[0], LANES), brain_floating)
    high = values.astype(brain_floating)
    low = (values - high.astype(jnp.float32)).astype(brain_floating)
    return transposed_times(high, ones) + transposed_times(low, ones)


def lanes_of(shape):
    return lax.broadcasted_iota(jnp.int32, shape, 1)


def rotate(values, cosine, sine):
    half = HEAD_SIZE // 2
    front = lax.rem(lanes_of(values.shape), HEAD_SIZE) < half
    swapped = jnp.where(
        front, pltpu.roll(values, LANES - half, 1), pltpu.roll(values, half, 1)
    )
    return values * cosine + swapped * sine


def both_halves(values, which):
    turned = pltpu.roll(values, HEAD_SIZE, 1)
    first = lanes_of(values.shape) < HEAD_SIZE
    return jnp.where(first == (which == 0), values, turned)


def only_half(values, which):
    first = lanes_of(values.shape) < HEAD_SIZE
    return jnp.where(first == (which == 0), values, 0.0)


def gates_of(rows, router, mask):
    logits = product(rows, router)
    peak = jnp.max(jnp.where(mask, logits, masked_value), axis=1, keepdims=True)
    weights = jnp.where(mask, jnp.exp(logits - peak), 0.0)
    return weights / jnp.sum(weights, axis=1, keepdims=True)


def adamw_step(weight, moment_old, square_old, gradient, step_rate, shrink):
    moment = beta_one * moment_old + (1.0 - beta_one) * gradient
    square = beta_two * square_old + (1.0 - beta_two) * gradient * gradient
    moment_hat = moment / (1.0 - beta_one**ADAM_STEP)
    square_hat = square / (1.0 - beta_two**ADAM_STEP)
    renewed = weight - step_rate * (
        moment_hat / (jnp.sqrt(square_hat) + adam_eps) + shrink * weight
    )
    return (moment, square, renewed)


MIB = 1024 * 1024
ANYWHERE = pl.BlockSpec(memory_space=pl.ANY)


def takes(microseconds):
    return pl.CostEstimate(
        flops=int(microseconds * 1e9), bytes_accessed=int(microseconds * 3.6e6), transcendentals=0
    )


def whole(shape):
    return pl.BlockSpec(shape, lambda *_: (0,) * len(shape), pipeline_mode=pl.Buffered(1))


def part(shape, place):
    return pl.BlockSpec(shape, lambda *_: place, pipeline_mode=pl.Buffered(1))


def out(shape, dtype):
    return jax.ShapeDtypeStruct(shape, dtype)


def split_kernel(odd_ref, gateup_ref, down_ref, out_ref):
    for k in range(2):
        out_ref[k, 0] = gateup_ref[k, 0].astype(brain_floating)
        out_ref[k, 1] = gateup_ref[k, 1].astype(brain_floating)
        out_ref[k, 2] = down_ref[k].T.astype(brain_floating)


def split_by_owner(odd, gateup, down):
    shard = gateup.shape[2]
    steps = GROUP // 2
    return pl.pallas_call(
        split_kernel,
        grid_spec=pltpu.PrefetchScalarGridSpec(
            num_scalar_prefetch=1,
            grid=(steps,),
            in_specs=[
                pl.BlockSpec((2, 2, shard, F), lambda e, odd: (e + steps * odd[0], 0, 0, 0)),
                pl.BlockSpec((2, F, shard), lambda e, odd: (e + steps * odd[0], 0, 0)),
            ],
            out_specs=pl.BlockSpec((2, 3, shard, F), lambda e, odd: (e, 0, 0, 0)),
        ),
        out_shape=out((GROUP, 3, shard, F), brain_floating),
        name="split",
    )(odd, gateup, down)


def front_kernel(
    x_ref, pack_ref, gains_ref, alive_ref, bias_ref, cos_ref, sin_ref, wait_ref, normed_ref, qkv_ref, mixed_ref, totals_ref, middle_ref, normed_two_ref, linear_ref,
):
    rows = x_ref.shape[0]
    scaled, _ = normalize(x_ref[...].astype(jnp.float32))
    normed = (scaled * gains_ref[0:1, :]).astype(brain_floating)
    normed_ref[...] = normed
    linear_ref[...] = product(normed, pack_ref[:, :PROJECTED])
    cosine, sine = (cos_ref[...], sin_ref[...])
    for at in range(0, WIDTH + KV_WIDTH, LANES):
        qkv_ref[:, at : at + LANES] = rotate(
            linear_ref[:, at : at + LANES], cosine, sine
        ).astype(brain_floating)
    qkv_ref[:, WIDTH + KV_WIDTH :] = linear_ref[:, WIDTH + KV_WIDTH :].astype(brain_floating)
    totals_ref[...] = jnp.zeros_like(totals_ref)

    @pl.loop(0, KEYVALUE_HEADS // 2)
    def _(pair):
        at = pl.multiple_of(pair * LANES, LANES)
        keys = qkv_ref[:, pl.ds(WIDTH + at, LANES)].astype(jnp.float32)
        values = qkv_ref[:, pl.ds(WIDTH + KV_WIDTH + at, LANES)].astype(jnp.float32)
        for a in range(2):
            head_keys = both_halves(keys, a).astype(brain_floating)
            head_values = both_halves(values, a)
            place = pl.multiple_of((2 * pair + a) * LANES, LANES)
            queries = qkv_ref[:, pl.ds(place, LANES)].astype(jnp.float32)
            for start in range(0, rows, SPAN):
                seen = min(start + SPAN, rows)
                mixed = jnp.zeros((SPAN, LANES), jnp.float32)
                for j in range(2):
                    head = 2 * (2 * pair + a) + j
                    query = only_half(queries[start : start + SPAN], j).astype(brain_floating)
                    scores = (
                        times_transposed(query, head_keys[:seen]) * SCORE_SCALE
                        + bias_ref[start : start + SPAN, :seen]
                    )
                    peak = jnp.max(scores, axis=1, keepdims=True)
                    weights = jnp.exp(scores - peak)
                    total = jnp.sum(weights, axis=1, keepdims=True)
                    probs = (weights * (1.0 / total)).astype(brain_floating)
                    mixed += product(probs, only_half(head_values[:seen], j).astype(brain_floating))
                    held = totals_ref[start : start + SPAN, :]
                    totals_ref[start : start + SPAN, :] = jnp.where(
                        lanes_of(held.shape) == head, peak + jnp.log(total), held
                    )
                mixed_ref[start : start + SPAN, pl.ds(place, LANES)] = mixed.astype(brain_floating)

    attended = product(mixed_ref[...], pack_ref[:, PROJECTED : PROJECTED + MODEL_WIDTH])
    middle = x_ref[...].astype(jnp.float32) + alive_ref[...] * attended
    middle_ref[...] = middle
    scaled_two, _ = normalize(middle)
    normed_two_ref[...] = (scaled_two * gains_ref[1:2, :]).astype(brain_floating)


def run_front(x, pack, gains, alive, bias, cosine, sine, wait):
    rows = x.shape[0]
    return pl.pallas_call(
        front_kernel,
        in_specs=[pl.BlockSpec(memory_space=pltpu.VMEM)] * 7 + [ANYWHERE],
        out_shape=[
            out((rows, MODEL_WIDTH), brain_floating),
            out((rows, PROJECTED), brain_floating),
            out((rows, WIDTH), brain_floating),
            out((rows, LANES), jnp.float32),
            out((rows, MODEL_WIDTH), jnp.float32),
            out((rows, MODEL_WIDTH), brain_floating),
        ],
        scratch_shapes=[pltpu.VMEM((rows, PROJECTED), jnp.float32)],
        compiler_params=pltpu.CompilerParams(vmem_limit_bytes=52 * MIB),
        name="front",
    )(x, pack, gains, alive, bias, cosine, sine, wait)


def middle_kernel(
    dx_ref, normed_two_ref, middle_ref, cot_ref, mask_ref, alive_ref, gains_ref, router_ref,
    output_ref, mixed_ref, wait_ref, d_middle_ref, d_mixed_ref, grads_ref,
):
    dx = dx_ref[...].astype(jnp.float32)
    normed_two = normed_two_ref[...]
    mask = mask_ref[...].astype(jnp.float32) > 0.5
    gates = gates_of(normed_two, router_ref[...], mask)
    extra = dx[:, MODEL_WIDTH:]
    d_gates = extra + pltpu.roll(extra, LANES - EXPERTS, 1)
    d_logits = (
        gates * (d_gates - jnp.sum(gates * d_gates, axis=1, keepdims=True))
    ).astype(brain_floating)
    d_normed = dx[:, :MODEL_WIDTH] + times_transposed(d_logits, router_ref[...])
    scaled, inverse = normalize(middle_ref[...])
    d_middle = cot_ref[...].astype(jnp.float32) + norm_back(
        d_normed, scaled, inverse, gains_ref[1:2, :]
    )
    d_middle_ref[...] = d_middle
    d_attended = (alive_ref[...] * d_middle).astype(brain_floating)
    grads_ref[:, :MODEL_WIDTH] = transposed_times(mixed_ref[...], d_attended).astype(brain_floating)
    small = transposed_times(normed_two, d_logits)
    small = jnp.where(lanes_of(small.shape) == EXPERTS + 1, column_sums(d_normed * scaled), small)
    grads_ref[:, MODEL_WIDTH:] = small.astype(brain_floating)
    d_mixed_ref[...] = times_transposed(d_attended, output_ref[...]).astype(brain_floating)


def run_middle(dx, normed_two, middle, cot, mask, alive, gains, pack, mixed, wait):
    rows = middle.shape[0]
    full = [whole(v.shape) for v in (dx, normed_two, middle, cot, mask, alive, gains)]
    return pl.pallas_call(
        middle_kernel,
        grid=(1,),
        in_specs=full
        + [
            part((MODEL_WIDTH, EXTRA), (0, ROUTER_BLOCK)),
            part((WIDTH, MODEL_WIDTH), (0, PROJECTED // MODEL_WIDTH)),
            whole(mixed.shape),
            ANYWHERE,
        ],
        out_specs=[
            whole((rows, MODEL_WIDTH)),
            whole((rows, WIDTH)),
            whole((MODEL_WIDTH, MODEL_WIDTH + EXTRA)),
        ],
        out_shape=[
            out((rows, MODEL_WIDTH), jnp.float32),
            out((rows, WIDTH), brain_floating),
            out((MODEL_WIDTH, MODEL_WIDTH + EXTRA), brain_floating),
        ],
        compiler_params=pltpu.CompilerParams(vmem_limit_bytes=52 * MIB),
        cost_estimate=takes(30),
        name="middle_back",
    )(dx, normed_two, middle, cot, mask, alive, gains, pack, pack, mixed, wait)


def back_kernel(
    d_mixed_ref, qkv_ref, totals_ref, bias_ref, cos_ref, sin_ref, normed_ref, x_ref, d_middle_ref,
    gains_ref, other_ref, pack_ref, wait_ref, also_ref, grads_ref, d_input_ref, d_linear_ref, d_keys_ref, d_values_ref,
):
    rows = x_ref.shape[0]
    cosine, sine = (cos_ref[...], -sin_ref[...])

    @pl.loop(0, KEYVALUE_HEADS // 2)
    def _(pair):
        at = pl.multiple_of(pair * LANES, LANES)
        keys = qkv_ref[:, pl.ds(WIDTH + at, LANES)].astype(jnp.float32)
        values = qkv_ref[:, pl.ds(WIDTH + KV_WIDTH + at, LANES)].astype(jnp.float32)
        pair_keys = jnp.zeros((rows, LANES), jnp.float32)
        pair_values = jnp.zeros((rows, LANES), jnp.float32)
        for a in range(2):
            both_keys = both_halves(keys, a)
            head_keys = both_keys.astype(brain_floating)
            head_values = both_halves(values, a).astype(brain_floating)
            place = pl.multiple_of((2 * pair + a) * LANES, LANES)
            queries = qkv_ref[:, pl.ds(place, LANES)].astype(jnp.float32)
            d_outs = d_mixed_ref[:, pl.ds(place, LANES)].astype(jnp.float32)
            d_keys_ref[...] = jnp.zeros_like(d_keys_ref)
            d_values_ref[...] = jnp.zeros_like(d_values_ref)
            for start in range(0, rows, SPAN):
                seen = min(start + SPAN, rows)
                d_query = jnp.zeros((SPAN, LANES), jnp.float32)
                for j in range(2):
                    head = 2 * (2 * pair + a) + j
                    query = only_half(queries[start : start + SPAN], j).astype(brain_floating)
                    d_out = only_half(d_outs[start : start + SPAN], j).astype(brain_floating)
                    held = totals_ref[start : start + SPAN, :]
                    total = jnp.sum(
                        jnp.where(lanes_of(held.shape) == head, held, 0.0), axis=1, keepdims=True
                    )
                    scores = (
                        times_transposed(query, head_keys[:seen]) * SCORE_SCALE
                        + bias_ref[start : start + SPAN, :seen]
                    )
                    probs = jnp.exp(scores - total)
                    d_probs = times_transposed(d_out, head_values[:seen])
                    inner = jnp.sum(probs * d_probs, axis=1, keepdims=True)
                    d_scores = (probs * (d_probs - inner)).astype(brain_floating)
                    d_query += product(
                        d_scores, only_half(both_keys[:seen], j).astype(brain_floating)
                    )
                    d_keys_ref[:seen, :] += transposed_times(d_scores, query)
                    d_values_ref[:seen, :] += transposed_times(probs.astype(brain_floating), d_out)
                d_linear_ref[start : start + SPAN, pl.ds(place, LANES)] = rotate(
                    d_query * SCORE_SCALE,
                    cosine[start : start + SPAN],
                    sine[start : start + SPAN],
                ).astype(brain_floating)
            d_keys = d_keys_ref[...]
            d_values = d_values_ref[...]
            pair_keys += only_half(d_keys + pltpu.roll(d_keys, HEAD_SIZE, 1), a)
            pair_values += only_half(d_values + pltpu.roll(d_values, HEAD_SIZE, 1), a)
        d_linear_ref[:, pl.ds(WIDTH + at, LANES)] = rotate(
            pair_keys * SCORE_SCALE, cosine, sine
        ).astype(brain_floating)
        d_linear_ref[:, pl.ds(WIDTH + KV_WIDTH + at, LANES)] = pair_values.astype(brain_floating)

    normed = normed_ref[...]
    for at in range(0, PROJECTED, 512):
        grads_ref[:, at : at + 512] = transposed_times(
            normed, d_linear_ref[:, at : at + 512]
        ).astype(brain_floating)
    d_normed = times_transposed(d_linear_ref[...], pack_ref[...])
    scaled, inverse = normalize(x_ref[...].astype(jnp.float32))
    sums = column_sums(d_normed * scaled)
    grads_ref[:, PROJECTED : PROJECTED + MODEL_WIDTH] = other_ref[:, :MODEL_WIDTH]
    small = other_ref[:, MODEL_WIDTH:].astype(jnp.float32)
    grads_ref[:, PROJECTED + MODEL_WIDTH :] = jnp.where(
        lanes_of(sums.shape) == EXPERTS, sums, small
    ).astype(brain_floating)
    d_input_ref[...] = d_middle_ref[...] + norm_back(d_normed, scaled, inverse, gains_ref[0:1, :])


def run_back(
    d_mixed, qkv, totals, bias, cosine, sine, normed, x, d_middle, gains, other, pack, wait, also
):
    rows = x.shape[0]
    held = (d_mixed, qkv, totals, bias, cosine, sine, normed, x, d_middle, gains, other)
    width = PROJECTED + other.shape[1]
    return pl.pallas_call(
        back_kernel,
        grid=(1,),
        in_specs=[whole(v.shape) for v in held]
        + [part((MODEL_WIDTH, PROJECTED), (0, 0)), ANYWHERE, ANYWHERE],
        out_specs=[whole((MODEL_WIDTH, width)), whole((rows, MODEL_WIDTH))],
        out_shape=[
            out((MODEL_WIDTH, width), brain_floating),
            out((rows, MODEL_WIDTH), jnp.float32),
        ],
        scratch_shapes=[
            pltpu.VMEM((rows, PROJECTED), brain_floating),
            pltpu.VMEM((rows, LANES), jnp.float32),
            pltpu.VMEM((rows, LANES), jnp.float32),
        ],
        compiler_params=pltpu.CompilerParams(vmem_limit_bytes=52 * MIB),
        cost_estimate=takes(30),
        name="attention_back",
    )(*held, pack, wait, also)


def expert_kernel(me_ref, x_ref, b_ref, w_one_ref, w_two_ref, router_ref, *refs):
    ga_ref, dgu_ref, dx_ref = refs[-3:]
    x = x_ref[...]
    branch = b_ref[:, 0, :, :MODEL_WIDTH].reshape(x.shape)
    mask = b_ref[:, 0, :, MODEL_WIDTH:].reshape(x.shape[0], EXTRA).astype(jnp.float32) > 0.5
    gates = gates_of(x, router_ref[...], mask)
    lane = lanes_of(gates.shape)
    d_gates = jnp.zeros_like(gates)
    dx = jnp.zeros((x.shape[0], MODEL_WIDTH), jnp.float32)
    for local in range(LOCAL):
        expert = me_ref[0] + GROUP * lax.rem(me_ref[1] + local, LOCAL)
        w_ref = (w_one_ref, w_two_ref)[local]
        gate_weight, up_weight, down_weight = (
            w_ref[:, p].reshape(MODEL_WIDTH, F) for p in range(3)
        )
        gate = jnp.sum(jnp.where(lane == expert, gates, 0.0), axis=1, keepdims=True)
        gate_linear = product(x, gate_weight)
        up_linear = product(x, up_weight)
        back = product(branch, down_weight)
        sig = jax.nn.sigmoid(gate_linear)
        silu = gate_linear * sig
        act = silu * up_linear
        ga_ref[:, local * F : (local + 1) * F] = (gate * act).astype(brain_floating)
        d_gate = jnp.sum(act * back, axis=1, keepdims=True)
        high = d_gate.astype(brain_floating).astype(jnp.float32)
        d_gates += jnp.where(lane == expert, high, 0.0)
        d_gates += jnp.where(lane == expert + EXPERTS, d_gate - high, 0.0)
        d_act = gate * back
        d_gl = (d_act * up_linear * (sig + silu * (1.0 - sig))).astype(brain_floating)
        d_ul = (d_act * silu).astype(brain_floating)
        dgu_ref[:, 2 * local * F : (2 * local + 1) * F] = d_gl
        dgu_ref[:, (2 * local + 1) * F : (2 * local + 2) * F] = d_ul
        dx += times_transposed(d_gl, gate_weight) + times_transposed(d_ul, up_weight)
    blocks, _, part_rows, _ = dx_ref.shape
    dx_ref[:, 0, :, :MODEL_WIDTH] = dx.astype(brain_floating).reshape(
        blocks, part_rows, MODEL_WIDTH
    )
    dx_ref[:, 0, :, MODEL_WIDTH:] = d_gates.astype(brain_floating).reshape(
        blocks, part_rows, EXTRA
    )


def run_experts(me, c, x, b, weights, pack, before):
    rows = x.shape[0]
    part_rows = b.shape[2]
    tile = 2 * part_rows
    wide = MODEL_WIDTH + EXTRA

    def rowed(width):
        return pl.BlockSpec((tile, width), lambda i, me_ref: (i, 0))

    return pl.pallas_call(
        expert_kernel,
        grid_spec=pltpu.PrefetchScalarGridSpec(
            num_scalar_prefetch=1,
            grid=(rows // tile,),
            in_specs=[
                rowed(MODEL_WIDTH),
                pl.BlockSpec((2, 1, part_rows, wide), lambda i, me_ref: (i, c, 0, 0)),
                whole(weights[0].shape),
                whole(weights[1].shape),
                part((MODEL_WIDTH, EXTRA), (0, ROUTER_BLOCK)),
            ]
            + [ANYWHERE] * len(before),
            out_specs=[
                rowed(LOCAL * F),
                rowed(2 * LOCAL * F),
                pl.BlockSpec((2, 1, part_rows, wide), lambda i, me_ref: (i, c, 0, 0)),
            ],
        ),
        out_shape=[
            out((rows, LOCAL * F), brain_floating),
            out((rows, 2 * LOCAL * F), brain_floating),
            out((rows // part_rows, CHUNKS, part_rows, wide), brain_floating),
        ],
        input_output_aliases={6 + i: 2 for i in range(len(before))},
        compiler_params=pltpu.CompilerParams(vmem_limit_bytes=56 * MIB),
        name="experts",
    )(me, x, b, *weights, pack, *before)


def chunked_specs(steps, shape, place):
    def index(c):
        return lambda i, *scalars: place(jnp.clip(i - c * steps, 0, steps - 1), c, *scalars)

    return [pl.BlockSpec(shape, index(c)) for c in range(CHUNKS)]


def grads_kernel(steps, sides, me_ref, *refs):
    count = len(sides)
    ins, out_ref, sums = (refs[: CHUNKS * 2 * count], refs[-count - 1], refs[-count:])
    blocks, _, shard, _ = out_ref.shape
    i = pl.program_id(0)

    @pl.when(i == 0)
    def _():
        for total in sums:
            total[...] = jnp.zeros_like(total)

    for c in range(CHUNKS):

        @pl.when(i // steps == c)
        def _():
            for k in range(count):
                left, right = (ins[2 * (k * CHUNKS + c)], ins[2 * (k * CHUNKS + c) + 1])
                sums[k][...] += transposed_times(
                    left[...].reshape(right.shape[0], MODEL_WIDTH), right[...]
                )

    @pl.when(i == CHUNKS * steps - 1)
    def _():
        for k, total in enumerate(sums):
            out_ref[:, k] = total[...].astype(brain_floating).reshape(blocks, shard, F)


def run_grads(me, local, sides, shard, xs, b, gas, dgus, wait, cost):
    blocks = MODEL_WIDTH // shard
    rows, part_rows = (xs[0].shape[0], b.shape[2])
    tile = 2 * part_rows
    steps = rows // tile
    specs, arrays = ([], [])
    for side in sides:
        if side == 2:
            left = chunked_specs(
                steps, (2, 1, part_rows, MODEL_WIDTH), lambda i, c, me: (i, c, 0, 0)
            )
            right = chunked_specs(
                steps, (tile, F), lambda i, c, me: (i, lax.rem(me[1] + local, LOCAL))
            )
        else:
            left = chunked_specs(steps, (tile, MODEL_WIDTH), lambda i, c, me: (i, 0))
            right = chunked_specs(
                steps,
                (tile, F),
                lambda i, c, me, side=side: (i, 2 * lax.rem(me[1] + local, LOCAL) + side),
            )
        for c in range(CHUNKS):
            specs += [left[c], right[c]]
            arrays += [b, gas[c]] if side == 2 else [xs[c], dgus[c]]
    return pl.pallas_call(
        functools.partial(grads_kernel, steps, sides),
        grid_spec=pltpu.PrefetchScalarGridSpec(
            num_scalar_prefetch=1,
            grid=(CHUNKS * steps,),
            in_specs=specs + [ANYWHERE],
            out_specs=whole((blocks, len(sides), shard, F)),
            scratch_shapes=[pltpu.VMEM((MODEL_WIDTH, F), jnp.float32)] * len(sides),
        ),
        out_shape=out((blocks, len(sides), shard, F), brain_floating),
        compiler_params=pltpu.CompilerParams(vmem_limit_bytes=52 * MIB),
        cost_estimate=takes(cost),
        name="grads",
    )(me, *arrays, wait)


def mix_kernel(steps, *refs):
    gas, w_refs, out_ref = (refs[:CHUNKS], refs[CHUNKS : CHUNKS + LOCAL], refs[-1])
    for c in range(CHUNKS):

        @pl.when(pl.program_id(0) // steps == c)
        def _():
            total = jnp.zeros((gas[c].shape[0], MODEL_WIDTH), jnp.float32)
            for local in range(LOCAL):
                total += times_transposed(
                    gas[c][:, local * F : (local + 1) * F],
                    w_refs[local][:, 0].reshape(MODEL_WIDTH, F),
                )
            out_ref[...] = total.astype(brain_floating).reshape(out_ref.shape)


def run_mix(gas, weights, part_rows, wait, cost):
    rows = gas[0].shape[0]
    tile = 2 * part_rows
    steps = rows // tile
    blocks, _, shard, _ = weights[0].shape
    return pl.pallas_call(
        functools.partial(mix_kernel, steps),
        grid=(CHUNKS * steps,),
        in_specs=chunked_specs(steps, (tile, LOCAL * F), lambda i, c: (i, 0))
        + [part((blocks, 1, shard, F), (0, 2, 0, 0))] * LOCAL
        + [ANYWHERE],
        out_specs=pl.BlockSpec(
            (2, 1, part_rows, MODEL_WIDTH), lambda i: (lax.rem(i, steps), i // steps, 0, 0)
        ),
        out_shape=out((rows // part_rows, CHUNKS, part_rows, MODEL_WIDTH), brain_floating),
        compiler_params=pltpu.CompilerParams(vmem_limit_bytes=52 * MIB),
        cost_estimate=takes(cost),
        name="mixture",
    )(*gas, *weights, wait)


def at_inner(place_ref):
    return (place_ref[0] == 1) | (place_ref[0] == 2)


def round_kernel(kinds, waits, place_ref, *refs):
    has_own, has_pair, has_next = kinds
    refs = list(refs)

    def take(count):
        taken, refs[:count] = (refs[:count], [])
        return [ref[...].astype(jnp.float32) for ref in taken]

    own = take(2) if has_own else None
    pair = take(2) if has_pair else None
    following = take(1) if has_next else None
    outs = refs[waits:]
    edge = None
    if has_next:
        edge = following[0].reshape(outs[-1].shape)
    if has_own:
        outs.pop(0)[...] = (own[0].reshape(own[1].shape) + own[1]).astype(brain_floating)
    if has_pair:
        total = pair[0] + pair[1]
        outs.pop(0)[...] = total.astype(brain_floating)
        edge = total if edge is None else jnp.where(at_inner(place_ref), total, edge)
    outs.pop(0)[...] = edge.astype(brain_floating)


def run_round(place, own, pair, following, waits):
    steps = GROUP // 2
    arrays, specs, count = ([], [], 0)

    def chunk_spec(source):
        values, at = source
        _, _, shard, width = values.shape
        return pl.BlockSpec((2, 1, shard, width), lambda i, _: (i, at, 0, 0))

    flat = None
    for source in (own[:1] if own else ()) + ((following,) if following else ()):
        flat = (GROUP,) + source[0].shape[2:]
    if pair:
        flat = pair[0].shape
    piece = pl.BlockSpec((2,) + flat[1:], lambda i, _: (i, 0, 0))
    if own:
        arrays += [own[0][0], own[1]]
        specs += [chunk_spec(own[0]), piece]
        count += 1
    if pair:
        arrays += list(pair)
        specs += [piece] * 2
        count += 1
    if following:
        arrays.append(following[0])
        specs.append(chunk_spec(following))
    count += 1
    return pl.pallas_call(
        functools.partial(
            round_kernel, (bool(own), bool(pair), bool(following)), len(waits)
        ),
        grid_spec=pltpu.PrefetchScalarGridSpec(
            num_scalar_prefetch=1,
            grid=(steps,),
            in_specs=specs + [ANYWHERE] * len(waits),
            out_specs=[piece] * count,
        ),
        out_shape=[out(flat, brain_floating)] * count,
        compiler_params=pltpu.CompilerParams(vmem_limit_bytes=40 * MIB),
        cost_estimate=takes(2),
        name="round",
    )(place, *arrays, *waits)


def after_kernel(values_ref, wait_ref, out_ref):
    del values_ref, wait_ref, out_ref


def after(values, wait):
    return pl.pallas_call(
        after_kernel,
        in_specs=[ANYWHERE] * 2,
        out_specs=ANYWHERE,
        out_shape=out(values.shape, values.dtype),
        input_output_aliases={0: 0},
        name="after",
    )(values, wait)


def adam_kernel(turned, rate, shrink, place_ref, t_ref, r_ref, w_ref, m_ref, v_ref, *rest):
    m_out, v_out, w_out, token_ref = rest[-4:]
    token_ref[...] = jnp.zeros_like(token_ref)
    inner = at_inner(place_ref)
    for k in range(t_ref.shape[0]):
        gradient = jnp.where(inner, t_ref[k].astype(jnp.float32), r_ref[k].astype(jnp.float32))
        if turned:
            at = (k,)
            gradient = gradient.T
        else:
            at = (k, 0)
        moment, square, renewed = adamw_step(
            w_ref[at], m_ref[at], v_ref[at], gradient, rate, shrink
        )
        m_out[at] = moment
        v_out[at] = square
        w_out[at] = renewed


def adam_part(place, total, ends, state, local, side, rate, before, wait, cost):
    weight, first, second = state
    turned = side == 2
    shard = total.shape[1]
    held = [] if before is None else list(before)
    if turned:
        spec = pl.BlockSpec((2, F, shard), lambda i, _: (i + local * (GROUP // 2), 0, 0))
    else:
        spec = pl.BlockSpec((2, 1, shard, F), lambda i, _: (i + local * (GROUP // 2), side, 0, 0))
    piece = pl.BlockSpec((2, shard, F), lambda i, _: (i, 0, 0))
    return pl.pallas_call(
        functools.partial(adam_kernel, turned, rate, decay_rate),
        grid_spec=pltpu.PrefetchScalarGridSpec(
            num_scalar_prefetch=1,
            grid=(GROUP // 2,),
            in_specs=[piece, piece, spec, spec, spec] + [ANYWHERE] * (len(held) + 1),
            out_specs=[spec] * 3 + [pl.BlockSpec((8, LANES), lambda i, _: (0, 0))],
        ),
        out_shape=[out(weight.shape, jnp.float32)] * 3 + [out((8, LANES), jnp.float32)],
        input_output_aliases={6 + i: i for i in range(len(held))},
        compiler_params=pltpu.CompilerParams(vmem_limit_bytes=60 * MIB),
        cost_estimate=takes(cost),
        name="adam",
    )(place, total, ends, weight, first, second, *held, wait)


def rest_kernel(rates, place_ref, t_ref, r_ref, *refs):
    inner = at_inner(place_ref)
    states, outs = (refs[:15], refs[15:])

    def gradient(j):
        return jnp.where(inner, t_ref[j].astype(jnp.float32), r_ref[j].astype(jnp.float32))

    def step(which, at, gradient):
        weight, first, second = states[3 * which : 3 * which + 3]
        rate, shrink = rates[which]
        results = adamw_step(weight[at], first[at], second[at], gradient, rate, shrink)
        for ref, value in zip(outs[3 * which : 3 * which + 3], results):
            ref[at] = value

    small = gradient(PROJECTED // F + 2)[:, :EXTRA]
    step(0, ..., small.T[EXPERTS : EXPERTS + 2, :])
    step(4, ..., small[:, :EXPERTS])
    for half in range(2):
        at = (slice(None), slice(half * F, half * F + F))
        step(1, at, gradient(half))
        step(2, half, gradient(2 + half))
        step(3, at, gradient(4 + half))


def adam_rest(place, total, ends, states, rates):
    flat = [v for state in states for v in state]
    in_vmem = pl.BlockSpec(memory_space=pltpu.VMEM)
    return pl.pallas_call(
        functools.partial(rest_kernel, rates),
        in_specs=[pl.BlockSpec(memory_space=pltpu.SMEM)] + [in_vmem] * (2 + len(flat)),
        out_shape=[out(v.shape, jnp.float32) for v in flat],
        compiler_params=pltpu.CompilerParams(vmem_limit_bytes=40 * MIB),
        name="adam_rest",
    )(place, total, ends, *flat)


fsdp = ("outer", "inner")


def body(
    sizes,
    tokens_in,
    cotangent,
    document_lengths,
    expert_choice,
    norm_gains,
    gains_first,
    gains_second,
    query_weight,
    query_first,
    query_second,
    keyvalue_weight,
    keyvalue_first_moment,
    keyvalue_second_moment,
    output_weight,
    output_first,
    output_second,
    router_weight,
    router_first,
    router_second,
    gateup_weight,
    gateup_first,
    gateup_second,
    down_weight,
    down_first,
    down_second,
):
    replicas, outer = sizes
    count_of_rows = tokens_in.shape[0]
    shard = query_weight.shape[0]
    place = lax.axis_index("replica").astype(jnp.int32).reshape(1)
    odd = lax.rem(place, LOCAL)
    me = jnp.concatenate([lax.axis_index("inner").astype(jnp.int32).reshape(1), odd])

    pack_own = jnp.concatenate(
        [
            query_weight,
            keyvalue_weight[0],
            keyvalue_weight[1],
            output_weight,
            router_weight,
            norm_gains.T,
            jnp.zeros((shard, EXTRA - EXPERTS - 2), jnp.float32),
        ],
        axis=1,
    ).astype(brain_floating)
    pack = lax.all_gather(pack_own, fsdp, axis=0, tiled=True)
    at = PROJECTED + MODEL_WIDTH + EXPERTS
    gains_value = pack[:, at : at + 2].astype(jnp.float32).T

    weights_own = lax.all_to_all(split_by_owner(odd, gateup_weight, down_weight), "inner", 0, 0)
    if outer > 1:
        weights_own = lax.all_gather(weights_own, "outer", axis=0, tiled=True)
    weights = (
        weights_own,
        lax.ppermute(weights_own, "replica", [(0, 1), (1, 0), (2, 3), (3, 2)]),
    )

    position, alive_mask, allowed = layout(document_lengths[0], count_of_rows)
    cosine, sine = rope_tables(position)
    alive = alive_mask[:, None]
    bias = jnp.where(allowed, 0.0, masked_value)

    expert_row = jnp.arange(EXPERTS, dtype=jnp.int32)
    chosen = jnp.any(expert_choice[:, :, None] == expert_row[None, None, :], axis=1)
    mask = jnp.concatenate(
        [
            chosen.astype(brain_floating),
            jnp.zeros((count_of_rows, EXTRA - EXPERTS), brain_floating),
        ],
        axis=1,
    )
    branch = (alive * cotangent.astype(jnp.float32)).astype(brain_floating)
    branch_pack = jnp.concatenate([branch, mask], axis=1)
    part_rows = count_of_rows // CHUNKS

    def gathered(values, c):
        return lax.all_gather(
            values[c * part_rows : (c + 1) * part_rows], "inner", axis=0, tiled=True
        )

    branch_all = lax.all_gather(branch_pack, "inner", axis=0, tiled=True).reshape(
        GROUP, CHUNKS, part_rows, MODEL_WIDTH + EXTRA
    )

    normed, qkv, mixed, totals, middle, normed_two = run_front(
        tokens_in, pack, gains_value, alive, bias, cosine, sine, weights_own
    )

    x_all, ga_all, dgu_all, dx = ([], [], [], None)
    for c in range(CHUNKS):
        x_part = gathered(normed_two, c)
        ga, dgu, dx = run_experts(
            me, c, x_part, branch_all, weights, pack, () if dx is None else (dx,)
        )
        x_all.append(x_part)
        ga_all.append(ga)
        dgu_all.append(dgu)
    dx_own = lax.psum_scatter(
        dx.reshape(GROUP * count_of_rows, MODEL_WIDTH + EXTRA),
        "inner",
        scatter_dimension=0,
        tiled=True,
    )

    def to_owner(parts):
        if outer > 1:
            parts = lax.psum_scatter(parts, "outer", scatter_dimension=0, tiled=True)
        return lax.all_to_all(parts, "inner", 0, 0)

    def swapped(values):
        return lax.ppermute(values, "replica", [(0, 1), (1, 0), (2, 3), (3, 2)])

    def across(values):
        return lax.ppermute(values, "replica", [(1, 2), (2, 1)])

    def grads_of(local, sides, wait, cost):
        return run_grads(me, local, sides, shard, x_all, branch_all, ga_all, dgu_all, wait, cost)

    chunks = [(local, side) for local in range(LOCAL) for side in (2, 0, 1)]
    last = len(chunks)
    root = MODEL_WIDTH ** (-0.5)
    states = (
        (gateup_weight, gateup_first, gateup_second),
        (down_weight, down_first, down_second),
    )
    renewed = [None, None]
    by_pairs, totals_of, ends, edges = ({}, {}, {}, {})

    def adam_of(k, wait, cost):
        local, side = chunks[k]
        which = side // 2
        *renewed[which], done = adam_part(
            place, totals_of[k], ends[k], states[which], local, side,
            (F // 16) ** (-0.5) if which else root, renewed[which], wait, cost,
        )
        return done

    first = grads_of(0, (2,), dgu_all[-1], 1)
    token = first
    mine = {0: (to_owner(first), 0)}
    for k in range(-1, last + 3):
        own, pair, following, waits = (None, None, None, [])
        if k in edges:
            arrived = swapped(edges[k])
            ends[k - 2] = arrived
            if k <= last:
                own = (mine[k], arrived)
            else:
                waits.append(arrived)
        if k - 1 in by_pairs:
            pair = (by_pairs[k - 1], across(by_pairs[k - 1]))

        if k == -1:
            second = grads_of(0, (0, 1), token, 1)
            done = second
        elif k == 0:
            got = to_owner(after(second, token))
            mine[1], mine[2] = ((got, 0), (got, 1))
            third = grads_of(1, (2,), token, 3)
            done = third
        elif k == 1:
            mine[3] = (to_owner(after(third, token)), 0)
            fourth = grads_of(1, (0, 1), token, 3)
            done = fourth
        elif k == 2:
            got = to_owner(after(fourth, token))
            mine[4], mine[5] = ((got, 0), (got, 1))
            d_middle, d_mixed, second_grads = run_middle(
                dx_own, normed_two, middle, cotangent, mask, alive, gains_value, pack, mixed, token
            )
            waits.append(got)
            done = d_mixed
        elif k == 3:
            rest_grads, input_gradient = run_back(
                d_mixed, qkv, totals, bias, cosine, sine, normed, tokens_in, d_middle, gains_value,
                second_grads, pack, token, token,
            )
            rest_own = lax.psum_scatter(rest_grads, fsdp, scatter_dimension=0, tiled=True)
            rest_own = jnp.pad(rest_own, ((0, 0), (0, GROUP * F - rest_own.shape[1])))
            rest_own = rest_own.reshape(shard, GROUP, F).swapaxes(0, 1)
            mine[last] = (rest_own.reshape(GROUP, 1, shard, F), 0)
            done = input_gradient
        elif k == 4:
            mixture = run_mix(ga_all, weights, part_rows, token, 60)
            mixture_own = lax.psum_scatter(
                mixture.reshape(GROUP * count_of_rows, MODEL_WIDTH),
                "inner",
                scatter_dimension=0,
                tiled=True,
            )
            done = mixture
        elif k == 5:
            done = adam_of(1, adam_of(0, token, 60), 1)
        elif k == 6:
            done = adam_of(3, adam_of(2, token, 60), 1)
        elif k - 3 < len(chunks):
            done = adam_of(k - 3, token, 60)
        waits.append(done)

        if k + 1 <= last:
            following = mine[k + 1]
        if k == last + 2:
            continue
        results = list(run_round(place, own, pair, following, waits))
        token = results[0]
        if own:
            by_pairs[k] = results.pop(0)
        if pair:
            totals_of[k - 1] = results.pop(0)
        edges[k + 1] = results.pop(0)

    block_output = (middle + alive * mixture_own.astype(jnp.float32)).astype(brain_floating)

    rest_states = (
        (norm_gains, gains_first, gains_second),
        (query_weight, query_first, query_second),
        (keyvalue_weight, keyvalue_first_moment, keyvalue_second_moment),
        (output_weight, output_first, output_second),
        (router_weight, router_first, router_second),
    )
    rates = (
        (gain_rate, 0.0),
        (root, decay_rate),
        (root, decay_rate),
        ((WIDTH // 16) ** (-0.5), decay_rate),
        ((4 * MODEL_WIDTH) ** (-0.5), decay_rate),
    )
    updated = adam_rest(place, totals_of[last], ends[last], rest_states, rates)
    return (block_output, input_gradient) + tuple(updated) + tuple(renewed[0]) + tuple(renewed[1])


def solution(mesh):
    replicas, shards = (mesh.shape["replica"], mesh.shape["fsdp"])
    outer = shards // GROUP
    split = Mesh(mesh.devices.reshape(replicas, outer, GROUP), ("replica",) + fsdp)
    rows = P(("replica",) + fsdp, None)
    by_first = P(fsdp, None)
    by_second = P(None, fsdp)
    by_middle = P(None, fsdp, None)
    by_third = P(None, None, fsdp, None)
    by_last = P(None, None, fsdp)
    weights = (by_second, by_first, by_middle, by_first, by_first, by_third, by_last)
    states = tuple(spec for spec in weights for _ in range(3))
    return jax.shard_map(
        functools.partial(body, (replicas, outer)),
        mesh=split,
        in_specs=(rows,) * 4 + states,
        out_specs=(rows,) * 2 + states,
        check_vma=False,
    )
```

```python
import functools
import math

import jax
import jax.numpy as jnp
from jax import lax
from jax.experimental import pallas as pl
from jax.experimental.pallas import tpu as pltpu
from jax.sharding import Mesh
from jax.sharding import PartitionSpec as P

MODEL_WIDTH = 1024
QUERY_HEADS = 16
KEYVALUE_HEADS = 8
HEAD_SIZE = 64
F = 512
TOPK = 8
EXPERTS = 16
ADAM_STEP = 5
GROUP = 8
LOCAL = EXPERTS // GROUP
EXTRA = 128
CHUNKS = 2
TILE = 512
SPAN = 256
LANES = 128
WIDTH = QUERY_HEADS * HEAD_SIZE
KV_WIDTH = KEYVALUE_HEADS * HEAD_SIZE
PROJECTED = WIDTH + 2 * KV_WIDTH
SCORE_SCALE = HEAD_SIZE ** (-0.5)
ROUTER_BLOCK = (PROJECTED + MODEL_WIDTH) // EXTRA


norm_eps = 1e-06
rope_base = 10000.0
beta_one = 0.9
beta_two = 0.95
adam_eps = 1e-08
decay_rate = 0.1
gain_rate = 0.25
masked_value = -1e30
brain_floating = jnp.bfloat16


def layout(lengths, count_of_rows):
    document_ends = jnp.cumsum(lengths)
    row_index = jnp.arange(count_of_rows, dtype=jnp.int32)
    passed = row_index[:, None] >= document_ends[None, :]
    segment = jnp.sum(passed.astype(jnp.int32), axis=1)
    start_row = jnp.sum(jnp.where(passed, lengths[None, :], 0), axis=1)
    position = (row_index - start_row).astype(jnp.float32)
    alive_mask = (segment < lengths.shape[0]).astype(jnp.float32)
    allowed = (segment[:, None] == segment[None, :]) & (row_index[None, :] <= row_index[:, None])
    return (position, alive_mask, allowed)


def rope_tables(position):
    half_width = HEAD_SIZE // 2
    exponents = jnp.arange(half_width, dtype=jnp.float32) * (2.0 / HEAD_SIZE)
    inverse = jnp.exp(exponents * -math.log(rope_base))
    angles = position[:, None] * inverse[None, :]
    cosine, sine = (jnp.cos(angles), jnp.sin(angles))
    return (
        jnp.concatenate([cosine] * 4, axis=1),
        jnp.concatenate([-sine, sine, -sine, sine], axis=1),
    )


def product(left, right):
    return jnp.dot(left, right, preferred_element_type=jnp.float32)


def times_transposed(left, right):
    return lax.dot_general(
        left, right, (((1,), (1,)), ((), ())), preferred_element_type=jnp.float32
    )


def transposed_times(left, right):
    return lax.dot_general(
        left, right, (((0,), (0,)), ((), ())), preferred_element_type=jnp.float32
    )


def normalize(values):
    inverse = lax.rsqrt(jnp.mean(values * values, axis=-1, keepdims=True) + norm_eps)
    return (values * inverse, inverse)


def norm_back(upstream, scaled_rows, inverse, gain_row):
    weighted = upstream * gain_row
    inner = jnp.mean(weighted * scaled_rows, axis=-1, keepdims=True)
    return inverse * (weighted - scaled_rows * inner)


def column_sums(values):
    ones = jnp.ones((values.shape[0], LANES), brain_floating)
    high = values.astype(brain_floating)
    low = (values - high.astype(jnp.float32)).astype(brain_floating)
    return transposed_times(high, ones) + transposed_times(low, ones)


def lanes_of(shape):
    return lax.broadcasted_iota(jnp.int32, shape, 1)


def rotate(values, cosine, sine):
    half = HEAD_SIZE // 2
    front = lax.rem(lanes_of(values.shape), HEAD_SIZE) < half
    swapped = jnp.where(
        front, pltpu.roll(values, LANES - half, 1), pltpu.roll(values, half, 1)
    )
    return values * cosine + swapped * sine


def both_halves(values, which):
    turned = pltpu.roll(values, HEAD_SIZE, 1)
    first = lanes_of(values.shape) < HEAD_SIZE
    return jnp.where(first == (which == 0), values, turned)


def only_half(values, which):
    first = lanes_of(values.shape) < HEAD_SIZE
    return jnp.where(first == (which == 0), values, 0.0)


def gates_of(rows, router, mask):
    logits = product(rows, router)
    peak = jnp.max(jnp.where(mask, logits, masked_value), axis=1, keepdims=True)
    weights = jnp.where(mask, jnp.exp(logits - peak), 0.0)
    return weights / jnp.sum(weights, axis=1, keepdims=True)


def adamw_step(weight, moment_old, square_old, gradient, step_rate, shrink):
    moment = beta_one * moment_old + (1.0 - beta_one) * gradient
    square = beta_two * square_old + (1.0 - beta_two) * gradient * gradient
    moment_hat = moment / (1.0 - beta_one**ADAM_STEP)
    square_hat = square / (1.0 - beta_two**ADAM_STEP)
    renewed = weight - step_rate * (
        moment_hat / (jnp.sqrt(square_hat) + adam_eps) + shrink * weight
    )
    return (moment, square, renewed)


MIB = 1024 * 1024
ANYWHERE = pl.BlockSpec(memory_space=pl.ANY)


def takes(microseconds):
    return pl.CostEstimate(
        flops=int(microseconds * 1e9), bytes_accessed=int(microseconds * 3.6e6), transcendentals=0
    )


def whole(shape):
    return pl.BlockSpec(shape, lambda *_: (0,) * len(shape), pipeline_mode=pl.Buffered(1))


def part(shape, place):
    return pl.BlockSpec(shape, lambda *_: place, pipeline_mode=pl.Buffered(1))


def out(shape, dtype):
    return jax.ShapeDtypeStruct(shape, dtype)


def split_kernel(odd_ref, gateup_ref, down_ref, out_ref):
    for k in range(2):
        out_ref[k, 0] = gateup_ref[k, 0].astype(brain_floating)
        out_ref[k, 1] = gateup_ref[k, 1].astype(brain_floating)
        out_ref[k, 2] = down_ref[k].T.astype(brain_floating)


def split_by_owner(odd, gateup, down):
    shard = gateup.shape[2]
    steps = GROUP // 2
    return pl.pallas_call(
        split_kernel,
        grid_spec=pltpu.PrefetchScalarGridSpec(
            num_scalar_prefetch=1,
            grid=(steps,),
            in_specs=[
                pl.BlockSpec((2, 2, shard, F), lambda e, odd: (e + steps * odd[0], 0, 0, 0)),
                pl.BlockSpec((2, F, shard), lambda e, odd: (e + steps * odd[0], 0, 0)),
            ],
            out_specs=pl.BlockSpec((2, 3, shard, F), lambda e, odd: (e, 0, 0, 0)),
        ),
        out_shape=out((GROUP, 3, shard, F), brain_floating),
        name="split",
    )(odd, gateup, down)


def front_kernel(
    x_ref, pack_ref, gains_ref, alive_ref, bias_ref, cos_ref, sin_ref, wait_ref, normed_ref, qkv_ref, mixed_ref, totals_ref, middle_ref, normed_two_ref, linear_ref,
):
    rows = x_ref.shape[0]
    scaled, _ = normalize(x_ref[...].astype(jnp.float32))
    normed = (scaled * gains_ref[0:1, :]).astype(brain_floating)
    normed_ref[...] = normed
    linear_ref[...] = product(normed, pack_ref[:, :PROJECTED])
    cosine, sine = (cos_ref[...], sin_ref[...])
    for at in range(0, WIDTH + KV_WIDTH, LANES):
        qkv_ref[:, at : at + LANES] = rotate(
            linear_ref[:, at : at + LANES], cosine, sine
        ).astype(brain_floating)
    qkv_ref[:, WIDTH + KV_WIDTH :] = linear_ref[:, WIDTH + KV_WIDTH :].astype(brain_floating)
    totals_ref[...] = jnp.zeros_like(totals_ref)

    @pl.loop(0, KEYVALUE_HEADS // 2)
    def _(pair):
        at = pl.multiple_of(pair * LANES, LANES)
        keys = qkv_ref[:, pl.ds(WIDTH + at, LANES)].astype(jnp.float32)
        values = qkv_ref[:, pl.ds(WIDTH + KV_WIDTH + at, LANES)].astype(jnp.float32)
        for a in range(2):
            head_keys = both_halves(keys, a).astype(brain_floating)
            head_values = both_halves(values, a)
            place = pl.multiple_of((2 * pair + a) * LANES, LANES)
            queries = qkv_ref[:, pl.ds(place, LANES)].astype(jnp.float32)
            for start in range(0, rows, SPAN):
                seen = min(start + SPAN, rows)
                mixed = jnp.zeros((SPAN, LANES), jnp.float32)
                for j in range(2):
                    head = 2 * (2 * pair + a) + j
                    query = only_half(queries[start : start + SPAN], j).astype(brain_floating)
                    scores = (
                        times_transposed(query, head_keys[:seen]) * SCORE_SCALE
                        + bias_ref[start : start + SPAN, :seen]
                    )
                    peak = jnp.max(scores, axis=1, keepdims=True)
                    weights = jnp.exp(scores - peak)
                    total = jnp.sum(weights, axis=1, keepdims=True)
                    probs = (weights * (1.0 / total)).astype(brain_floating)
                    mixed += product(probs, only_half(head_values[:seen], j).astype(brain_floating))
                    held = totals_ref[start : start + SPAN, :]
                    totals_ref[start : start + SPAN, :] = jnp.where(
                        lanes_of(held.shape) == head, peak + jnp.log(total), held
                    )
                mixed_ref[start : start + SPAN, pl.ds(place, LANES)] = mixed.astype(brain_floating)

    attended = product(mixed_ref[...], pack_ref[:, PROJECTED : PROJECTED + MODEL_WIDTH])
    middle = x_ref[...].astype(jnp.float32) + alive_ref[...] * attended
    middle_ref[...] = middle
    scaled_two, _ = normalize(middle)
    normed_two_ref[...] = (scaled_two * gains_ref[1:2, :]).astype(brain_floating)


def run_front(x, pack, gains, alive, bias, cosine, sine, wait):
    rows = x.shape[0]
    return pl.pallas_call(
        front_kernel,
        in_specs=[pl.BlockSpec(memory_space=pltpu.VMEM)] * 7 + [ANYWHERE],
        out_shape=[
            out((rows, MODEL_WIDTH), brain_floating),
            out((rows, PROJECTED), brain_floating),
            out((rows, WIDTH), brain_floating),
            out((rows, LANES), jnp.float32),
            out((rows, MODEL_WIDTH), jnp.float32),
            out((rows, MODEL_WIDTH), brain_floating),
        ],
        scratch_shapes=[pltpu.VMEM((rows, PROJECTED), jnp.float32)],
        compiler_params=pltpu.CompilerParams(vmem_limit_bytes=52 * MIB),
        name="front",
    )(x, pack, gains, alive, bias, cosine, sine, wait)


def middle_kernel(
    dx_ref, normed_two_ref, middle_ref, cot_ref, mask_ref, alive_ref, gains_ref, router_ref,
    output_ref, mixed_ref, wait_ref, d_middle_ref, d_mixed_ref, grads_ref,
):
    dx = dx_ref[...].astype(jnp.float32)
    normed_two = normed_two_ref[...]
    mask = mask_ref[...].astype(jnp.float32) > 0.5
    gates = gates_of(normed_two, router_ref[...], mask)
    extra = dx[:, MODEL_WIDTH:]
    d_gates = extra + pltpu.roll(extra, LANES - EXPERTS, 1)
    d_logits = (
        gates * (d_gates - jnp.sum(gates * d_gates, axis=1, keepdims=True))
    ).astype(brain_floating)
    d_normed = dx[:, :MODEL_WIDTH] + times_transposed(d_logits, router_ref[...])
    scaled, inverse = normalize(middle_ref[...])
    d_middle = cot_ref[...].astype(jnp.float32) + norm_back(
        d_normed, scaled, inverse, gains_ref[1:2, :]
    )
    d_middle_ref[...] = d_middle
    d_attended = (alive_ref[...] * d_middle).astype(brain_floating)
    grads_ref[:, :MODEL_WIDTH] = transposed_times(mixed_ref[...], d_attended).astype(brain_floating)
    small = transposed_times(normed_two, d_logits)
    small = jnp.where(lanes_of(small.shape) == EXPERTS + 1, column_sums(d_normed * scaled), small)
    grads_ref[:, MODEL_WIDTH:] = small.astype(brain_floating)
    d_mixed_ref[...] = times_transposed(d_attended, output_ref[...]).astype(brain_floating)


def run_middle(dx, normed_two, middle, cot, mask, alive, gains, pack, mixed, wait):
    rows = middle.shape[0]
    full = [whole(v.shape) for v in (dx, normed_two, middle, cot, mask, alive, gains)]
    return pl.pallas_call(
        middle_kernel,
        grid=(1,),
        in_specs=full
        + [
            part((MODEL_WIDTH, EXTRA), (0, ROUTER_BLOCK)),
            part((WIDTH, MODEL_WIDTH), (0, PROJECTED // MODEL_WIDTH)),
            whole(mixed.shape),
            ANYWHERE,
        ],
        out_specs=[
            whole((rows, MODEL_WIDTH)),
            whole((rows, WIDTH)),
            whole((MODEL_WIDTH, MODEL_WIDTH + EXTRA)),
        ],
        out_shape=[
            out((rows, MODEL_WIDTH), jnp.float32),
            out((rows, WIDTH), brain_floating),
            out((MODEL_WIDTH, MODEL_WIDTH + EXTRA), brain_floating),
        ],
        compiler_params=pltpu.CompilerParams(vmem_limit_bytes=52 * MIB),
        cost_estimate=takes(30),
        name="middle_back",
    )(dx, normed_two, middle, cot, mask, alive, gains, pack, pack, mixed, wait)


def back_kernel(
    d_mixed_ref, qkv_ref, totals_ref, bias_ref, cos_ref, sin_ref, normed_ref, x_ref, d_middle_ref,
    gains_ref, other_ref, pack_ref, wait_ref, also_ref, grads_ref, d_input_ref, d_linear_ref, d_keys_ref, d_values_ref,
):
    rows = x_ref.shape[0]
    cosine, sine = (cos_ref[...], -sin_ref[...])

    @pl.loop(0, KEYVALUE_HEADS // 2)
    def _(pair):
        at = pl.multiple_of(pair * LANES, LANES)
        keys = qkv_ref[:, pl.ds(WIDTH + at, LANES)].astype(jnp.float32)
        values = qkv_ref[:, pl.ds(WIDTH + KV_WIDTH + at, LANES)].astype(jnp.float32)
        pair_keys = jnp.zeros((rows, LANES), jnp.float32)
        pair_values = jnp.zeros((rows, LANES), jnp.float32)
        for a in range(2):
            both_keys = both_halves(keys, a)
            head_keys = both_keys.astype(brain_floating)
            head_values = both_halves(values, a).astype(brain_floating)
            place = pl.multiple_of((2 * pair + a) * LANES, LANES)
            queries = qkv_ref[:, pl.ds(place, LANES)].astype(jnp.float32)
            d_outs = d_mixed_ref[:, pl.ds(place, LANES)].astype(jnp.float32)
            d_keys_ref[...] = jnp.zeros_like(d_keys_ref)
            d_values_ref[...] = jnp.zeros_like(d_values_ref)
            for start in range(0, rows, SPAN):
                seen = min(start + SPAN, rows)
                d_query = jnp.zeros((SPAN, LANES), jnp.float32)
                for j in range(2):
                    head = 2 * (2 * pair + a) + j
                    query = only_half(queries[start : start + SPAN], j).astype(brain_floating)
                    d_out = only_half(d_outs[start : start + SPAN], j).astype(brain_floating)
                    held = totals_ref[start : start + SPAN, :]
                    total = jnp.sum(
                        jnp.where(lanes_of(held.shape) == head, held, 0.0), axis=1, keepdims=True
                    )
                    scores = (
                        times_transposed(query, head_keys[:seen]) * SCORE_SCALE
                        + bias_ref[start : start + SPAN, :seen]
                    )
                    probs = jnp.exp(scores - total)
                    d_probs = times_transposed(d_out, head_values[:seen])
                    inner = jnp.sum(probs * d_probs, axis=1, keepdims=True)
                    d_scores = (probs * (d_probs - inner)).astype(brain_floating)
                    d_query += product(
                        d_scores, only_half(both_keys[:seen], j).astype(brain_floating)
                    )
                    d_keys_ref[:seen, :] += transposed_times(d_scores, query)
                    d_values_ref[:seen, :] += transposed_times(probs.astype(brain_floating), d_out)
                d_linear_ref[start : start + SPAN, pl.ds(place, LANES)] = rotate(
                    d_query * SCORE_SCALE,
                    cosine[start : start + SPAN],
                    sine[start : start + SPAN],
                ).astype(brain_floating)
            d_keys = d_keys_ref[...]
            d_values = d_values_ref[...]
            pair_keys += only_half(d_keys + pltpu.roll(d_keys, HEAD_SIZE, 1), a)
            pair_values += only_half(d_values + pltpu.roll(d_values, HEAD_SIZE, 1), a)
        d_linear_ref[:, pl.ds(WIDTH + at, LANES)] = rotate(
            pair_keys * SCORE_SCALE, cosine, sine
        ).astype(brain_floating)
        d_linear_ref[:, pl.ds(WIDTH + KV_WIDTH + at, LANES)] = pair_values.astype(brain_floating)

    normed = normed_ref[...]
    for at in range(0, PROJECTED, 512):
        grads_ref[:, at : at + 512] = transposed_times(
            normed, d_linear_ref[:, at : at + 512]
        ).astype(brain_floating)
    d_normed = times_transposed(d_linear_ref[...], pack_ref[...])
    scaled, inverse = normalize(x_ref[...].astype(jnp.float32))
    sums = column_sums(d_normed * scaled)
    grads_ref[:, PROJECTED : PROJECTED + MODEL_WIDTH] = other_ref[:, :MODEL_WIDTH]
    small = other_ref[:, MODEL_WIDTH:].astype(jnp.float32)
    grads_ref[:, PROJECTED + MODEL_WIDTH :] = jnp.where(
        lanes_of(sums.shape) == EXPERTS, sums, small
    ).astype(brain_floating)
    d_input_ref[...] = d_middle_ref[...] + norm_back(d_normed, scaled, inverse, gains_ref[0:1, :])


def run_back(
    d_mixed, qkv, totals, bias, cosine, sine, normed, x, d_middle, gains, other, pack, wait, also
):
    rows = x.shape[0]
    held = (d_mixed, qkv, totals, bias, cosine, sine, normed, x, d_middle, gains, other)
    width = PROJECTED + other.shape[1]
    return pl.pallas_call(
        back_kernel,
        grid=(1,),
        in_specs=[whole(v.shape) for v in held]
        + [part((MODEL_WIDTH, PROJECTED), (0, 0)), ANYWHERE, ANYWHERE],
        out_specs=[whole((MODEL_WIDTH, width)), whole((rows, MODEL_WIDTH))],
        out_shape=[
            out((MODEL_WIDTH, width), brain_floating),
            out((rows, MODEL_WIDTH), jnp.float32),
        ],
        scratch_shapes=[
            pltpu.VMEM((rows, PROJECTED), brain_floating),
            pltpu.VMEM((rows, LANES), jnp.float32),
            pltpu.VMEM((rows, LANES), jnp.float32),
        ],
        compiler_params=pltpu.CompilerParams(vmem_limit_bytes=52 * MIB),
        cost_estimate=takes(30),
        name="attention_back",
    )(*held, pack, wait, also)


def expert_kernel(me_ref, x_ref, b_ref, w_one_ref, w_two_ref, router_ref, *refs):
    ga_ref, dgu_ref, dx_ref = refs[-3:]
    x = x_ref[...]
    branch = b_ref[:, 0, :, :MODEL_WIDTH].reshape(x.shape)
    mask = b_ref[:, 0, :, MODEL_WIDTH:].reshape(x.shape[0], EXTRA).astype(jnp.float32) > 0.5
    gates = gates_of(x, router_ref[...], mask)
    lane = lanes_of(gates.shape)
    d_gates = jnp.zeros_like(gates)
    dx = jnp.zeros((x.shape[0], MODEL_WIDTH), jnp.float32)
    for local in range(LOCAL):
        expert = me_ref[0] + GROUP * lax.rem(me_ref[1] + local, LOCAL)
        w_ref = (w_one_ref, w_two_ref)[local]
        gate_weight, up_weight, down_weight = (
            w_ref[:, p].reshape(MODEL_WIDTH, F) for p in range(3)
        )
        gate = jnp.sum(jnp.where(lane == expert, gates, 0.0), axis=1, keepdims=True)
        gate_linear = product(x, gate_weight)
        up_linear = product(x, up_weight)
        back = product(branch, down_weight)
        sig = jax.nn.sigmoid(gate_linear)
        silu = gate_linear * sig
        act = silu * up_linear
        ga_ref[:, local * F : (local + 1) * F] = (gate * act).astype(brain_floating)
        d_gate = jnp.sum(act * back, axis=1, keepdims=True)
        high = d_gate.astype(brain_floating).astype(jnp.float32)
        d_gates += jnp.where(lane == expert, high, 0.0)
        d_gates += jnp.where(lane == expert + EXPERTS, d_gate - high, 0.0)
        d_act = gate * back
        d_gl = (d_act * up_linear * (sig + silu * (1.0 - sig))).astype(brain_floating)
        d_ul = (d_act * silu).astype(brain_floating)
        dgu_ref[:, 2 * local * F : (2 * local + 1) * F] = d_gl
        dgu_ref[:, (2 * local + 1) * F : (2 * local + 2) * F] = d_ul
        dx += times_transposed(d_gl, gate_weight) + times_transposed(d_ul, up_weight)
    blocks, _, part_rows, _ = dx_ref.shape
    dx_ref[:, 0, :, :MODEL_WIDTH] = dx.astype(brain_floating).reshape(
        blocks, part_rows, MODEL_WIDTH
    )
    dx_ref[:, 0, :, MODEL_WIDTH:] = d_gates.astype(brain_floating).reshape(
        blocks, part_rows, EXTRA
    )


def run_experts(me, c, x, b, weights, pack, before):
    rows = x.shape[0]
    part_rows = b.shape[2]
    tile = 2 * part_rows
    wide = MODEL_WIDTH + EXTRA

    def rowed(width):
        return pl.BlockSpec((tile, width), lambda i, me_ref: (i, 0))

    return pl.pallas_call(
        expert_kernel,
        grid_spec=pltpu.PrefetchScalarGridSpec(
            num_scalar_prefetch=1,
            grid=(rows // tile,),
            in_specs=[
                rowed(MODEL_WIDTH),
                pl.BlockSpec((2, 1, part_rows, wide), lambda i, me_ref: (i, c, 0, 0)),
                whole(weights[0].shape),
                whole(weights[1].shape),
                part((MODEL_WIDTH, EXTRA), (0, ROUTER_BLOCK)),
            ]
            + [ANYWHERE] * len(before),
            out_specs=[
                rowed(LOCAL * F),
                rowed(2 * LOCAL * F),
                pl.BlockSpec((2, 1, part_rows, wide), lambda i, me_ref: (i, c, 0, 0)),
            ],
        ),
        out_shape=[
            out((rows, LOCAL * F), brain_floating),
            out((rows, 2 * LOCAL * F), brain_floating),
            out((rows // part_rows, CHUNKS, part_rows, wide), brain_floating),
        ],
        input_output_aliases={6 + i: 2 for i in range(len(before))},
        compiler_params=pltpu.CompilerParams(vmem_limit_bytes=56 * MIB),
        name="experts",
    )(me, x, b, *weights, pack, *before)


def chunked_specs(steps, shape, place):
    def index(c):
        return lambda i, *scalars: place(jnp.clip(i - c * steps, 0, steps - 1), c, *scalars)

    return [pl.BlockSpec(shape, index(c)) for c in range(CHUNKS)]


def grads_kernel(steps, sides, me_ref, *refs):
    count = len(sides)
    ins, outs, sums = (refs[: CHUNKS * 2 * count], refs[-2 * count : -count], refs[-count:])
    i = pl.program_id(0)

    @pl.when(i == 0)
    def _():
        for total in sums:
            total[...] = jnp.zeros_like(total)

    for c in range(CHUNKS):

        @pl.when(i // steps == c)
        def _():
            for k in range(count):
                left, right = (ins[2 * (k * CHUNKS + c)], ins[2 * (k * CHUNKS + c) + 1])
                sums[k][...] += transposed_times(
                    left[...].reshape(right.shape[0], MODEL_WIDTH), right[...]
                )

    @pl.when(i == CHUNKS * steps - 1)
    def _():
        for result, total in zip(outs, sums):
            result[...] = total[...].astype(brain_floating).reshape(result.shape)


def run_grads(me, local, sides, shard, xs, b, gas, dgus, wait, cost):
    blocks = MODEL_WIDTH // shard
    rows, part_rows = (xs[0].shape[0], b.shape[2])
    tile = 2 * part_rows
    steps = rows // tile
    specs, arrays = ([], [])
    for side in sides:
        if side == 2:
            left = chunked_specs(
                steps, (2, 1, part_rows, MODEL_WIDTH), lambda i, c, me: (i, c, 0, 0)
            )
            right = chunked_specs(
                steps, (tile, F), lambda i, c, me: (i, lax.rem(me[1] + local, LOCAL))
            )
        else:
            left = chunked_specs(steps, (tile, MODEL_WIDTH), lambda i, c, me: (i, 0))
            right = chunked_specs(
                steps,
                (tile, F),
                lambda i, c, me, side=side: (i, 2 * lax.rem(me[1] + local, LOCAL) + side),
            )
        for c in range(CHUNKS):
            specs += [left[c], right[c]]
            arrays += [b, gas[c]] if side == 2 else [xs[c], dgus[c]]
    return pl.pallas_call(
        functools.partial(grads_kernel, steps, sides),
        grid_spec=pltpu.PrefetchScalarGridSpec(
            num_scalar_prefetch=1,
            grid=(CHUNKS * steps,),
            in_specs=specs + [ANYWHERE],
            out_specs=[whole((blocks, shard, F))] * len(sides),
            scratch_shapes=[pltpu.VMEM((MODEL_WIDTH, F), jnp.float32)] * len(sides),
        ),
        out_shape=[out((blocks, shard, F), brain_floating)] * len(sides),
        compiler_params=pltpu.CompilerParams(vmem_limit_bytes=52 * MIB),
        cost_estimate=takes(cost),
        name="grads",
    )(me, *arrays, wait)


def mix_kernel(steps, *refs):
    gas, w_refs, out_ref = (refs[:CHUNKS], refs[CHUNKS : CHUNKS + LOCAL], refs[-1])
    for c in range(CHUNKS):

        @pl.when(pl.program_id(0) // steps == c)
        def _():
            total = jnp.zeros((gas[c].shape[0], MODEL_WIDTH), jnp.float32)
            for local in range(LOCAL):
                total += times_transposed(
                    gas[c][:, local * F : (local + 1) * F],
                    w_refs[local][:, 0].reshape(MODEL_WIDTH, F),
                )
            out_ref[...] = total.astype(brain_floating).reshape(out_ref.shape)


def run_mix(gas, weights, part_rows, wait, cost):
    rows = gas[0].shape[0]
    tile = 2 * part_rows
    steps = rows // tile
    blocks, _, shard, _ = weights[0].shape
    return pl.pallas_call(
        functools.partial(mix_kernel, steps),
        grid=(CHUNKS * steps,),
        in_specs=chunked_specs(steps, (tile, LOCAL * F), lambda i, c: (i, 0))
        + [part((blocks, 1, shard, F), (0, 2, 0, 0))] * LOCAL
        + [ANYWHERE],
        out_specs=pl.BlockSpec(
            (2, 1, part_rows, MODEL_WIDTH), lambda i: (lax.rem(i, steps), i // steps, 0, 0)
        ),
        out_shape=out((rows // part_rows, CHUNKS, part_rows, MODEL_WIDTH), brain_floating),
        compiler_params=pltpu.CompilerParams(vmem_limit_bytes=52 * MIB),
        cost_estimate=takes(cost),
        name="mixture",
    )(*gas, *weights, wait)


def at_inner(place_ref):
    return (place_ref[0] == 1) | (place_ref[0] == 2)


def as_chunk(values):
    if values.ndim == 2:
        return jnp.stack([values[:, :F], values[:, F:]])
    return values


def round_kernel(kinds, waits, place_ref, *refs):
    has_own, has_pair, has_next = kinds
    refs = list(refs)

    def take(count):
        taken, refs[:count] = (refs[:count], [])
        return [as_chunk(ref[...].astype(jnp.float32)) for ref in taken]

    own = take(2) if has_own else None
    pair = take(2) if has_pair else None
    edge = take(1)[0] if has_next else None
    outs = refs[waits:]
    if has_own:
        outs.pop(0)[...] = (own[0] + own[1]).astype(brain_floating)
    if has_pair:
        total = pair[0] + pair[1]
        outs.pop(0)[...] = total.astype(brain_floating)
        edge = total if edge is None else jnp.where(at_inner(place_ref), total, edge)
    outs.pop(0)[...] = edge.astype(brain_floating)


def run_round(place, own, pair, following, waits):
    steps = GROUP // 2
    arrays, specs, count = ([], [], 0)

    flat = pair[0].shape if pair else following.shape
    piece = pl.BlockSpec((2,) + flat[1:], lambda i, _: (i, 0, 0))

    def chunk_spec(values):
        if values.ndim == 2:
            return pl.BlockSpec((values.shape[0], 2 * F), lambda i, _: (0, i))
        return piece

    if own:
        arrays += list(own)
        specs += [chunk_spec(own[0]), piece]
        count += 1
    if pair:
        arrays += list(pair)
        specs += [piece] * 2
        count += 1
    if following is not None:
        arrays.append(following)
        specs.append(chunk_spec(following))
    count += 1
    return pl.pallas_call(
        functools.partial(
            round_kernel, (bool(own), bool(pair), following is not None), len(waits)
        ),
        grid_spec=pltpu.PrefetchScalarGridSpec(
            num_scalar_prefetch=1,
            grid=(steps,),
            in_specs=specs + [ANYWHERE] * len(waits),
            out_specs=[piece] * count,
        ),
        out_shape=[out(flat, brain_floating)] * count,
        compiler_params=pltpu.CompilerParams(vmem_limit_bytes=40 * MIB),
        cost_estimate=takes(2),
        name="round",
    )(place, *arrays, *waits)


def after_kernel(values_ref, wait_ref, out_ref):
    del values_ref, wait_ref, out_ref


def after(values, wait):
    return pl.pallas_call(
        after_kernel,
        in_specs=[ANYWHERE] * 2,
        out_specs=ANYWHERE,
        out_shape=out(values.shape, values.dtype),
        input_output_aliases={0: 0},
        name="after",
    )(values, wait)


def adam_kernel(turned, rate, shrink, place_ref, t_ref, r_ref, w_ref, m_ref, v_ref, *rest):
    m_out, v_out, w_out, token_ref = rest[-4:]
    token_ref[...] = jnp.zeros_like(token_ref)
    inner = at_inner(place_ref)
    for k in range(t_ref.shape[0]):
        gradient = jnp.where(inner, t_ref[k].astype(jnp.float32), r_ref[k].astype(jnp.float32))
        if turned:
            at = (k,)
            gradient = gradient.T
        else:
            at = (k, 0)
        moment, square, renewed = adamw_step(
            w_ref[at], m_ref[at], v_ref[at], gradient, rate, shrink
        )
        m_out[at] = moment
        v_out[at] = square
        w_out[at] = renewed


def adam_part(place, total, ends, state, local, side, rate, before, wait, cost):
    weight, first, second = state
    turned = side == 2
    shard = total.shape[1]
    held = [] if before is None else list(before)
    if turned:
        spec = pl.BlockSpec((2, F, shard), lambda i, _: (i + local * (GROUP // 2), 0, 0))
    else:
        spec = pl.BlockSpec((2, 1, shard, F), lambda i, _: (i + local * (GROUP // 2), side, 0, 0))
    piece = pl.BlockSpec((2, shard, F), lambda i, _: (i, 0, 0))
    return pl.pallas_call(
        functools.partial(adam_kernel, turned, rate, decay_rate),
        grid_spec=pltpu.PrefetchScalarGridSpec(
            num_scalar_prefetch=1,
            grid=(GROUP // 2,),
            in_specs=[piece, piece, spec, spec, spec] + [ANYWHERE] * (len(held) + 1),
            out_specs=[spec] * 3 + [pl.BlockSpec((8, LANES), lambda i, _: (0, 0))],
        ),
        out_shape=[out(weight.shape, jnp.float32)] * 3 + [out((8, LANES), jnp.float32)],
        input_output_aliases={6 + i: i for i in range(len(held))},
        compiler_params=pltpu.CompilerParams(vmem_limit_bytes=60 * MIB),
        cost_estimate=takes(cost),
        name="adam",
    )(place, total, ends, weight, first, second, *held, wait)


def rest_kernel(rates, place_ref, t_ref, r_ref, *refs):
    inner = at_inner(place_ref)
    states, outs = (refs[:15], refs[15:])

    def gradient(j):
        return jnp.where(inner, t_ref[j].astype(jnp.float32), r_ref[j].astype(jnp.float32))

    def step(which, at, gradient):
        weight, first, second = states[3 * which : 3 * which + 3]
        rate, shrink = rates[which]
        results = adamw_step(weight[at], first[at], second[at], gradient, rate, shrink)
        for ref, value in zip(outs[3 * which : 3 * which + 3], results):
            ref[at] = value

    small = gradient(PROJECTED // F + 2)[:, :EXTRA]
    step(0, ..., small.T[EXPERTS : EXPERTS + 2, :])
    step(4, ..., small[:, :EXPERTS])
    for half in range(2):
        at = (slice(None), slice(half * F, half * F + F))
        step(1, at, gradient(half))
        step(2, half, gradient(2 + half))
        step(3, at, gradient(4 + half))


def adam_rest(place, total, ends, states, rates):
    flat = [v for state in states for v in state]
    in_vmem = pl.BlockSpec(memory_space=pltpu.VMEM)
    return pl.pallas_call(
        functools.partial(rest_kernel, rates),
        in_specs=[pl.BlockSpec(memory_space=pltpu.SMEM)] + [in_vmem] * (2 + len(flat)),
        out_shape=[out(v.shape, jnp.float32) for v in flat],
        compiler_params=pltpu.CompilerParams(vmem_limit_bytes=40 * MIB),
        name="adam_rest",
    )(place, total, ends, *flat)


fsdp = ("outer", "inner")


def body(
    sizes,
    tokens_in,
    cotangent,
    document_lengths,
    expert_choice,
    norm_gains,
    gains_first,
    gains_second,
    query_weight,
    query_first,
    query_second,
    keyvalue_weight,
    keyvalue_first_moment,
    keyvalue_second_moment,
    output_weight,
    output_first,
    output_second,
    router_weight,
    router_first,
    router_second,
    gateup_weight,
    gateup_first,
    gateup_second,
    down_weight,
    down_first,
    down_second,
):
    replicas, outer = sizes
    count_of_rows = tokens_in.shape[0]
    shard = query_weight.shape[0]
    place = lax.axis_index("replica").astype(jnp.int32).reshape(1)
    odd = lax.rem(place, LOCAL)
    me = jnp.concatenate([lax.axis_index("inner").astype(jnp.int32).reshape(1), odd])

    pack_own = jnp.concatenate(
        [
            query_weight,
            keyvalue_weight[0],
            keyvalue_weight[1],
            output_weight,
            router_weight,
            norm_gains.T,
            jnp.zeros((shard, EXTRA - EXPERTS - 2), jnp.float32),
        ],
        axis=1,
    ).astype(brain_floating)
    pack = lax.all_gather(pack_own, fsdp, axis=0, tiled=True)
    at = PROJECTED + MODEL_WIDTH + EXPERTS
    gains_value = pack[:, at : at + 2].astype(jnp.float32).T

    weights_own = lax.all_to_all(split_by_owner(odd, gateup_weight, down_weight), "inner", 0, 0)
    if outer > 1:
        weights_own = lax.all_gather(weights_own, "outer", axis=0, tiled=True)
    weights = (
        weights_own,
        lax.ppermute(weights_own, "replica", [(0, 1), (1, 0), (2, 3), (3, 2)]),
    )

    position, alive_mask, allowed = layout(document_lengths[0], count_of_rows)
    cosine, sine = rope_tables(position)
    alive = alive_mask[:, None]
    bias = jnp.where(allowed, 0.0, masked_value)

    expert_row = jnp.arange(EXPERTS, dtype=jnp.int32)
    chosen = jnp.any(expert_choice[:, :, None] == expert_row[None, None, :], axis=1)
    mask = jnp.concatenate(
        [
            chosen.astype(brain_floating),
            jnp.zeros((count_of_rows, EXTRA - EXPERTS), brain_floating),
        ],
        axis=1,
    )
    branch = (alive * cotangent.astype(jnp.float32)).astype(brain_floating)
    branch_pack = jnp.concatenate([branch, mask], axis=1)
    part_rows = count_of_rows // CHUNKS

    def gathered(values, c):
        return lax.all_gather(
            values[c * part_rows : (c + 1) * part_rows], "inner", axis=0, tiled=True
        )

    branch_all = lax.all_gather(branch_pack, "inner", axis=0, tiled=True).reshape(
        GROUP, CHUNKS, part_rows, MODEL_WIDTH + EXTRA
    )

    normed, qkv, mixed, totals, middle, normed_two = run_front(
        tokens_in, pack, gains_value, alive, bias, cosine, sine, weights_own
    )

    x_all, ga_all, dgu_all, dx = ([], [], [], None)
    for c in range(CHUNKS):
        x_part = gathered(normed_two, c)
        ga, dgu, dx = run_experts(
            me, c, x_part, branch_all, weights, pack, () if dx is None else (dx,)
        )
        x_all.append(x_part)
        ga_all.append(ga)
        dgu_all.append(dgu)
    dx_own = lax.psum_scatter(
        dx.reshape(GROUP * count_of_rows, MODEL_WIDTH + EXTRA),
        "inner",
        scatter_dimension=0,
        tiled=True,
    )

    def to_owner(parts):
        if outer > 1:
            parts = lax.psum_scatter(parts, "outer", scatter_dimension=0, tiled=True)
        return lax.all_to_all(parts, "inner", 0, 0)

    def swapped(values):
        return lax.ppermute(values, "replica", [(0, 1), (1, 0), (2, 3), (3, 2)])

    def across(values):
        return lax.ppermute(values, "replica", [(1, 2), (2, 1)])

    def grads_of(local, sides, wait, cost):
        return run_grads(me, local, sides, shard, x_all, branch_all, ga_all, dgu_all, wait, cost)

    chunks = [(local, side) for local in range(LOCAL) for side in (2, 0, 1)]
    last = len(chunks)
    root = MODEL_WIDTH ** (-0.5)
    states = (
        (gateup_weight, gateup_first, gateup_second),
        (down_weight, down_first, down_second),
    )
    renewed = [None, None]
    by_pairs, totals_of, ends, edges = ({}, {}, {}, {})

    def adam_of(k, wait, cost):
        local, side = chunks[k]
        which = side // 2
        *renewed[which], done = adam_part(
            place, totals_of[k], ends[k], states[which], local, side,
            (F // 16) ** (-0.5) if which else root, renewed[which], wait, cost,
        )
        return done

    ready = grads_of(0, (2,), dgu_all[-1], 1)
    token = ready[0]
    mine = {0: to_owner(token)}
    for k in range(-1, last + 3):
        own, pair, following, waits = (None, None, None, [])
        if k in edges:
            arrived = swapped(edges[k])
            ends[k - 2] = arrived
            if k <= last:
                own = (mine[k], arrived)
            else:
                waits.append(arrived)
        if k - 1 in by_pairs:
            pair = (by_pairs[k - 1], across(by_pairs[k - 1]))

        if 0 <= k < len(chunks) - 1:
            mine[k + 1] = to_owner(after(ready[k + 1], token))
        if k == -1:
            ready += grads_of(0, (0, 1), token, 1)
            done = ready[1]
        elif k == 0:
            ready += grads_of(1, (2,), token, 3)
            done = ready[3]
        elif k == 1:
            ready += grads_of(1, (0, 1), token, 3)
            done = ready[4]
        elif k == 2:
            d_middle, d_mixed, second_grads = run_middle(
                dx_own, normed_two, middle, cotangent, mask, alive, gains_value, pack, mixed, token
            )
            done = d_mixed
        elif k == 3:
            rest_grads, input_gradient = run_back(
                d_mixed, qkv, totals, bias, cosine, sine, normed, tokens_in, d_middle, gains_value,
                second_grads, pack, token, token,
            )
            mine[last] = lax.psum_scatter(rest_grads, fsdp, scatter_dimension=0, tiled=True)
            done = input_gradient
        elif k == 4:
            mixture = run_mix(ga_all, weights, part_rows, token, 300)
            mixture_own = lax.psum_scatter(
                mixture.reshape(GROUP * count_of_rows, MODEL_WIDTH),
                "inner",
                scatter_dimension=0,
                tiled=True,
            )
            done = mixture
        elif k == 5:
            done = adam_of(1, adam_of(0, token, 300), 1)
        elif k == 6:
            done = adam_of(3, adam_of(2, token, 300), 1)
        elif k - 3 < len(chunks):
            done = adam_of(k - 3, token, 300)
        waits.append(done)

        if k + 1 <= last:
            following = mine[k + 1]
        if k == last + 2:
            continue
        results = list(run_round(place, own, pair, following, waits))
        token = results[0]
        if own:
            by_pairs[k] = results.pop(0)
        if pair:
            totals_of[k - 1] = results.pop(0)
        edges[k + 1] = results.pop(0)

    block_output = (middle + alive * mixture_own.astype(jnp.float32)).astype(brain_floating)

    rest_states = (
        (norm_gains, gains_first, gains_second),
        (query_weight, query_first, query_second),
        (keyvalue_weight, keyvalue_first_moment, keyvalue_second_moment),
        (output_weight, output_first, output_second),
        (router_weight, router_first, router_second),
    )
    rates = (
        (gain_rate, 0.0),
        (root, decay_rate),
        (root, decay_rate),
        ((WIDTH // 16) ** (-0.5), decay_rate),
        ((4 * MODEL_WIDTH) ** (-0.5), decay_rate),
    )
    updated = adam_rest(place, totals_of[last], ends[last], rest_states, rates)
    return (block_output, input_gradient) + tuple(updated) + tuple(renewed[0]) + tuple(renewed[1])


def solution(mesh):
    replicas, shards = (mesh.shape["replica"], mesh.shape["fsdp"])
    outer = shards // GROUP
    split = Mesh(mesh.devices.reshape(replicas, outer, GROUP), ("replica",) + fsdp)
    rows = P(("replica",) + fsdp, None)
    by_first = P(fsdp, None)
    by_second = P(None, fsdp)
    by_middle = P(None, fsdp, None)
    by_third = P(None, None, fsdp, None)
    by_last = P(None, None, fsdp)
    weights = (by_second, by_first, by_middle, by_first, by_first, by_third, by_last)
    states = tuple(spec for spec in weights for _ in range(3))
    return jax.shard_map(
        functools.partial(body, (replicas, outer)),
        mesh=split,
        in_specs=(rows,) * 4 + states,
        out_specs=(rows,) * 2 + states,
        check_vma=False,
    )
```

```python
import functools
import math

import jax
import jax.numpy as jnp
from jax import lax
from jax.experimental import pallas as pl
from jax.experimental.pallas import tpu as pltpu
from jax.sharding import Mesh
from jax.sharding import PartitionSpec as P

MODEL_WIDTH = 1024
QUERY_HEADS = 16
KEYVALUE_HEADS = 8
HEAD_SIZE = 64
F = 512
TOPK = 8
EXPERTS = 16
ADAM_STEP = 5
GROUP = 8
LOCAL = EXPERTS // GROUP
EXTRA = 128
CHUNKS = 2
TILE = 512
SPAN = 256
LANES = 128
WIDTH = QUERY_HEADS * HEAD_SIZE
KV_WIDTH = KEYVALUE_HEADS * HEAD_SIZE
PROJECTED = WIDTH + 2 * KV_WIDTH
SCORE_SCALE = HEAD_SIZE ** (-0.5)
ROUTER_BLOCK = (PROJECTED + MODEL_WIDTH) // EXTRA


norm_eps = 1e-06
rope_base = 10000.0
beta_one = 0.9
beta_two = 0.95
adam_eps = 1e-08
decay_rate = 0.1
gain_rate = 0.25
masked_value = -1e30
brain_floating = jnp.bfloat16


def layout(lengths, count_of_rows):
    document_ends = jnp.cumsum(lengths)
    row_index = jnp.arange(count_of_rows, dtype=jnp.int32)
    passed = row_index[:, None] >= document_ends[None, :]
    segment = jnp.sum(passed.astype(jnp.int32), axis=1)
    start_row = jnp.sum(jnp.where(passed, lengths[None, :], 0), axis=1)
    position = (row_index - start_row).astype(jnp.float32)
    alive_mask = (segment < lengths.shape[0]).astype(jnp.float32)
    allowed = (segment[:, None] == segment[None, :]) & (row_index[None, :] <= row_index[:, None])
    return (position, alive_mask, allowed)


def rope_tables(position):
    half_width = HEAD_SIZE // 2
    exponents = jnp.arange(half_width, dtype=jnp.float32) * (2.0 / HEAD_SIZE)
    inverse = jnp.exp(exponents * -math.log(rope_base))
    angles = position[:, None] * inverse[None, :]
    cosine, sine = (jnp.cos(angles), jnp.sin(angles))
    return (
        jnp.concatenate([cosine] * 4, axis=1),
        jnp.concatenate([-sine, sine, -sine, sine], axis=1),
    )


def product(left, right):
    return jnp.dot(left, right, preferred_element_type=jnp.float32)


def times_transposed(left, right):
    return lax.dot_general(
        left, right, (((1,), (1,)), ((), ())), preferred_element_type=jnp.float32
    )


def transposed_times(left, right):
    return lax.dot_general(
        left, right, (((0,), (0,)), ((), ())), preferred_element_type=jnp.float32
    )


def normalize(values):
    inverse = lax.rsqrt(jnp.mean(values * values, axis=-1, keepdims=True) + norm_eps)
    return (values * inverse, inverse)


def norm_back(upstream, scaled_rows, inverse, gain_row):
    weighted = upstream * gain_row
    inner = jnp.mean(weighted * scaled_rows, axis=-1, keepdims=True)
    return inverse * (weighted - scaled_rows * inner)


def column_sums(values):
    ones = jnp.ones((values.shape[0], LANES), brain_floating)
    high = values.astype(brain_floating)
    low = (values - high.astype(jnp.float32)).astype(brain_floating)
    return transposed_times(high, ones) + transposed_times(low, ones)


def lanes_of(shape):
    return lax.broadcasted_iota(jnp.int32, shape, 1)


def rotate(values, cosine, sine):
    half = HEAD_SIZE // 2
    front = lax.rem(lanes_of(values.shape), HEAD_SIZE) < half
    swapped = jnp.where(
        front, pltpu.roll(values, LANES - half, 1), pltpu.roll(values, half, 1)
    )
    return values * cosine + swapped * sine


def both_halves(values, which):
    turned = pltpu.roll(values, HEAD_SIZE, 1)
    first = lanes_of(values.shape) < HEAD_SIZE
    return jnp.where(first == (which == 0), values, turned)


def only_half(values, which):
    first = lanes_of(values.shape) < HEAD_SIZE
    return jnp.where(first == (which == 0), values, 0.0)


def gates_of(rows, router, mask):
    logits = product(rows, router)
    peak = jnp.max(jnp.where(mask, logits, masked_value), axis=1, keepdims=True)
    weights = jnp.where(mask, jnp.exp(logits - peak), 0.0)
    return weights / jnp.sum(weights, axis=1, keepdims=True)


def adamw_step(weight, moment_old, square_old, gradient, step_rate, shrink):
    moment = beta_one * moment_old + (1.0 - beta_one) * gradient
    square = beta_two * square_old + (1.0 - beta_two) * gradient * gradient
    moment_hat = moment / (1.0 - beta_one**ADAM_STEP)
    square_hat = square / (1.0 - beta_two**ADAM_STEP)
    renewed = weight - step_rate * (
        moment_hat / (jnp.sqrt(square_hat) + adam_eps) + shrink * weight
    )
    return (moment, square, renewed)


MIB = 1024 * 1024
ANYWHERE = pl.BlockSpec(memory_space=pl.ANY)


def takes(microseconds):
    return pl.CostEstimate(
        flops=int(microseconds * 1e9), bytes_accessed=int(microseconds * 3.6e6), transcendentals=0
    )


def whole(shape):
    return pl.BlockSpec(shape, lambda *_: (0,) * len(shape), pipeline_mode=pl.Buffered(1))


def part(shape, place):
    return pl.BlockSpec(shape, lambda *_: place, pipeline_mode=pl.Buffered(1))


def out(shape, dtype):
    return jax.ShapeDtypeStruct(shape, dtype)


def split_kernel(odd_ref, gateup_ref, down_ref, out_ref):
    for k in range(2):
        out_ref[k, 0] = gateup_ref[k, 0].astype(brain_floating)
        out_ref[k, 1] = gateup_ref[k, 1].astype(brain_floating)
        out_ref[k, 2] = down_ref[k].T.astype(brain_floating)


def split_by_owner(odd, gateup, down):
    shard = gateup.shape[2]
    steps = GROUP // 2
    return pl.pallas_call(
        split_kernel,
        grid_spec=pltpu.PrefetchScalarGridSpec(
            num_scalar_prefetch=1,
            grid=(steps,),
            in_specs=[
                pl.BlockSpec((2, 2, shard, F), lambda e, odd: (e + steps * odd[0], 0, 0, 0)),
                pl.BlockSpec((2, F, shard), lambda e, odd: (e + steps * odd[0], 0, 0)),
            ],
            out_specs=pl.BlockSpec((2, 3, shard, F), lambda e, odd: (e, 0, 0, 0)),
        ),
        out_shape=out((GROUP, 3, shard, F), brain_floating),
        name="split",
    )(odd, gateup, down)


def front_kernel(
    x_ref, pack_ref, gains_ref, alive_ref, bias_ref, cos_ref, sin_ref, wait_ref, normed_ref, qkv_ref, mixed_ref, totals_ref, middle_ref, normed_two_ref, linear_ref,
):
    rows = x_ref.shape[0]
    scaled, _ = normalize(x_ref[...].astype(jnp.float32))
    normed = (scaled * gains_ref[0:1, :]).astype(brain_floating)
    normed_ref[...] = normed
    linear_ref[...] = product(normed, pack_ref[:, :PROJECTED])
    cosine, sine = (cos_ref[...], sin_ref[...])
    for at in range(0, WIDTH + KV_WIDTH, LANES):
        qkv_ref[:, at : at + LANES] = rotate(
            linear_ref[:, at : at + LANES], cosine, sine
        ).astype(brain_floating)
    qkv_ref[:, WIDTH + KV_WIDTH :] = linear_ref[:, WIDTH + KV_WIDTH :].astype(brain_floating)
    totals_ref[...] = jnp.zeros_like(totals_ref)

    @pl.loop(0, KEYVALUE_HEADS // 2)
    def _(pair):
        at = pl.multiple_of(pair * LANES, LANES)
        keys = qkv_ref[:, pl.ds(WIDTH + at, LANES)].astype(jnp.float32)
        values = qkv_ref[:, pl.ds(WIDTH + KV_WIDTH + at, LANES)].astype(jnp.float32)
        for a in range(2):
            head_keys = both_halves(keys, a).astype(brain_floating)
            head_values = both_halves(values, a)
            place = pl.multiple_of((2 * pair + a) * LANES, LANES)
            queries = qkv_ref[:, pl.ds(place, LANES)].astype(jnp.float32)
            for start in range(0, rows, SPAN):
                seen = min(start + SPAN, rows)
                mixed = jnp.zeros((SPAN, LANES), jnp.float32)
                for j in range(2):
                    head = 2 * (2 * pair + a) + j
                    query = only_half(queries[start : start + SPAN], j).astype(brain_floating)
                    scores = (
                        times_transposed(query, head_keys[:seen]) * SCORE_SCALE
                        + bias_ref[start : start + SPAN, :seen]
                    )
                    peak = jnp.max(scores, axis=1, keepdims=True)
                    weights = jnp.exp(scores - peak)
                    total = jnp.sum(weights, axis=1, keepdims=True)
                    probs = (weights * (1.0 / total)).astype(brain_floating)
                    mixed += product(probs, only_half(head_values[:seen], j).astype(brain_floating))
                    held = totals_ref[start : start + SPAN, :]
                    totals_ref[start : start + SPAN, :] = jnp.where(
                        lanes_of(held.shape) == head, peak + jnp.log(total), held
                    )
                mixed_ref[start : start + SPAN, pl.ds(place, LANES)] = mixed.astype(brain_floating)

    attended = product(mixed_ref[...], pack_ref[:, PROJECTED : PROJECTED + MODEL_WIDTH])
    middle = x_ref[...].astype(jnp.float32) + alive_ref[...] * attended
    middle_ref[...] = middle
    scaled_two, _ = normalize(middle)
    normed_two_ref[...] = (scaled_two * gains_ref[1:2, :]).astype(brain_floating)


def run_front(x, pack, gains, alive, bias, cosine, sine, wait):
    rows = x.shape[0]
    return pl.pallas_call(
        front_kernel,
        in_specs=[pl.BlockSpec(memory_space=pltpu.VMEM)] * 7 + [ANYWHERE],
        out_shape=[
            out((rows, MODEL_WIDTH), brain_floating),
            out((rows, PROJECTED), brain_floating),
            out((rows, WIDTH), brain_floating),
            out((rows, LANES), jnp.float32),
            out((rows, MODEL_WIDTH), jnp.float32),
            out((rows, MODEL_WIDTH), brain_floating),
        ],
        scratch_shapes=[pltpu.VMEM((rows, PROJECTED), jnp.float32)],
        compiler_params=pltpu.CompilerParams(vmem_limit_bytes=52 * MIB),
        name="front",
    )(x, pack, gains, alive, bias, cosine, sine, wait)


def middle_kernel(
    dx_ref, normed_two_ref, middle_ref, cot_ref, mask_ref, alive_ref, gains_ref, router_ref,
    output_ref, mixed_ref, wait_ref, d_middle_ref, d_mixed_ref, grads_ref,
):
    dx = dx_ref[...].astype(jnp.float32)
    normed_two = normed_two_ref[...]
    mask = mask_ref[...].astype(jnp.float32) > 0.5
    gates = gates_of(normed_two, router_ref[...], mask)
    extra = dx[:, MODEL_WIDTH:]
    d_gates = extra + pltpu.roll(extra, LANES - EXPERTS, 1)
    d_logits = (
        gates * (d_gates - jnp.sum(gates * d_gates, axis=1, keepdims=True))
    ).astype(brain_floating)
    d_normed = dx[:, :MODEL_WIDTH] + times_transposed(d_logits, router_ref[...])
    scaled, inverse = normalize(middle_ref[...])
    d_middle = cot_ref[...].astype(jnp.float32) + norm_back(
        d_normed, scaled, inverse, gains_ref[1:2, :]
    )
    d_middle_ref[...] = d_middle
    d_attended = (alive_ref[...] * d_middle).astype(brain_floating)
    grads_ref[:, :MODEL_WIDTH] = transposed_times(mixed_ref[...], d_attended).astype(brain_floating)
    small = transposed_times(normed_two, d_logits)
    small = jnp.where(lanes_of(small.shape) == EXPERTS + 1, column_sums(d_normed * scaled), small)
    grads_ref[:, MODEL_WIDTH:] = small.astype(brain_floating)
    d_mixed_ref[...] = times_transposed(d_attended, output_ref[...]).astype(brain_floating)


def run_middle(dx, normed_two, middle, cot, mask, alive, gains, pack, mixed, wait):
    rows = middle.shape[0]
    full = [whole(v.shape) for v in (dx, normed_two, middle, cot, mask, alive, gains)]
    return pl.pallas_call(
        middle_kernel,
        grid=(1,),
        in_specs=full
        + [
            part((MODEL_WIDTH, EXTRA), (0, ROUTER_BLOCK)),
            part((WIDTH, MODEL_WIDTH), (0, PROJECTED // MODEL_WIDTH)),
            whole(mixed.shape),
            ANYWHERE,
        ],
        out_specs=[
            whole((rows, MODEL_WIDTH)),
            whole((rows, WIDTH)),
            whole((MODEL_WIDTH, MODEL_WIDTH + EXTRA)),
        ],
        out_shape=[
            out((rows, MODEL_WIDTH), jnp.float32),
            out((rows, WIDTH), brain_floating),
            out((MODEL_WIDTH, MODEL_WIDTH + EXTRA), brain_floating),
        ],
        compiler_params=pltpu.CompilerParams(vmem_limit_bytes=52 * MIB),
        cost_estimate=takes(30),
        name="middle_back",
    )(dx, normed_two, middle, cot, mask, alive, gains, pack, pack, mixed, wait)


def back_kernel(
    d_mixed_ref, qkv_ref, totals_ref, bias_ref, cos_ref, sin_ref, wait_ref, d_linear_ref,
    d_keys_ref, d_values_ref,
):
    rows = d_mixed_ref.shape[0]
    cosine, sine = (cos_ref[...], -sin_ref[...])

    @pl.loop(0, KEYVALUE_HEADS // 2)
    def _(pair):
        at = pl.multiple_of(pair * LANES, LANES)
        keys = qkv_ref[:, pl.ds(WIDTH + at, LANES)].astype(jnp.float32)
        values = qkv_ref[:, pl.ds(WIDTH + KV_WIDTH + at, LANES)].astype(jnp.float32)
        pair_keys = jnp.zeros((rows, LANES), jnp.float32)
        pair_values = jnp.zeros((rows, LANES), jnp.float32)
        for a in range(2):
            both_keys = both_halves(keys, a)
            head_keys = both_keys.astype(brain_floating)
            head_values = both_halves(values, a).astype(brain_floating)
            place = pl.multiple_of((2 * pair + a) * LANES, LANES)
            queries = qkv_ref[:, pl.ds(place, LANES)].astype(jnp.float32)
            d_outs = d_mixed_ref[:, pl.ds(place, LANES)].astype(jnp.float32)
            d_keys_ref[...] = jnp.zeros_like(d_keys_ref)
            d_values_ref[...] = jnp.zeros_like(d_values_ref)
            for start in range(0, rows, SPAN):
                seen = min(start + SPAN, rows)
                d_query = jnp.zeros((SPAN, LANES), jnp.float32)
                for j in range(2):
                    head = 2 * (2 * pair + a) + j
                    query = only_half(queries[start : start + SPAN], j).astype(brain_floating)
                    d_out = only_half(d_outs[start : start + SPAN], j).astype(brain_floating)
                    held = totals_ref[start : start + SPAN, :]
                    total = jnp.sum(
                        jnp.where(lanes_of(held.shape) == head, held, 0.0), axis=1, keepdims=True
                    )
                    scores = (
                        times_transposed(query, head_keys[:seen]) * SCORE_SCALE
                        + bias_ref[start : start + SPAN, :seen]
                    )
                    probs = jnp.exp(scores - total)
                    d_probs = times_transposed(d_out, head_values[:seen])
                    inner = jnp.sum(probs * d_probs, axis=1, keepdims=True)
                    d_scores = (probs * (d_probs - inner)).astype(brain_floating)
                    d_query += product(
                        d_scores, only_half(both_keys[:seen], j).astype(brain_floating)
                    )
                    d_keys_ref[:seen, :] += transposed_times(d_scores, query)
                    d_values_ref[:seen, :] += transposed_times(probs.astype(brain_floating), d_out)
                d_linear_ref[start : start + SPAN, pl.ds(place, LANES)] = rotate(
                    d_query * SCORE_SCALE,
                    cosine[start : start + SPAN],
                    sine[start : start + SPAN],
                ).astype(brain_floating)
            d_keys = d_keys_ref[...]
            d_values = d_values_ref[...]
            pair_keys += only_half(d_keys + pltpu.roll(d_keys, HEAD_SIZE, 1), a)
            pair_values += only_half(d_values + pltpu.roll(d_values, HEAD_SIZE, 1), a)
        d_linear_ref[:, pl.ds(WIDTH + at, LANES)] = rotate(
            pair_keys * SCORE_SCALE, cosine, sine
        ).astype(brain_floating)
        d_linear_ref[:, pl.ds(WIDTH + KV_WIDTH + at, LANES)] = pair_values.astype(brain_floating)


def run_back(d_mixed, qkv, totals, bias, cosine, sine, wait):
    rows = d_mixed.shape[0]
    held = (d_mixed, qkv, totals, bias, cosine, sine)
    return pl.pallas_call(
        back_kernel,
        grid=(1,),
        in_specs=[whole(v.shape) for v in held] + [ANYWHERE],
        out_specs=whole((rows, PROJECTED)),
        out_shape=out((rows, PROJECTED), brain_floating),
        scratch_shapes=[pltpu.VMEM((rows, LANES), jnp.float32)] * 2,
        compiler_params=pltpu.CompilerParams(vmem_limit_bytes=52 * MIB),
        cost_estimate=takes(30),
        name="attention_back",
    )(*held, wait)


def projection_kernel(
    d_linear_ref, normed_ref, x_ref, d_middle_ref, gains_ref, other_ref, pack_ref, wait_ref,
    grads_ref, d_input_ref,
):
    normed = normed_ref[...]
    for at in range(0, PROJECTED, 512):
        grads_ref[:, at : at + 512] = transposed_times(
            normed, d_linear_ref[:, at : at + 512]
        ).astype(brain_floating)
    d_normed = times_transposed(d_linear_ref[...], pack_ref[...])
    scaled, inverse = normalize(x_ref[...].astype(jnp.float32))
    sums = column_sums(d_normed * scaled)
    grads_ref[:, PROJECTED : PROJECTED + MODEL_WIDTH] = other_ref[:, :MODEL_WIDTH]
    small = other_ref[:, MODEL_WIDTH:].astype(jnp.float32)
    grads_ref[:, PROJECTED + MODEL_WIDTH :] = jnp.where(
        lanes_of(sums.shape) == EXPERTS, sums, small
    ).astype(brain_floating)
    d_input_ref[...] = d_middle_ref[...] + norm_back(d_normed, scaled, inverse, gains_ref[0:1, :])


def run_projection(d_linear, normed, x, d_middle, gains, other, pack, wait):
    rows = x.shape[0]
    held = (d_linear, normed, x, d_middle, gains, other)
    width = PROJECTED + other.shape[1]
    return pl.pallas_call(
        projection_kernel,
        grid=(1,),
        in_specs=[whole(v.shape) for v in held]
        + [part((MODEL_WIDTH, PROJECTED), (0, 0)), ANYWHERE],
        out_specs=[whole((MODEL_WIDTH, width)), whole((rows, MODEL_WIDTH))],
        out_shape=[
            out((MODEL_WIDTH, width), brain_floating),
            out((rows, MODEL_WIDTH), jnp.float32),
        ],
        compiler_params=pltpu.CompilerParams(vmem_limit_bytes=52 * MIB),
        cost_estimate=takes(30),
        name="projection_back",
    )(*held, pack, wait)


def expert_kernel(me_ref, x_ref, b_ref, w_one_ref, w_two_ref, router_ref, *refs):
    ga_ref, dgu_ref, dx_ref = refs[-3:]
    x = x_ref[...]
    branch = b_ref[:, 0, :, :MODEL_WIDTH].reshape(x.shape)
    mask = b_ref[:, 0, :, MODEL_WIDTH:].reshape(x.shape[0], EXTRA).astype(jnp.float32) > 0.5
    gates = gates_of(x, router_ref[...], mask)
    lane = lanes_of(gates.shape)
    d_gates = jnp.zeros_like(gates)
    dx = jnp.zeros((x.shape[0], MODEL_WIDTH), jnp.float32)
    for local in range(LOCAL):
        expert = me_ref[0] + GROUP * lax.rem(me_ref[1] + local, LOCAL)
        w_ref = (w_one_ref, w_two_ref)[local]
        gate_weight, up_weight, down_weight = (
            w_ref[:, p].reshape(MODEL_WIDTH, F) for p in range(3)
        )
        gate = jnp.sum(jnp.where(lane == expert, gates, 0.0), axis=1, keepdims=True)
        gate_linear = product(x, gate_weight)
        up_linear = product(x, up_weight)
        back = product(branch, down_weight)
        sig = jax.nn.sigmoid(gate_linear)
        silu = gate_linear * sig
        act = silu * up_linear
        ga_ref[:, local * F : (local + 1) * F] = (gate * act).astype(brain_floating)
        d_gate = jnp.sum(act * back, axis=1, keepdims=True)
        high = d_gate.astype(brain_floating).astype(jnp.float32)
        d_gates += jnp.where(lane == expert, high, 0.0)
        d_gates += jnp.where(lane == expert + EXPERTS, d_gate - high, 0.0)
        d_act = gate * back
        d_gl = (d_act * up_linear * (sig + silu * (1.0 - sig))).astype(brain_floating)
        d_ul = (d_act * silu).astype(brain_floating)
        dgu_ref[:, 2 * local * F : (2 * local + 1) * F] = d_gl
        dgu_ref[:, (2 * local + 1) * F : (2 * local + 2) * F] = d_ul
        dx += times_transposed(d_gl, gate_weight) + times_transposed(d_ul, up_weight)
    blocks, _, part_rows, _ = dx_ref.shape
    dx_ref[:, 0, :, :MODEL_WIDTH] = dx.astype(brain_floating).reshape(
        blocks, part_rows, MODEL_WIDTH
    )
    dx_ref[:, 0, :, MODEL_WIDTH:] = d_gates.astype(brain_floating).reshape(
        blocks, part_rows, EXTRA
    )


def run_experts(me, c, x, b, weights, pack, before):
    rows = x.shape[0]
    part_rows = b.shape[2]
    tile = 2 * part_rows
    wide = MODEL_WIDTH + EXTRA

    def rowed(width):
        return pl.BlockSpec((tile, width), lambda i, me_ref: (i, 0))

    return pl.pallas_call(
        expert_kernel,
        grid_spec=pltpu.PrefetchScalarGridSpec(
            num_scalar_prefetch=1,
            grid=(rows // tile,),
            in_specs=[
                rowed(MODEL_WIDTH),
                pl.BlockSpec((2, 1, part_rows, wide), lambda i, me_ref: (i, c, 0, 0)),
                whole(weights[0].shape),
                whole(weights[1].shape),
                part((MODEL_WIDTH, EXTRA), (0, ROUTER_BLOCK)),
            ]
            + [ANYWHERE] * len(before),
            out_specs=[
                rowed(LOCAL * F),
                rowed(2 * LOCAL * F),
                pl.BlockSpec((2, 1, part_rows, wide), lambda i, me_ref: (i, c, 0, 0)),
            ],
        ),
        out_shape=[
            out((rows, LOCAL * F), brain_floating),
            out((rows, 2 * LOCAL * F), brain_floating),
            out((rows // part_rows, CHUNKS, part_rows, wide), brain_floating),
        ],
        input_output_aliases={6 + i: 2 for i in range(len(before))},
        compiler_params=pltpu.CompilerParams(vmem_limit_bytes=56 * MIB),
        name="experts",
    )(me, x, b, *weights, pack, *before)


def chunked_specs(steps, shape, place):
    def index(c):
        return lambda i, *scalars: place(jnp.clip(i - c * steps, 0, steps - 1), c, *scalars)

    return [pl.BlockSpec(shape, index(c)) for c in range(CHUNKS)]


def grads_kernel(steps, sides, me_ref, *refs):
    count = len(sides)
    ins, outs, sums = (refs[: CHUNKS * 2 * count], refs[-2 * count : -count], refs[-count:])
    i = pl.program_id(0)

    @pl.when(i == 0)
    def _():
        for total in sums:
            total[...] = jnp.zeros_like(total)

    for c in range(CHUNKS):

        @pl.when(i // steps == c)
        def _():
            for k in range(count):
                left, right = (ins[2 * (k * CHUNKS + c)], ins[2 * (k * CHUNKS + c) + 1])
                sums[k][...] += transposed_times(
                    left[...].reshape(right.shape[0], MODEL_WIDTH), right[...]
                )

    @pl.when(i == CHUNKS * steps - 1)
    def _():
        for result, total in zip(outs, sums):
            result[...] = total[...].astype(brain_floating).reshape(result.shape)


def run_grads(me, local, sides, shard, xs, b, gas, dgus, wait, cost):
    blocks = MODEL_WIDTH // shard
    rows, part_rows = (xs[0].shape[0], b.shape[2])
    tile = 2 * part_rows
    steps = rows // tile
    specs, arrays = ([], [])
    for side in sides:
        if side == 2:
            left = chunked_specs(
                steps, (2, 1, part_rows, MODEL_WIDTH), lambda i, c, me: (i, c, 0, 0)
            )
            right = chunked_specs(
                steps, (tile, F), lambda i, c, me: (i, lax.rem(me[1] + local, LOCAL))
            )
        else:
            left = chunked_specs(steps, (tile, MODEL_WIDTH), lambda i, c, me: (i, 0))
            right = chunked_specs(
                steps,
                (tile, F),
                lambda i, c, me, side=side: (i, 2 * lax.rem(me[1] + local, LOCAL) + side),
            )
        for c in range(CHUNKS):
            specs += [left[c], right[c]]
            arrays += [b, gas[c]] if side == 2 else [xs[c], dgus[c]]
    return pl.pallas_call(
        functools.partial(grads_kernel, steps, sides),
        grid_spec=pltpu.PrefetchScalarGridSpec(
            num_scalar_prefetch=1,
            grid=(CHUNKS * steps,),
            in_specs=specs + [ANYWHERE],
            out_specs=[whole((blocks, shard, F))] * len(sides),
            scratch_shapes=[pltpu.VMEM((MODEL_WIDTH, F), jnp.float32)] * len(sides),
        ),
        out_shape=[out((blocks, shard, F), brain_floating)] * len(sides),
        compiler_params=pltpu.CompilerParams(vmem_limit_bytes=52 * MIB),
        cost_estimate=takes(cost),
        name="grads",
    )(me, *arrays, wait)


def mix_kernel(steps, *refs):
    gas, w_refs, out_ref = (refs[:CHUNKS], refs[CHUNKS : CHUNKS + LOCAL], refs[-1])
    for c in range(CHUNKS):

        @pl.when(pl.program_id(0) // steps == c)
        def _():
            total = jnp.zeros((gas[c].shape[0], MODEL_WIDTH), jnp.float32)
            for local in range(LOCAL):
                total += times_transposed(
                    gas[c][:, local * F : (local + 1) * F],
                    w_refs[local][:, 0].reshape(MODEL_WIDTH, F),
                )
            out_ref[...] = total.astype(brain_floating).reshape(out_ref.shape)


def run_mix(gas, weights, part_rows, wait, cost):
    rows = gas[0].shape[0]
    tile = 2 * part_rows
    steps = rows // tile
    blocks, _, shard, _ = weights[0].shape
    return pl.pallas_call(
        functools.partial(mix_kernel, steps),
        grid=(CHUNKS * steps,),
        in_specs=chunked_specs(steps, (tile, LOCAL * F), lambda i, c: (i, 0))
        + [part((blocks, 1, shard, F), (0, 2, 0, 0))] * LOCAL
        + [ANYWHERE],
        out_specs=pl.BlockSpec(
            (2, 1, part_rows, MODEL_WIDTH), lambda i: (lax.rem(i, steps), i // steps, 0, 0)
        ),
        out_shape=out((rows // part_rows, CHUNKS, part_rows, MODEL_WIDTH), brain_floating),
        compiler_params=pltpu.CompilerParams(vmem_limit_bytes=52 * MIB),
        cost_estimate=takes(cost),
        name="mixture",
    )(*gas, *weights, wait)


def at_inner(place_ref):
    return (place_ref[0] == 1) | (place_ref[0] == 2)


def as_chunk(values):
    if values.ndim == 2:
        return jnp.stack([values[:, :F], values[:, F:]])
    return values


def round_kernel(kinds, waits, place_ref, *refs):
    has_own, has_pair, has_next = kinds
    refs = list(refs)

    def take(count):
        taken, refs[:count] = (refs[:count], [])
        return [as_chunk(ref[...].astype(jnp.float32)) for ref in taken]

    own = take(2) if has_own else None
    pair = take(2) if has_pair else None
    edge = take(1)[0] if has_next else None
    outs = refs[waits:]
    if has_own:
        outs.pop(0)[...] = (own[0] + own[1]).astype(brain_floating)
    if has_pair:
        total = pair[0] + pair[1]
        outs.pop(0)[...] = total.astype(brain_floating)
        edge = total if edge is None else jnp.where(at_inner(place_ref), total, edge)
    outs.pop(0)[...] = edge.astype(brain_floating)


def run_round(place, own, pair, following, waits):
    steps = GROUP // 2
    arrays, specs, count = ([], [], 0)

    flat = pair[0].shape if pair else following.shape
    piece = pl.BlockSpec((2,) + flat[1:], lambda i, _: (i, 0, 0))

    def chunk_spec(values):
        if values.ndim == 2:
            return pl.BlockSpec((values.shape[0], 2 * F), lambda i, _: (0, i))
        return piece

    if own:
        arrays += list(own)
        specs += [chunk_spec(own[0]), piece]
        count += 1
    if pair:
        arrays += list(pair)
        specs += [piece] * 2
        count += 1
    if following is not None:
        arrays.append(following)
        specs.append(chunk_spec(following))
    count += 1
    return pl.pallas_call(
        functools.partial(
            round_kernel, (bool(own), bool(pair), following is not None), len(waits)
        ),
        grid_spec=pltpu.PrefetchScalarGridSpec(
            num_scalar_prefetch=1,
            grid=(steps,),
            in_specs=specs + [ANYWHERE] * len(waits),
            out_specs=[piece] * count,
        ),
        out_shape=[out(flat, brain_floating)] * count,
        compiler_params=pltpu.CompilerParams(vmem_limit_bytes=40 * MIB),
        cost_estimate=takes(2),
        name="round",
    )(place, *arrays, *waits)


def after_kernel(values_ref, wait_ref, out_ref):
    del values_ref, wait_ref, out_ref


def after(values, wait):
    return pl.pallas_call(
        after_kernel,
        in_specs=[ANYWHERE] * 2,
        out_specs=ANYWHERE,
        out_shape=out(values.shape, values.dtype),
        input_output_aliases={0: 0},
        name="after",
    )(values, wait)


def adam_kernel(turned, rate, shrink, place_ref, t_ref, r_ref, w_ref, m_ref, v_ref, *rest):
    m_out, v_out, w_out, token_ref = rest[-4:]
    token_ref[...] = jnp.zeros_like(token_ref)
    inner = at_inner(place_ref)
    for k in range(t_ref.shape[0]):
        gradient = jnp.where(inner, t_ref[k].astype(jnp.float32), r_ref[k].astype(jnp.float32))
        if turned:
            at = (k,)
            gradient = gradient.T
        else:
            at = (k, 0)
        moment, square, renewed = adamw_step(
            w_ref[at], m_ref[at], v_ref[at], gradient, rate, shrink
        )
        m_out[at] = moment
        v_out[at] = square
        w_out[at] = renewed


def adam_part(place, total, ends, state, local, side, rate, before, wait, cost):
    weight, first, second = state
    turned = side == 2
    shard = total.shape[1]
    held = [] if before is None else list(before)
    if turned:
        spec = pl.BlockSpec((2, F, shard), lambda i, _: (i + local * (GROUP // 2), 0, 0))
    else:
        spec = pl.BlockSpec((2, 1, shard, F), lambda i, _: (i + local * (GROUP // 2), side, 0, 0))
    piece = pl.BlockSpec((2, shard, F), lambda i, _: (i, 0, 0))
    return pl.pallas_call(
        functools.partial(adam_kernel, turned, rate, decay_rate),
        grid_spec=pltpu.PrefetchScalarGridSpec(
            num_scalar_prefetch=1,
            grid=(GROUP // 2,),
            in_specs=[piece, piece, spec, spec, spec] + [ANYWHERE] * (len(held) + 1),
            out_specs=[spec] * 3 + [pl.BlockSpec((8, LANES), lambda i, _: (0, 0))],
        ),
        out_shape=[out(weight.shape, jnp.float32)] * 3 + [out((8, LANES), jnp.float32)],
        input_output_aliases={6 + i: i for i in range(len(held))},
        compiler_params=pltpu.CompilerParams(vmem_limit_bytes=60 * MIB),
        cost_estimate=takes(cost),
        name="adam",
    )(place, total, ends, weight, first, second, *held, wait)


def rest_kernel(rates, place_ref, t_ref, r_ref, *refs):
    inner = at_inner(place_ref)
    states, outs = (refs[:15], refs[15:])

    def gradient(j):
        return jnp.where(inner, t_ref[j].astype(jnp.float32), r_ref[j].astype(jnp.float32))

    def step(which, at, gradient):
        weight, first, second = states[3 * which : 3 * which + 3]
        rate, shrink = rates[which]
        results = adamw_step(weight[at], first[at], second[at], gradient, rate, shrink)
        for ref, value in zip(outs[3 * which : 3 * which + 3], results):
            ref[at] = value

    small = gradient(PROJECTED // F + 2)[:, :EXTRA]
    step(0, ..., small.T[EXPERTS : EXPERTS + 2, :])
    step(4, ..., small[:, :EXPERTS])
    for half in range(2):
        at = (slice(None), slice(half * F, half * F + F))
        step(1, at, gradient(half))
        step(2, half, gradient(2 + half))
        step(3, at, gradient(4 + half))


def adam_rest(place, total, ends, states, rates):
    flat = [v for state in states for v in state]
    in_vmem = pl.BlockSpec(memory_space=pltpu.VMEM)
    return pl.pallas_call(
        functools.partial(rest_kernel, rates),
        in_specs=[pl.BlockSpec(memory_space=pltpu.SMEM)] + [in_vmem] * (2 + len(flat)),
        out_shape=[out(v.shape, jnp.float32) for v in flat],
        compiler_params=pltpu.CompilerParams(vmem_limit_bytes=40 * MIB),
        name="adam_rest",
    )(place, total, ends, *flat)


fsdp = ("outer", "inner")


def body(
    sizes,
    tokens_in,
    cotangent,
    document_lengths,
    expert_choice,
    norm_gains,
    gains_first,
    gains_second,
    query_weight,
    query_first,
    query_second,
    keyvalue_weight,
    keyvalue_first_moment,
    keyvalue_second_moment,
    output_weight,
    output_first,
    output_second,
    router_weight,
    router_first,
    router_second,
    gateup_weight,
    gateup_first,
    gateup_second,
    down_weight,
    down_first,
    down_second,
):
    replicas, outer = sizes
    count_of_rows = tokens_in.shape[0]
    shard = query_weight.shape[0]
    place = lax.axis_index("replica").astype(jnp.int32).reshape(1)
    odd = lax.rem(place, LOCAL)
    me = jnp.concatenate([lax.axis_index("inner").astype(jnp.int32).reshape(1), odd])

    pack_own = jnp.concatenate(
        [
            query_weight,
            keyvalue_weight[0],
            keyvalue_weight[1],
            output_weight,
            router_weight,
            norm_gains.T,
            jnp.zeros((shard, EXTRA - EXPERTS - 2), jnp.float32),
        ],
        axis=1,
    ).astype(brain_floating)
    pack = lax.all_gather(pack_own, fsdp, axis=0, tiled=True)
    at = PROJECTED + MODEL_WIDTH + EXPERTS
    gains_value = pack[:, at : at + 2].astype(jnp.float32).T

    weights_own = lax.all_to_all(split_by_owner(odd, gateup_weight, down_weight), "inner", 0, 0)
    if outer > 1:
        weights_own = lax.all_gather(weights_own, "outer", axis=0, tiled=True)
    weights = (
        weights_own,
        lax.ppermute(weights_own, "replica", [(0, 1), (1, 0), (2, 3), (3, 2)]),
    )

    position, alive_mask, allowed = layout(document_lengths[0], count_of_rows)
    cosine, sine = rope_tables(position)
    alive = alive_mask[:, None]
    bias = jnp.where(allowed, 0.0, masked_value)

    expert_row = jnp.arange(EXPERTS, dtype=jnp.int32)
    chosen = jnp.any(expert_choice[:, :, None] == expert_row[None, None, :], axis=1)
    mask = jnp.concatenate(
        [
            chosen.astype(brain_floating),
            jnp.zeros((count_of_rows, EXTRA - EXPERTS), brain_floating),
        ],
        axis=1,
    )
    branch = (alive * cotangent.astype(jnp.float32)).astype(brain_floating)
    branch_pack = jnp.concatenate([branch, mask], axis=1)
    part_rows = count_of_rows // CHUNKS

    def gathered(values, c):
        return lax.all_gather(
            values[c * part_rows : (c + 1) * part_rows], "inner", axis=0, tiled=True
        )

    branch_all = lax.all_gather(branch_pack, "inner", axis=0, tiled=True).reshape(
        GROUP, CHUNKS, part_rows, MODEL_WIDTH + EXTRA
    )

    normed, qkv, mixed, totals, middle, normed_two = run_front(
        tokens_in, pack, gains_value, alive, bias, cosine, sine, weights_own
    )

    x_all, ga_all, dgu_all, dx = ([], [], [], None)
    for c in range(CHUNKS):
        x_part = gathered(normed_two, c)
        ga, dgu, dx = run_experts(
            me, c, x_part, branch_all, weights, pack, () if dx is None else (dx,)
        )
        x_all.append(x_part)
        ga_all.append(ga)
        dgu_all.append(dgu)
    dx_own = lax.psum_scatter(
        dx.reshape(GROUP * count_of_rows, MODEL_WIDTH + EXTRA),
        "inner",
        scatter_dimension=0,
        tiled=True,
    )

    def to_owner(parts):
        if outer > 1:
            parts = lax.psum_scatter(parts, "outer", scatter_dimension=0, tiled=True)
        return lax.all_to_all(parts, "inner", 0, 0)

    def swapped(values):
        return lax.ppermute(values, "replica", [(0, 1), (1, 0), (2, 3), (3, 2)])

    def across(values):
        return lax.ppermute(values, "replica", [(1, 2), (2, 1)])

    def grads_of(local, sides, wait, cost):
        return run_grads(me, local, sides, shard, x_all, branch_all, ga_all, dgu_all, wait, cost)

    chunks = [(local, side) for local in range(LOCAL) for side in (2, 0, 1)]
    last = len(chunks)
    root = MODEL_WIDTH ** (-0.5)
    states = (
        (gateup_weight, gateup_first, gateup_second),
        (down_weight, down_first, down_second),
    )
    renewed = [None, None]
    by_pairs, totals_of, ends, edges = ({}, {}, {}, {})

    def adam_of(k, wait, cost):
        local, side = chunks[k]
        which = side // 2
        *renewed[which], done = adam_part(
            place, totals_of[k], ends[k], states[which], local, side,
            (F // 16) ** (-0.5) if which else root, renewed[which], wait, cost,
        )
        return done

    ready = grads_of(0, (2,), dgu_all[-1], 1)
    token = ready[0]
    mine = {0: to_owner(token)}
    for k in range(-1, last + 3):
        own, pair, following, waits = (None, None, None, [])
        if k in edges:
            arrived = swapped(edges[k])
            ends[k - 2] = arrived
            if k <= last:
                own = (mine[k], arrived)
            else:
                waits.append(arrived)
        if k - 1 in by_pairs:
            pair = (by_pairs[k - 1], across(by_pairs[k - 1]))

        if 0 <= k < len(chunks) - 1:
            mine[k + 1] = to_owner(after(ready[k + 1], token))
        if k == -1:
            ready += grads_of(0, (0, 1), token, 1)
            done = ready[1]
        elif k == 0:
            ready += grads_of(1, (2,), token, 3)
            done = ready[3]
        elif k == 1:
            ready += grads_of(1, (0, 1), token, 3)
            done = ready[4]
        elif k == 2:
            d_middle, d_mixed, second_grads = run_middle(
                dx_own, normed_two, middle, cotangent, mask, alive, gains_value, pack, mixed, token
            )
            d_linear = run_back(d_mixed, qkv, totals, bias, cosine, sine, token)
            done = d_linear
        elif k == 3:
            rest_grads, input_gradient = run_projection(
                d_linear, normed, tokens_in, d_middle, gains_value, second_grads, pack, token
            )
            mine[last] = lax.psum_scatter(rest_grads, fsdp, scatter_dimension=0, tiled=True)
            done = input_gradient
        elif k == 4:
            mixture = run_mix(ga_all, weights, part_rows, token, 300)
            mixture_own = lax.psum_scatter(
                mixture.reshape(GROUP * count_of_rows, MODEL_WIDTH),
                "inner",
                scatter_dimension=0,
                tiled=True,
            )
            done = mixture
        elif k == 5:
            done = adam_of(1, adam_of(0, token, 300), 1)
        elif k == 6:
            done = adam_of(3, adam_of(2, token, 300), 1)
        elif k == last + 2:
            block_output = (middle + alive * mixture_own.astype(jnp.float32)).astype(
                brain_floating
            )
            done = adam_of(k - 3, block_output, 300)
        elif k - 3 < len(chunks):
            done = adam_of(k - 3, token, 300)
        waits.append(done)

        if k + 1 <= last:
            following = mine[k + 1]
        if k == last + 2:
            continue
        results = list(run_round(place, own, pair, following, waits))
        token = results[0]
        if own:
            by_pairs[k] = results.pop(0)
        if pair:
            totals_of[k - 1] = results.pop(0)
        edges[k + 1] = results.pop(0)

    rest_states = (
        (norm_gains, gains_first, gains_second),
        (query_weight, query_first, query_second),
        (keyvalue_weight, keyvalue_first_moment, keyvalue_second_moment),
        (output_weight, output_first, output_second),
        (router_weight, router_first, router_second),
    )
    rates = (
        (gain_rate, 0.0),
        (root, decay_rate),
        (root, decay_rate),
        ((WIDTH // 16) ** (-0.5), decay_rate),
        ((4 * MODEL_WIDTH) ** (-0.5), decay_rate),
    )
    updated = adam_rest(place, totals_of[last], ends[last], rest_states, rates)
    return (block_output, input_gradient) + tuple(updated) + tuple(renewed[0]) + tuple(renewed[1])


def solution(mesh):
    replicas, shards = (mesh.shape["replica"], mesh.shape["fsdp"])
    outer = shards // GROUP
    split = Mesh(mesh.devices.reshape(replicas, outer, GROUP), ("replica",) + fsdp)
    rows = P(("replica",) + fsdp, None)
    by_first = P(fsdp, None)
    by_second = P(None, fsdp)
    by_middle = P(None, fsdp, None)
    by_third = P(None, None, fsdp, None)
    by_last = P(None, None, fsdp)
    weights = (by_second, by_first, by_middle, by_first, by_first, by_third, by_last)
    states = tuple(spec for spec in weights for _ in range(3))
    return jax.shard_map(
        functools.partial(body, (replicas, outer)),
        mesh=split,
        in_specs=(rows,) * 4 + states,
        out_specs=(rows,) * 2 + states,
        check_vma=False,
    )
```
